32 devices in a mesh: row: 2 (over y), col: 16 (over z, x, core).
Axes of the slice: x: 2, y: 2, z: 4, core: 2. Of those that a mesh axis runs over, the one named last changes fastest.
Arguments:
- feature_map: bfloat16 [128, 128, 64], P('row', 'col'), may hold values from -6 to 6
- first_conv_weight: bfloat16 [3, 3, 64, 64], replicated, may hold values from -0.25 to 0.25
- first_conv_bias: float32 [64], replicated, may hold values from -3 to 3
- second_conv_weight: bfloat16 [3, 3, 64, 64], replicated, may hold values from -0.25 to 0.25
- second_conv_bias: float32 [64], replicated, may hold values from -3 to 3
- cotangent: bfloat16 [128, 128, 64], P('row', 'col'), may hold values from -6 to 6
Outputs:
- output: bfloat16 [128, 128, 64], P('row', 'col')
- grad_input: bfloat16 [128, 128, 64], P('row', 'col')
The draws below stay inside these ranges and needn't reach their ends.
All inputs are finite; a program needn't handle non-finite values.
Results may differ from the reference program's by a relative error of at most 0.0058.
Values may be sent and summed in bfloat16 or wider, within the bound.
No kernel may reach another device: no remote copies, remote signals or barrier semaphores. Data moves between devices by JAX's collectives and lax.ppermute only.
A program may use at most 64 MiB of HBM per device.

```python
import jax
import jax.numpy as jnp
from jax import lax

C = 64
DILATION_STEP = 4
NB = 128
N_ROW = 2


def level_of(stream_key, shape, cuts, smallest, top_value):
    factor_of = 1.0
    for position, parts in cuts:
        heights = jax.random.uniform(jax.random.fold_in(jax.random.fold_in(stream_key, 6), position), (parts,), jnp.float32, smallest / len(cuts), top_value / len(cuts))
        factor_of = factor_of * jnp.repeat(jnp.exp(heights), shape[position] // parts).reshape((-1,) + (1,) * (len(shape) - 1 - position))
    return factor_of


def scatter_about(stream_key, extent, spread, reach, shards=(), held_as=jnp.bfloat16):
    factor_of = level_of(stream_key, extent, shards, -0.22, 0.18) if shards else 1.0
    array = jax.random.normal(stream_key, extent, jnp.float32) * spread * factor_of
    return jnp.minimum(jnp.maximum(array, -reach), reach).astype(held_as)


def setup_inputs(seed: int = 0) -> dict:
    key_list = jax.random.split(jax.random.key(seed), 7)
    return {
        "feature_map": scatter_about(key_list[0], (NB, NB, C), 1.0, 6.0, ((0, 2), (1, 16))),
        "first_conv_weight": scatter_about(key_list[1], (3, 3, C, C), (9 * C) ** -0.5, 0.25),
        "first_conv_bias": scatter_about(key_list[2], (C,), 0.5, 3.0, (), jnp.float32),
        "second_conv_weight": scatter_about(key_list[3], (3, 3, C, C), (9 * C) ** -0.5, 0.25),
        "second_conv_bias": scatter_about(key_list[4], (C,), 0.5, 3.0, (), jnp.float32),
        "cotangent": scatter_about(key_list[5], (NB, NB, C), 1.0, 6.0, ((0, 2), (1, 16))),
    }


root_half = 0.7071067811865476
inv_root_tau = 0.3989422804014327


def gelu_value(value_array):
    return 0.5 * value_array * (1.0 + lax.erf(value_array * root_half))


def gelu_slope(value_array):
    return 0.5 * (1.0 + lax.erf(value_array * root_half)) + value_array * jnp.exp(-0.5 * value_array * value_array) * inv_root_tau


def dilated_conv(padded_input, conv_kernel):
    return lax.conv_general_dilated(padded_input[None].astype(jnp.float32), conv_kernel.astype(jnp.float32), (1, 1), "VALID", rhs_dilation=(DILATION_STEP, DILATION_STEP), dimension_numbers=("NHWC", "HWIO", "NHWC"), precision=lax.Precision.HIGHEST)[0]


def reversed_kernel(conv_kernel):
    return jnp.transpose(conv_kernel[::-1, ::-1], (0, 1, 3, 2))


def margin(input_array):
    return jnp.pad(input_array, ((DILATION_STEP, DILATION_STEP), (DILATION_STEP, DILATION_STEP), (0, 0)))


def reference(feature_map, first_conv_weight, first_conv_bias, second_conv_weight, second_conv_bias, cotangent):
    band_len = NB // N_ROW
    offsets = jnp.arange(N_ROW, dtype=jnp.int32) * band_len

    def stacked(result):
        return result.reshape(NB, NB, C)

    def row_strip(input_array, shift_amount, extra):
        return lax.dynamic_slice_in_dim(input_array, shift_amount, band_len + extra, 0)

    def mirror_band(input_array, shift_amount):
        return jnp.transpose(lax.dynamic_slice_in_dim(input_array, shift_amount, band_len, 1), (1, 0, 2))

    def make_symmetric(shift_amount):
        total_sum = row_strip(feature_map, shift_amount, 0).astype(jnp.float32) + mirror_band(feature_map, shift_amount).astype(jnp.float32)
        return total_sum.astype(jnp.bfloat16)

    symmetric = stacked(lax.map(make_symmetric, offsets))
    symmetric_padding = margin(symmetric)

    def pre_first(shift_amount):
        return dilated_conv(row_strip(symmetric_padding, shift_amount, 2 * DILATION_STEP), first_conv_weight) + first_conv_bias

    def make_hidden(shift_amount):
        return gelu_value(pre_first(shift_amount)).astype(jnp.bfloat16)

    hidden_padding = margin(stacked(lax.map(make_hidden, offsets)))

    def second_section(shift_amount):
        second_preactivation = dilated_conv(row_strip(hidden_padding, shift_amount, 2 * DILATION_STEP), second_conv_weight) + second_conv_bias
        result = (row_strip(symmetric, shift_amount, 0).astype(jnp.float32) + gelu_value(second_preactivation)).astype(jnp.bfloat16)
        grad_second = (row_strip(cotangent, shift_amount, 0).astype(jnp.float32) * gelu_slope(second_preactivation)).astype(jnp.bfloat16)
        return result, grad_second

    result_bands, second_bands = lax.map(second_section, offsets)
    output = stacked(result_bands)
    second_padding = margin(stacked(second_bands))

    def third_section(shift_amount):
        hidden_gradient = dilated_conv(row_strip(second_padding, shift_amount, 2 * DILATION_STEP), reversed_kernel(second_conv_weight))
        return (hidden_gradient * gelu_slope(pre_first(shift_amount))).astype(jnp.bfloat16)

    first_padding = margin(stacked(lax.map(third_section, offsets)))

    def fourth_section(shift_amount):
        total_sum = row_strip(cotangent, shift_amount, 0).astype(jnp.float32) + dilated_conv(row_strip(first_padding, shift_amount, 2 * DILATION_STEP), reversed_kernel(first_conv_weight))
        return total_sum.astype(jnp.bfloat16)

    grad_sym = stacked(lax.map(fourth_section, offsets))

    def fifth_section(shift_amount):
        total_sum = row_strip(grad_sym, shift_amount, 0).astype(jnp.float32) + mirror_band(grad_sym, shift_amount).astype(jnp.float32)
        return total_sum.astype(jnp.bfloat16)

    grad_input = stacked(lax.map(fifth_section, offsets))
    return output, grad_input
```

```python
import jax
import jax.numpy as jnp
from jax import lax
from jax.sharding import PartitionSpec as P

DILATION_STEP = 4
CORES = 2
CONVS = 4


root_half = 0.7071067811865476
inv_root_tau = 0.3989422804014327
both = ("row", "col")


def with_halo(array, sides, width):
    for axis, dim in sides:
        size, length = (lax.axis_size(axis), array.shape[dim])
        up = [(i, (i + 1) % size) for i in range(size - 1)]
        down = [(j, i) for i, j in up]
        last = lax.slice_in_dim(array, length - width, length, axis=dim)
        first = lax.slice_in_dim(array, 0, width, axis=dim)
        before = lax.ppermute(last, axis, up)
        after = lax.ppermute(first, axis, down)
        array = jnp.concatenate([before, array, after], axis=dim)
    return array


def gelu_value(value_array):
    return 0.5 * value_array * (1.0 + lax.erf(value_array * root_half))


def gelu_slope(value_array):
    return (
        0.5 * (1.0 + lax.erf(value_array * root_half))
        + value_array * jnp.exp(-0.5 * value_array * value_array) * inv_root_tau
    )


def conv(padded_input, conv_kernel, step):
    return lax.conv_general_dilated(
        padded_input[None],
        conv_kernel,
        (1, 1),
        "VALID",
        rhs_dilation=(step, step),
        dimension_numbers=("NHWC", "HWIO", "NHWC"),
        preferred_element_type=jnp.float32,
    )[0]


def dilated_conv(padded_input, conv_kernel):
    return conv(padded_input, conv_kernel, DILATION_STEP)


def reversed_kernel(conv_kernel):
    return jnp.transpose(conv_kernel[::-1, ::-1], (0, 1, 3, 2))


def extend(value_array):
    return with_halo(value_array, (("row", 0), ("col", 1)), DILATION_STEP)


def mirror(tile):
    row_count = lax.axis_size("row")
    col_count = lax.axis_size("col")
    tile_rows, tile_cols, channels = tile.shape
    unit_len = tile_rows // col_count
    col_ratio = col_count // row_count
    spread_parts = tile.reshape(1, 1, col_ratio, row_count, unit_len, tile_cols * channels)
    spread_parts = lax.all_to_all(spread_parts, "row", split_axis=3, concat_axis=1, tiled=True)
    across_parts = spread_parts.reshape(1, col_count, unit_len, 1, tile_cols * channels)
    across_parts = lax.all_to_all(across_parts, "col", split_axis=1, concat_axis=3, tiled=True)
    settle_parts = across_parts.reshape(1, 1, unit_len, row_count, tile_rows * channels)
    settle_parts = lax.all_to_all(settle_parts, "row", split_axis=3, concat_axis=1, tiled=True)
    turned = settle_parts.reshape(tile_cols, tile_rows, channels)
    return jnp.transpose(turned, (1, 0, 2))


def add_rounded(first, second):
    return (first.astype(jnp.float32) + second.astype(jnp.float32)).astype(jnp.bfloat16)


def by_tiles(feature_map, kernel_first, bias_first, kernel_second, bias_second, cotangent):
    symmetric = add_rounded(feature_map, mirror(feature_map))
    pre_first = dilated_conv(extend(symmetric), kernel_first) + bias_first
    hidden = gelu_value(pre_first).astype(jnp.bfloat16)
    pre_second = dilated_conv(extend(hidden), kernel_second) + bias_second
    output = (symmetric.astype(jnp.float32) + gelu_value(pre_second)).astype(jnp.bfloat16)
    grad_second = (cotangent.astype(jnp.float32) * gelu_slope(pre_second)).astype(jnp.bfloat16)
    hidden_gradient = dilated_conv(extend(grad_second), reversed_kernel(kernel_second))
    grad_first = (hidden_gradient * gelu_slope(pre_first)).astype(jnp.bfloat16)
    total_sum = cotangent.astype(jnp.float32) + dilated_conv(
        extend(grad_first), reversed_kernel(kernel_first)
    )
    grad_sym = total_sum.astype(jnp.bfloat16)
    return output, add_rounded(grad_sym, mirror(grad_sym))


def flipped_pair(conv_kernel):
    return jnp.transpose(conv_kernel, (1, 0, 2, 3)), conv_kernel


def block_diagonal(first, second):
    zeros = jnp.zeros_like(first)
    return jnp.concatenate(
        [jnp.concatenate([first, zeros], 3), jnp.concatenate([zeros, second], 3)], 2
    )


def dense_conv(image, conv_kernel):
    return conv(jnp.pad(image, ((1, 1), (1, 1), (0, 0))), conv_kernel, 1)


def by_classes(feature_map, kernel_first, bias_first, kernel_second, bias_second, cotangent):
    row_count, col_count = lax.axis_size("row"), lax.axis_size("col")
    device_count = row_count * col_count
    tile_rows, tile_cols, channels = feature_map.shape
    step = DILATION_STEP
    part_rows, part_cols = tile_rows // step, tile_cols // step
    class_rows, class_cols = part_rows * row_count, part_cols * col_count
    core = lax.axis_index("col") % CORES

    tile = jnp.concatenate([feature_map, cotangent], -1)
    parts = tile.reshape(part_rows, step, part_cols, step, 2 * channels)
    parts = jnp.transpose(parts, (1, 3, 2, 0, 4))
    parts = jnp.stack([parts, jnp.swapaxes(parts, 0, 1)], 2)
    parts = parts.reshape(device_count, part_cols * part_rows, 2 * channels)
    own = lax.all_to_all(parts, both, 0, 0, tiled=True)
    other = lax.ppermute(own, "col", [(i, i ^ 1) for i in range(col_count)])
    straight = jnp.where(core == 0, own, other)
    turned = jnp.where(core == 0, other, own)

    def image(pieces):
        pieces = pieces.reshape(row_count, col_count, part_cols, part_rows, 2 * channels)
        return jnp.transpose(pieces, (1, 2, 0, 3, 4)).reshape(class_cols, class_rows, 2 * channels)

    straight, turned = image(straight), jnp.swapaxes(image(turned), 0, 1)
    share = class_cols // CORES
    straight, turned = (
        lax.dynamic_slice_in_dim(v, core * (share - CONVS), share + CONVS, 0)
        for v in (straight, turned)
    )
    symmetric = add_rounded(straight[..., :channels], turned[..., :channels])
    gradient = jnp.concatenate([straight[..., channels:], turned[..., channels:]], -1)

    pre_first = dense_conv(symmetric, jnp.concatenate(flipped_pair(kernel_first), 3)) + jnp.tile(
        bias_first, 2
    )
    hidden = gelu_value(pre_first).astype(jnp.bfloat16)
    pre_second = dense_conv(hidden, block_diagonal(*flipped_pair(kernel_second))) + jnp.tile(
        bias_second, 2
    )
    output = (
        symmetric.astype(jnp.float32) + gelu_value(pre_second[..., :channels])
    ).astype(jnp.bfloat16)
    grad_second = (gradient.astype(jnp.float32) * gelu_slope(pre_second)).astype(jnp.bfloat16)
    hidden_gradient = dense_conv(
        grad_second, block_diagonal(*flipped_pair(reversed_kernel(kernel_second)))
    )
    grad_first = (hidden_gradient * gelu_slope(pre_first)).astype(jnp.bfloat16)
    total_sum = gradient.astype(jnp.float32) + dense_conv(
        grad_first, block_diagonal(*flipped_pair(reversed_kernel(kernel_first)))
    )
    grad_sym = total_sum.astype(jnp.bfloat16)
    grad_input = add_rounded(grad_sym[..., :channels], grad_sym[..., channels:])
    result = jnp.concatenate([output, grad_input], -1)
    result = lax.dynamic_slice_in_dim(result, core * CONVS, share, 0)

    half = col_count // CORES
    result = result.reshape(half, part_cols, row_count, part_rows, 2 * channels)
    result = jnp.transpose(result, (2, 0, 1, 3, 4))[:, None]
    result = jnp.broadcast_to(result, (row_count, CORES) + result.shape[2:])
    result = result.reshape(device_count, part_cols * part_rows, 2 * channels)
    back = lax.all_to_all(result, both, 0, 0, tiled=True)
    back = back.reshape(step, step, CORES, part_cols, part_rows, 2 * channels)
    back = lax.dynamic_index_in_dim(back, lax.axis_index("col") // half, 2, keepdims=False)
    back = jnp.transpose(back, (3, 0, 2, 1, 4)).reshape(tile_rows, tile_cols, 2 * channels)
    return back[..., :channels], back[..., channels:]


def solution(mesh):
    row_count, col_count = mesh.shape["row"], mesh.shape["col"]
    classes = DILATION_STEP * DILATION_STEP
    paired = row_count * col_count == CORES * classes and col_count % CORES == 0
    in_specs = (P("row", "col", None), P(), P(), P(), P(), P("row", "col", None))
    out_specs = (P("row", "col", None), P("row", "col", None))

    def whole(feature_map, *others):
        size = feature_map.shape[0]
        fits = size % (DILATION_STEP * row_count) == 0 and size % (DILATION_STEP * col_count) == 0
        per_device = by_classes if paired and fits else by_tiles
        return jax.shard_map(
            per_device, mesh=mesh, in_specs=in_specs, out_specs=out_specs, check_vma=False
        )(feature_map, *others)

    return whole
```

```python
import functools

import jax
import jax.numpy as jnp
from jax import lax
from jax.experimental import pallas as pl
from jax.experimental.pallas import tpu as pltpu
from jax.sharding import PartitionSpec as P

DILATION_STEP = 4
CORES = 2
CONVS = 4


root_half = 0.7071067811865476
inv_root_tau = 0.3989422804014327
both = ("row", "col")


def with_halo(array, sides, width):
    for axis, dim in sides:
        size, length = (lax.axis_size(axis), array.shape[dim])
        up = [(i, (i + 1) % size) for i in range(size - 1)]
        down = [(j, i) for i, j in up]
        last = lax.slice_in_dim(array, length - width, length, axis=dim)
        first = lax.slice_in_dim(array, 0, width, axis=dim)
        before = lax.ppermute(last, axis, up)
        after = lax.ppermute(first, axis, down)
        array = jnp.concatenate([before, array, after], axis=dim)
    return array


def gelu_value(value_array):
    return 0.5 * value_array * (1.0 + lax.erf(value_array * root_half))


def gelu_slope(value_array):
    return (
        0.5 * (1.0 + lax.erf(value_array * root_half))
        + value_array * jnp.exp(-0.5 * value_array * value_array) * inv_root_tau
    )


def conv(padded_input, conv_kernel, step):
    return lax.conv_general_dilated(
        padded_input[None],
        conv_kernel,
        (1, 1),
        "VALID",
        rhs_dilation=(step, step),
        dimension_numbers=("NHWC", "HWIO", "NHWC"),
        preferred_element_type=jnp.float32,
    )[0]


def dilated_conv(padded_input, conv_kernel):
    return conv(padded_input, conv_kernel, DILATION_STEP)


def reversed_kernel(conv_kernel):
    return jnp.transpose(conv_kernel[::-1, ::-1], (0, 1, 3, 2))


def extend(value_array):
    return with_halo(value_array, (("row", 0), ("col", 1)), DILATION_STEP)


def mirror(tile):
    row_count = lax.axis_size("row")
    col_count = lax.axis_size("col")
    tile_rows, tile_cols, channels = tile.shape
    unit_len = tile_rows // col_count
    col_ratio = col_count // row_count
    spread_parts = tile.reshape(1, 1, col_ratio, row_count, unit_len, tile_cols * channels)
    spread_parts = lax.all_to_all(spread_parts, "row", split_axis=3, concat_axis=1, tiled=True)
    across_parts = spread_parts.reshape(1, col_count, unit_len, 1, tile_cols * channels)
    across_parts = lax.all_to_all(across_parts, "col", split_axis=1, concat_axis=3, tiled=True)
    settle_parts = across_parts.reshape(1, 1, unit_len, row_count, tile_rows * channels)
    settle_parts = lax.all_to_all(settle_parts, "row", split_axis=3, concat_axis=1, tiled=True)
    turned = settle_parts.reshape(tile_cols, tile_rows, channels)
    return jnp.transpose(turned, (1, 0, 2))


def add_rounded(first, second):
    return (first.astype(jnp.float32) + second.astype(jnp.float32)).astype(jnp.bfloat16)


def by_tiles(feature_map, kernel_first, bias_first, kernel_second, bias_second, cotangent):
    symmetric = add_rounded(feature_map, mirror(feature_map))
    pre_first = dilated_conv(extend(symmetric), kernel_first) + bias_first
    hidden = gelu_value(pre_first).astype(jnp.bfloat16)
    pre_second = dilated_conv(extend(hidden), kernel_second) + bias_second
    output = (symmetric.astype(jnp.float32) + gelu_value(pre_second)).astype(jnp.bfloat16)
    grad_second = (cotangent.astype(jnp.float32) * gelu_slope(pre_second)).astype(jnp.bfloat16)
    hidden_gradient = dilated_conv(extend(grad_second), reversed_kernel(kernel_second))
    grad_first = (hidden_gradient * gelu_slope(pre_first)).astype(jnp.bfloat16)
    total_sum = cotangent.astype(jnp.float32) + dilated_conv(
        extend(grad_first), reversed_kernel(kernel_first)
    )
    grad_sym = total_sum.astype(jnp.bfloat16)
    return output, add_rounded(grad_sym, mirror(grad_sym))


def flipped_pair(conv_kernel):
    return jnp.transpose(conv_kernel, (1, 0, 2, 3)), conv_kernel


def block_diagonal(first, second):
    zeros = jnp.zeros_like(first)
    return jnp.concatenate(
        [jnp.concatenate([first, zeros], 3), jnp.concatenate([zeros, second], 3)], 2
    )


def tap_matrix(first, second):
    taps = jnp.transpose(block_diagonal(first, second), (0, 2, 1, 3))
    return taps.reshape(taps.shape[0] * taps.shape[1], -1)


def class_kernel(
    row_count,
    part_cols,
    own,
    other,
    weight_first,
    weight_second,
    weight_third,
    weight_fourth,
    bias_first,
    bias_second,
    result,
    turning,
    window,
):
    blocks, part, width = own.shape
    channels = width // 2
    part_rows = part // part_cols
    col_count = blocks // row_count
    class_cols, class_rows = col_count * part_cols, row_count * part_rows
    share = class_cols // CORES
    count = share + CONVS
    core = lax.rem(lax.axis_index("col"), CORES)
    begin = core * (share - CONVS)
    low = lax.broadcasted_iota(jnp.int32, (count * class_rows, width), 1) < channels
    place = lax.rem(lax.broadcasted_iota(jnp.int32, (count * class_rows, width), 0), class_rows)

    pieces = []
    for r in range(row_count):
        reach = pl.ds(r * col_count + core * ((share - CONVS) // part_cols), count // part_cols)
        piece = jnp.where(core == 0, own[reach], other[reach])
        pieces.append(piece.reshape(count, part_rows, width))
    straight = jnp.concatenate(pieces, 1).astype(jnp.float32)
    straight = straight.reshape(count * class_rows, width)

    for r in range(row_count):
        reach = pl.ds(r * col_count, col_count)
        piece = jnp.where(core == 0, other[reach], own[reach]).astype(jnp.float32)
        piece = piece.reshape(class_cols, part_rows, width)
        for k in range(class_cols):
            turning[pl.ds(k * class_rows + r * part_rows, part_rows), :] = piece[k]
    turned = jnp.concatenate(
        [turning[pl.ds(begin + i, class_cols, stride=class_rows), :] for i in range(count)], 0
    )

    def swapped(value):
        return pltpu.roll(value, channels, 1)

    def tap_sum(image, matrix):
        gap = jnp.zeros((class_rows, width), image.dtype)
        before = jnp.concatenate([gap, image[:-class_rows]], 0)
        after = jnp.concatenate([image[class_rows:], gap], 0)
        taps = jnp.dot(
            jnp.concatenate([before, image, after], 1),
            matrix[...],
            preferred_element_type=jnp.float32,
        )
        above = jnp.where(place == 0, 0.0, pltpu.roll(taps[:, :width], 1, 0))
        below = pltpu.roll(taps[:, 2 * width :], count * class_rows - 1, 0)
        below = jnp.where(place == class_rows - 1, 0.0, below)
        return above + taps[:, width : 2 * width] + below

    symmetric = straight + turned
    symmetric = jnp.where(low, symmetric, swapped(symmetric)).astype(jnp.bfloat16)
    gradient = jnp.where(low, swapped(straight), turned)

    pre_first = tap_sum(symmetric, weight_first) + bias_first[...]
    hidden = gelu_value(pre_first).astype(jnp.bfloat16)
    slope_first = gelu_slope(pre_first)
    pre_second = tap_sum(hidden, weight_second) + bias_second[...]
    output = symmetric.astype(jnp.float32) + gelu_value(pre_second)
    grad_second = (gradient * gelu_slope(pre_second)).astype(jnp.bfloat16)
    grad_first = (tap_sum(grad_second, weight_third) * slope_first).astype(jnp.bfloat16)
    grad_sym = (gradient + tap_sum(grad_first, weight_fourth)).astype(jnp.bfloat16)
    grad_sym = grad_sym.astype(jnp.float32)
    both_results = jnp.where(low, output, grad_sym + swapped(grad_sym)).astype(jnp.bfloat16)
    window[...] = both_results.reshape(count, class_rows, width)
    kept = window[pl.ds(core * CONVS, share)]
    half = share // part_cols
    for r in range(row_count):
        piece = kept[:, r * part_rows : (r + 1) * part_rows]
        result[r * half : (r + 1) * half] = piece.reshape(half, part, width)


def class_chains(row_count, part_cols, own, other, *parameters):
    blocks, part, width = own.shape
    class_cols, class_rows = blocks // row_count * part_cols, row_count * (part // part_cols)
    share = class_cols // CORES
    return pl.pallas_call(
        functools.partial(class_kernel, row_count, part_cols),
        out_shape=jax.ShapeDtypeStruct((blocks // CORES, part, width), jnp.bfloat16),
        in_specs=[pl.BlockSpec(memory_space=pltpu.VMEM)] * 8,
        out_specs=pl.BlockSpec(memory_space=pltpu.VMEM),
        scratch_shapes=[
            pltpu.VMEM((class_cols * class_rows, width), jnp.float32),
            pltpu.VMEM((share + CONVS, class_rows, width), jnp.bfloat16),
        ],
        compiler_params=pltpu.CompilerParams(vmem_limit_bytes=32 * 2**20),
    )(own, other, *parameters)


def by_classes(feature_map, kernel_first, bias_first, kernel_second, bias_second, cotangent):
    row_count, col_count = lax.axis_size("row"), lax.axis_size("col")
    device_count = row_count * col_count
    tile_rows, tile_cols, channels = feature_map.shape
    step = DILATION_STEP
    part_rows, part_cols = tile_rows // step, tile_cols // step

    tile = jnp.concatenate([feature_map, cotangent], -1)
    parts = tile.reshape(part_rows, step, part_cols, step, 2 * channels)
    parts = jnp.transpose(parts, (1, 3, 2, 0, 4))
    parts = jnp.stack([parts, jnp.swapaxes(parts, 0, 1)], 2)
    parts = parts.reshape(device_count, part_cols * part_rows, 2 * channels)
    own = lax.all_to_all(parts, both, 0, 0, tiled=True)
    other = lax.ppermute(own, "col", [(i, i ^ 1) for i in range(col_count)])
    result = class_chains(
        row_count,
        part_cols,
        own,
        other,
        tap_matrix(*flipped_pair(kernel_first)),
        tap_matrix(*flipped_pair(kernel_second)),
        tap_matrix(*flipped_pair(reversed_kernel(kernel_second))),
        tap_matrix(*flipped_pair(reversed_kernel(kernel_first))),
        jnp.tile(bias_first, 2)[None],
        jnp.tile(bias_second, 2)[None],
    )

    half = col_count // CORES
    result = result.reshape(row_count, 1, half, part_cols * part_rows, 2 * channels)
    result = jnp.broadcast_to(result, (row_count, CORES) + result.shape[2:])
    result = result.reshape(device_count, part_cols * part_rows, 2 * channels)
    back = lax.all_to_all(result, both, 0, 0, tiled=True)
    back = back.reshape(step, step, CORES, part_cols, part_rows, 2 * channels)
    back = lax.dynamic_index_in_dim(back, lax.axis_index("col") // half, 2, keepdims=False)
    back = jnp.transpose(back, (3, 0, 2, 1, 4)).reshape(tile_rows, tile_cols, 2 * channels)
    return back[..., :channels], back[..., channels:]


def solution(mesh):
    row_count, col_count = mesh.shape["row"], mesh.shape["col"]
    classes = DILATION_STEP * DILATION_STEP
    paired = row_count * col_count == CORES * classes and col_count % CORES == 0
    in_specs = (P("row", "col", None), P(), P(), P(), P(), P("row", "col", None))
    out_specs = (P("row", "col", None), P("row", "col", None))

    def whole(feature_map, *others):
        size = feature_map.shape[0]
        fits = size % (DILATION_STEP * row_count) == 0 and size % (DILATION_STEP * col_count) == 0
        per_device = by_classes if paired and fits else by_tiles
        return jax.shard_map(
            per_device, mesh=mesh, in_specs=in_specs, out_specs=out_specs, check_vma=False
        )(feature_map, *others)

    return whole
```

```python
import functools

import jax
import jax.numpy as jnp
from jax import lax
from jax.experimental import pallas as pl
from jax.experimental.pallas import tpu as pltpu
from jax.sharding import PartitionSpec as P

DILATION_STEP = 4
HALVES = 2
CONVS = 4


root_half = 0.7071067811865476
inv_root_tau = 0.3989422804014327
both = ("row", "col")


def with_halo(array, sides, width):
    for axis, dim in sides:
        size, length = (lax.axis_size(axis), array.shape[dim])
        up = [(i, (i + 1) % size) for i in range(size - 1)]
        down = [(j, i) for i, j in up]
        last = lax.slice_in_dim(array, length - width, length, axis=dim)
        first = lax.slice_in_dim(array, 0, width, axis=dim)
        before = lax.ppermute(last, axis, up)
        after = lax.ppermute(first, axis, down)
        array = jnp.concatenate([before, array, after], axis=dim)
    return array


def gelu_value(value_array):
    return 0.5 * value_array * (1.0 + lax.erf(value_array * root_half))


def gelu_slope(value_array):
    return (
        0.5 * (1.0 + lax.erf(value_array * root_half))
        + value_array * jnp.exp(-0.5 * value_array * value_array) * inv_root_tau
    )


def conv(padded_input, conv_kernel, step):
    return lax.conv_general_dilated(
        padded_input[None],
        conv_kernel,
        (1, 1),
        "VALID",
        rhs_dilation=(step, step),
        dimension_numbers=("NHWC", "HWIO", "NHWC"),
        preferred_element_type=jnp.float32,
    )[0]


def dilated_conv(padded_input, conv_kernel):
    return conv(padded_input, conv_kernel, DILATION_STEP)


def reversed_kernel(conv_kernel):
    return jnp.transpose(conv_kernel[::-1, ::-1], (0, 1, 3, 2))


def extend(value_array):
    return with_halo(value_array, (("row", 0), ("col", 1)), DILATION_STEP)


def mirror(tile):
    row_count = lax.axis_size("row")
    col_count = lax.axis_size("col")
    tile_rows, tile_cols, channels = tile.shape
    unit_len = tile_rows // col_count
    col_ratio = col_count // row_count
    spread_parts = tile.reshape(1, 1, col_ratio, row_count, unit_len, tile_cols * channels)
    spread_parts = lax.all_to_all(spread_parts, "row", split_axis=3, concat_axis=1, tiled=True)
    across_parts = spread_parts.reshape(1, col_count, unit_len, 1, tile_cols * channels)
    across_parts = lax.all_to_all(across_parts, "col", split_axis=1, concat_axis=3, tiled=True)
    settle_parts = across_parts.reshape(1, 1, unit_len, row_count, tile_rows * channels)
    settle_parts = lax.all_to_all(settle_parts, "row", split_axis=3, concat_axis=1, tiled=True)
    turned = settle_parts.reshape(tile_cols, tile_rows, channels)
    return jnp.transpose(turned, (1, 0, 2))


def add_rounded(first, second):
    return (first.astype(jnp.float32) + second.astype(jnp.float32)).astype(jnp.bfloat16)


def by_tiles(feature_map, kernel_first, bias_first, kernel_second, bias_second, cotangent):
    symmetric = add_rounded(feature_map, mirror(feature_map))
    pre_first = dilated_conv(extend(symmetric), kernel_first) + bias_first
    hidden = gelu_value(pre_first).astype(jnp.bfloat16)
    pre_second = dilated_conv(extend(hidden), kernel_second) + bias_second
    output = (symmetric.astype(jnp.float32) + gelu_value(pre_second)).astype(jnp.bfloat16)
    grad_second = (cotangent.astype(jnp.float32) * gelu_slope(pre_second)).astype(jnp.bfloat16)
    hidden_gradient = dilated_conv(extend(grad_second), reversed_kernel(kernel_second))
    grad_first = (hidden_gradient * gelu_slope(pre_first)).astype(jnp.bfloat16)
    total_sum = cotangent.astype(jnp.float32) + dilated_conv(
        extend(grad_first), reversed_kernel(kernel_first)
    )
    grad_sym = total_sum.astype(jnp.bfloat16)
    return output, add_rounded(grad_sym, mirror(grad_sym))


def flipped_pair(conv_kernel):
    return jnp.transpose(conv_kernel, (1, 0, 2, 3)), conv_kernel


def block_diagonal(first, second):
    zeros = jnp.zeros_like(first)
    return jnp.concatenate(
        [jnp.concatenate([first, zeros], 3), jnp.concatenate([zeros, second], 3)], 2
    )


def tap_matrix(first, second):
    taps = jnp.transpose(block_diagonal(first, second), (0, 2, 1, 3))
    return taps.reshape(taps.shape[0] * taps.shape[1], -1)


def class_order():
    step = range(DILATION_STEP)
    uneven = [[(a, b), (b, a)] for a in step for b in step if a < b]
    return sum(uneven, []) + [(a, a) for a in step]


def part_kernel(tile_cols, tile, parts):
    step = DILATION_STEP
    part_cols = tile_cols // step
    part_rows = tile.shape[0] // (tile_cols * step)
    for index, (a, b) in enumerate(class_order()):
        columns = [
            tile[pl.ds(a * tile_cols + k * step + b, part_rows, stride=step * tile_cols), :]
            for k in range(part_cols)
        ]
        part = jnp.concatenate(columns, 0).astype(jnp.bfloat16)
        r, c = divmod(index, parts.shape[2])
        for half in range(HALVES):
            parts[r, half, c] = part


def class_parts(row_count, feature_map, cotangent):
    tile_rows, tile_cols, channels = feature_map.shape
    classes = DILATION_STEP * DILATION_STEP
    cells = tile_rows * tile_cols
    shape = (row_count, HALVES, classes // row_count, cells // classes, 2 * channels)
    tile = jnp.concatenate([feature_map, cotangent], 2).astype(jnp.float32)
    return pl.pallas_call(
        functools.partial(part_kernel, tile_cols),
        out_shape=jax.ShapeDtypeStruct(shape, jnp.bfloat16),
        in_specs=[pl.BlockSpec(memory_space=pltpu.VMEM)],
        out_specs=pl.BlockSpec(memory_space=pltpu.VMEM),
        compiler_params=pltpu.CompilerParams(vmem_limit_bytes=16 * 2**20),
    )(tile.reshape(cells, 2 * channels))


def class_kernel(
    row_count,
    part_cols,
    own,
    other,
    weight_first,
    weight_second,
    weight_third,
    weight_fourth,
    bias_first,
    bias_second,
    result,
    turning,
    window,
):
    blocks, part, width = own.shape
    channels = width // 2
    part_rows = part // part_cols
    col_count = blocks // row_count
    half_count = col_count // HALVES
    class_cols, class_rows = col_count * part_cols, row_count * part_rows
    share = class_cols // HALVES
    count = share + CONVS
    column = lax.axis_index("col")
    half = lax.div(column, half_count)
    place = lax.axis_index("row") * half_count + lax.rem(column, half_count)
    even = place >= len(class_order()) - DILATION_STEP
    begin = half * (share - CONVS)
    cells = count * class_rows
    low = lax.broadcasted_iota(jnp.int32, (cells, width), 1) < channels
    row = lax.rem(lax.broadcasted_iota(jnp.int32, (cells, width), 0), class_rows)

    pieces = []
    for r in range(row_count):
        reach = pl.ds(r * col_count + half * ((share - CONVS) // part_cols), count // part_cols)
        pieces.append(own[reach].reshape(count, part_rows, width))
    straight = jnp.concatenate(pieces, 1).astype(jnp.float32).reshape(cells, width)

    for r in range(row_count):
        reach = slice(r * col_count, (r + 1) * col_count)
        piece = jnp.where(even, own[reach], other[reach]).astype(jnp.float32)
        piece = piece.reshape(class_cols, part_rows, width)
        for k in range(class_cols):
            turning[pl.ds(k * class_rows + r * part_rows, part_rows), :] = piece[k]
    turned = jnp.concatenate(
        [turning[pl.ds(begin + i, class_cols, stride=class_rows), :] for i in range(count)], 0
    )

    def swapped(value):
        return pltpu.roll(value, channels, 1)

    def tap_sum(image, matrix):
        gap = jnp.zeros((class_rows, width), image.dtype)
        before = jnp.concatenate([gap, image[:-class_rows]], 0)
        after = jnp.concatenate([image[class_rows:], gap], 0)
        taps = jnp.dot(
            jnp.concatenate([before, image, after], 1),
            matrix[...],
            preferred_element_type=jnp.float32,
        )
        above = jnp.where(row == 0, 0.0, pltpu.roll(taps[:, :width], 1, 0))
        below = pltpu.roll(taps[:, 2 * width :], cells - 1, 0)
        below = jnp.where(row == class_rows - 1, 0.0, below)
        return above + taps[:, width : 2 * width] + below

    symmetric = straight + turned
    symmetric = jnp.where(low, symmetric, swapped(symmetric)).astype(jnp.bfloat16)
    gradient = jnp.where(low, swapped(straight), turned)

    pre_first = tap_sum(symmetric, weight_first) + bias_first[...]
    hidden = gelu_value(pre_first).astype(jnp.bfloat16)
    slope_first = gelu_slope(pre_first)
    pre_second = tap_sum(hidden, weight_second) + bias_second[...]
    output = symmetric.astype(jnp.float32) + gelu_value(pre_second)
    grad_second = (gradient * gelu_slope(pre_second)).astype(jnp.bfloat16)
    grad_first = (tap_sum(grad_second, weight_third) * slope_first).astype(jnp.bfloat16)
    grad_sym = (gradient + tap_sum(grad_first, weight_fourth)).astype(jnp.bfloat16)
    grad_sym = grad_sym.astype(jnp.float32)
    finished = jnp.where(low, output, grad_sym + swapped(grad_sym)).astype(jnp.bfloat16)
    window[...] = finished.reshape(count, class_rows, width)

    for index, (a, b) in enumerate(class_order()):
        r, c = divmod(index, half_count)
        kept = window[pl.ds(half * CONVS + c * part_cols, part_cols)]
        kept = kept[:, r * part_rows : (r + 1) * part_rows]
        result[a * DILATION_STEP + b] = kept.reshape(part, width)


def class_chains(row_count, part_cols, own, other, *parameters):
    blocks, part, width = own.shape
    class_cols, class_rows = blocks // row_count * part_cols, row_count * (part // part_cols)
    count = class_cols // HALVES + CONVS
    return pl.pallas_call(
        functools.partial(class_kernel, row_count, part_cols),
        out_shape=jax.ShapeDtypeStruct((blocks // HALVES, part, width), jnp.bfloat16),
        in_specs=[pl.BlockSpec(memory_space=pltpu.VMEM)] * 8,
        out_specs=pl.BlockSpec(memory_space=pltpu.VMEM),
        scratch_shapes=[
            pltpu.VMEM((class_cols * class_rows, width), jnp.float32),
            pltpu.VMEM((count, class_rows, width), jnp.bfloat16),
        ],
        compiler_params=pltpu.CompilerParams(vmem_limit_bytes=32 * 2**20),
    )(own, other, *parameters)


def by_classes(feature_map, kernel_first, bias_first, kernel_second, bias_second, cotangent):
    row_count, col_count = lax.axis_size("row"), lax.axis_size("col")
    tile_rows, tile_cols, channels = feature_map.shape
    step = DILATION_STEP
    part_rows, part_cols = tile_rows // step, tile_cols // step

    parts = class_parts(row_count, feature_map, cotangent)
    parts = parts.reshape(row_count * col_count, part_cols * part_rows, 2 * channels)
    own = lax.all_to_all(parts, both, 0, 0, tiled=True)
    parameters = (
        tap_matrix(*flipped_pair(kernel_first)),
        tap_matrix(*flipped_pair(kernel_second)),
        tap_matrix(*flipped_pair(reversed_kernel(kernel_second))),
        tap_matrix(*flipped_pair(reversed_kernel(kernel_first))),
        jnp.tile(bias_first, 2)[None],
        jnp.tile(bias_second, 2)[None],
    )
    own, *parameters = lax.optimization_barrier((own,) + parameters)
    other = lax.ppermute(own, "col", [(i, i ^ 1) for i in range(col_count)])
    result = class_chains(row_count, part_cols, own, other, *parameters)

    half_count = col_count // HALVES
    order = sorted(range(step * step), key=lambda index: class_order()[index])
    halves = [
        [i // half_count * col_count + h * half_count + i % half_count for i in order]
        for h in range(HALVES)
    ]
    back = lax.all_to_all(result, both, 0, 0, axis_index_groups=halves, tiled=True)
    back = back.reshape(step, step, part_cols, part_rows, 2 * channels)
    back = jnp.transpose(back, (3, 0, 2, 1, 4)).reshape(tile_rows, tile_cols, 2 * channels)
    return back[..., :channels], back[..., channels:]


def solution(mesh):
    row_count, col_count = mesh.shape["row"], mesh.shape["col"]
    classes = DILATION_STEP * DILATION_STEP
    paired = row_count * col_count == HALVES * classes and col_count % (2 * HALVES) == 0
    in_specs = (P("row", "col", None), P(), P(), P(), P(), P("row", "col", None))
    out_specs = (P("row", "col", None), P("row", "col", None))

    def whole(feature_map, *others):
        size = feature_map.shape[0]
        part_rows, part_cols = size // row_count // DILATION_STEP, size // col_count // DILATION_STEP
        fits = size % (DILATION_STEP * row_count) == 0 and size % (DILATION_STEP * col_count) == 0
        fits = fits and part_rows % 16 == 0 and CONVS % part_cols == 0
        per_device = by_classes if paired and fits else by_tiles
        return jax.shard_map(
            per_device, mesh=mesh, in_specs=in_specs, out_specs=out_specs, check_vma=False
        )(feature_map, *others)

    return whole
```

```python
import functools

import jax
import jax.numpy as jnp
from jax import lax
from jax.experimental import pallas as pl
from jax.experimental.pallas import tpu as pltpu
from jax.sharding import PartitionSpec as P

DILATION_STEP = 4
HALVES = 2
CONVS = 4


root_half = 0.7071067811865476
inv_root_tau = 0.3989422804014327
both = ("row", "col")


def with_halo(array, sides, width):
    for axis, dim in sides:
        size, length = (lax.axis_size(axis), array.shape[dim])
        up = [(i, (i + 1) % size) for i in range(size - 1)]
        down = [(j, i) for i, j in up]
        last = lax.slice_in_dim(array, length - width, length, axis=dim)
        first = lax.slice_in_dim(array, 0, width, axis=dim)
        before = lax.ppermute(last, axis, up)
        after = lax.ppermute(first, axis, down)
        array = jnp.concatenate([before, array, after], axis=dim)
    return array


def gelu_value(value_array):
    return 0.5 * value_array * (1.0 + lax.erf(value_array * root_half))


def gelu_slope(value_array):
    return (
        0.5 * (1.0 + lax.erf(value_array * root_half))
        + value_array * jnp.exp(-0.5 * value_array * value_array) * inv_root_tau
    )


def conv(padded_input, conv_kernel, step):
    return lax.conv_general_dilated(
        padded_input[None],
        conv_kernel,
        (1, 1),
        "VALID",
        rhs_dilation=(step, step),
        dimension_numbers=("NHWC", "HWIO", "NHWC"),
        preferred_element_type=jnp.float32,
    )[0]


def dilated_conv(padded_input, conv_kernel):
    return conv(padded_input, conv_kernel, DILATION_STEP)


def reversed_kernel(conv_kernel):
    return jnp.transpose(conv_kernel[::-1, ::-1], (0, 1, 3, 2))


def extend(value_array):
    return with_halo(value_array, (("row", 0), ("col", 1)), DILATION_STEP)


def mirror(tile):
    row_count = lax.axis_size("row")
    col_count = lax.axis_size("col")
    tile_rows, tile_cols, channels = tile.shape
    unit_len = tile_rows // col_count
    col_ratio = col_count // row_count
    spread_parts = tile.reshape(1, 1, col_ratio, row_count, unit_len, tile_cols * channels)
    spread_parts = lax.all_to_all(spread_parts, "row", split_axis=3, concat_axis=1, tiled=True)
    across_parts = spread_parts.reshape(1, col_count, unit_len, 1, tile_cols * channels)
    across_parts = lax.all_to_all(across_parts, "col", split_axis=1, concat_axis=3, tiled=True)
    settle_parts = across_parts.reshape(1, 1, unit_len, row_count, tile_rows * channels)
    settle_parts = lax.all_to_all(settle_parts, "row", split_axis=3, concat_axis=1, tiled=True)
    turned = settle_parts.reshape(tile_cols, tile_rows, channels)
    return jnp.transpose(turned, (1, 0, 2))


def add_rounded(first, second):
    return (first.astype(jnp.float32) + second.astype(jnp.float32)).astype(jnp.bfloat16)


def by_tiles(feature_map, kernel_first, bias_first, kernel_second, bias_second, cotangent):
    symmetric = add_rounded(feature_map, mirror(feature_map))
    pre_first = dilated_conv(extend(symmetric), kernel_first) + bias_first
    hidden = gelu_value(pre_first).astype(jnp.bfloat16)
    pre_second = dilated_conv(extend(hidden), kernel_second) + bias_second
    output = (symmetric.astype(jnp.float32) + gelu_value(pre_second)).astype(jnp.bfloat16)
    grad_second = (cotangent.astype(jnp.float32) * gelu_slope(pre_second)).astype(jnp.bfloat16)
    hidden_gradient = dilated_conv(extend(grad_second), reversed_kernel(kernel_second))
    grad_first = (hidden_gradient * gelu_slope(pre_first)).astype(jnp.bfloat16)
    total_sum = cotangent.astype(jnp.float32) + dilated_conv(
        extend(grad_first), reversed_kernel(kernel_first)
    )
    grad_sym = total_sum.astype(jnp.bfloat16)
    return output, add_rounded(grad_sym, mirror(grad_sym))


def matrix_kernel(weight_first, weight_second, bias_first, bias_second, *outputs):
    first, second, third, fourth, first_bias, second_bias = outputs
    taps, channels = weight_first.shape[0], weight_first.shape[2]
    gap = jnp.zeros(weight_first.shape[2:], weight_first.dtype)
    for weight, ahead, behind in (
        (weight_first, first, fourth),
        (weight_second, second, third),
    ):
        for p in range(taps):
            for q in range(taps):
                upper = jnp.concatenate([weight[q, p], gap], 1)
                lower = jnp.concatenate([gap, weight[p, q]], 1)
                block = jnp.concatenate([upper, lower], 0)
                ahead[pl.ds(2 * channels * p, 2 * channels), pl.ds(2 * channels * q, 2 * channels)] = block
                p_back, q_back = taps - 1 - p, taps - 1 - q
                behind[
                    pl.ds(2 * channels * q_back, 2 * channels),
                    pl.ds(2 * channels * p_back, 2 * channels),
                ] = block
    for bias, wide in ((bias_first, first_bias), (bias_second, second_bias)):
        wide[...] = jnp.concatenate([bias[...], bias[...]], 1)


def chain_matrices(weight_first, weight_second, bias_first, bias_second):
    taps, channels = weight_first.shape[0], weight_first.shape[2]
    size = taps * 2 * channels
    vmem = pl.BlockSpec(memory_space=pltpu.VMEM)
    return pl.pallas_call(
        matrix_kernel,
        out_shape=[jax.ShapeDtypeStruct((size, size), jnp.bfloat16)] * 4
        + [jax.ShapeDtypeStruct((1, 2 * channels), jnp.float32)] * 2,
        in_specs=[vmem] * 4,
        out_specs=[vmem] * 6,
        compiler_params=pltpu.CompilerParams(vmem_limit_bytes=16 * 2**20),
    )(weight_first, weight_second, bias_first[None], bias_second[None])


def class_order():
    step = range(DILATION_STEP)
    uneven = [[(a, b), (b, a)] for a in step for b in step if a < b]
    return sum(uneven, []) + [(a, a) for a in step]


def part_kernel(tile_cols, tile, parts):
    step = DILATION_STEP
    part_cols = tile_cols // step
    part_rows = tile.shape[0] // (tile_cols * step)
    for index, (a, b) in enumerate(class_order()):
        columns = [
            tile[pl.ds(a * tile_cols + k * step + b, part_rows, stride=step * tile_cols), :]
            for k in range(part_cols)
        ]
        part = jnp.concatenate(columns, 0).astype(jnp.bfloat16)
        r, c = divmod(index, parts.shape[2])
        for half in range(HALVES):
            parts[r, half, c] = part


def class_parts(row_count, feature_map, cotangent):
    tile_rows, tile_cols, channels = feature_map.shape
    classes = DILATION_STEP * DILATION_STEP
    cells = tile_rows * tile_cols
    shape = (row_count, HALVES, classes // row_count, cells // classes, 2 * channels)
    tile = jnp.concatenate([feature_map, cotangent], 2).astype(jnp.float32)
    return pl.pallas_call(
        functools.partial(part_kernel, tile_cols),
        out_shape=jax.ShapeDtypeStruct(shape, jnp.bfloat16),
        in_specs=[pl.BlockSpec(memory_space=pltpu.VMEM)],
        out_specs=pl.BlockSpec(memory_space=pltpu.VMEM),
        compiler_params=pltpu.CompilerParams(vmem_limit_bytes=16 * 2**20),
    )(tile.reshape(cells, 2 * channels))


def class_kernel(
    row_count,
    part_cols,
    own,
    other,
    weight_first,
    weight_second,
    weight_third,
    weight_fourth,
    bias_first,
    bias_second,
    result,
    turning,
    window,
):
    blocks, part, width = own.shape
    channels = width // 2
    part_rows = part // part_cols
    col_count = blocks // row_count
    half_count = col_count // HALVES
    class_cols, class_rows = col_count * part_cols, row_count * part_rows
    share = class_cols // HALVES
    count = share + CONVS
    column = lax.axis_index("col")
    half = lax.div(column, half_count)
    place = lax.axis_index("row") * half_count + lax.rem(column, half_count)
    even = place >= len(class_order()) - DILATION_STEP
    begin = half * (share - CONVS)
    cells = count * class_rows
    low = lax.broadcasted_iota(jnp.int32, (cells, width), 1) < channels
    row = lax.rem(lax.broadcasted_iota(jnp.int32, (cells, width), 0), class_rows)

    pieces = []
    for r in range(row_count):
        reach = pl.ds(r * col_count + half * ((share - CONVS) // part_cols), count // part_cols)
        pieces.append(own[reach].reshape(count, part_rows, width))
    straight = jnp.concatenate(pieces, 1).astype(jnp.float32).reshape(cells, width)

    for r in range(row_count):
        reach = slice(r * col_count, (r + 1) * col_count)
        piece = jnp.where(even, own[reach], other[reach]).astype(jnp.float32)
        piece = piece.reshape(class_cols, part_rows, width)
        for k in range(class_cols):
            turning[pl.ds(k * class_rows + r * part_rows, part_rows), :] = piece[k]
    turned = jnp.concatenate(
        [turning[pl.ds(begin + i, class_cols, stride=class_rows), :] for i in range(count)], 0
    )

    def swapped(value):
        return pltpu.roll(value, channels, 1)

    def tap_sum(image, matrix, dimension):
        gap = jnp.zeros((class_rows, width), image.dtype)
        before = jnp.concatenate([gap, image[:-class_rows]], 0)
        after = jnp.concatenate([image[class_rows:], gap], 0)
        taps = lax.dot_general(
            jnp.concatenate([before, image, after], 1),
            matrix[...],
            (((1,), (dimension,)), ((), ())),
            preferred_element_type=jnp.float32,
        )
        above = jnp.where(row == 0, 0.0, pltpu.roll(taps[:, :width], 1, 0))
        below = pltpu.roll(taps[:, 2 * width :], cells - 1, 0)
        below = jnp.where(row == class_rows - 1, 0.0, below)
        return above + taps[:, width : 2 * width] + below

    symmetric = straight + turned
    symmetric = jnp.where(low, symmetric, swapped(symmetric)).astype(jnp.bfloat16)
    gradient = jnp.where(low, swapped(straight), turned)

    pre_first = tap_sum(symmetric, weight_first, 0) + bias_first[...]
    hidden = gelu_value(pre_first).astype(jnp.bfloat16)
    slope_first = gelu_slope(pre_first)
    pre_second = tap_sum(hidden, weight_second, 0) + bias_second[...]
    output = symmetric.astype(jnp.float32) + gelu_value(pre_second)
    grad_second = (gradient * gelu_slope(pre_second)).astype(jnp.bfloat16)
    grad_first = (tap_sum(grad_second, weight_third, 1) * slope_first).astype(jnp.bfloat16)
    grad_sym = (gradient + tap_sum(grad_first, weight_fourth, 1)).astype(jnp.bfloat16)
    grad_sym = grad_sym.astype(jnp.float32)
    finished = jnp.where(low, output, grad_sym + swapped(grad_sym)).astype(jnp.bfloat16)
    window[...] = finished.reshape(count, class_rows, width)

    for index, (a, b) in enumerate(class_order()):
        r, c = divmod(index, half_count)
        kept = window[pl.ds(half * CONVS + c * part_cols, part_cols)]
        kept = kept[:, r * part_rows : (r + 1) * part_rows]
        result[a * DILATION_STEP + b] = kept.reshape(part, width)


def class_chains(row_count, part_cols, own, other, *parameters):
    blocks, part, width = own.shape
    class_cols, class_rows = blocks // row_count * part_cols, row_count * (part // part_cols)
    count = class_cols // HALVES + CONVS
    return pl.pallas_call(
        functools.partial(class_kernel, row_count, part_cols),
        out_shape=jax.ShapeDtypeStruct((blocks // HALVES, part, width), jnp.bfloat16),
        in_specs=[pl.BlockSpec(memory_space=pltpu.VMEM)] * 8,
        out_specs=pl.BlockSpec(memory_space=pltpu.VMEM),
        scratch_shapes=[
            pltpu.VMEM((class_cols * class_rows, width), jnp.float32),
            pltpu.VMEM((count, class_rows, width), jnp.bfloat16),
        ],
        compiler_params=pltpu.CompilerParams(vmem_limit_bytes=32 * 2**20),
    )(own, other, *parameters)


def by_classes(feature_map, kernel_first, bias_first, kernel_second, bias_second, cotangent):
    row_count, col_count = lax.axis_size("row"), lax.axis_size("col")
    tile_rows, tile_cols, channels = feature_map.shape
    step = DILATION_STEP
    part_rows, part_cols = tile_rows // step, tile_cols // step

    parts = class_parts(row_count, feature_map, cotangent)
    parts = parts.reshape(row_count * col_count, part_cols * part_rows, 2 * channels)
    own = lax.all_to_all(parts, both, 0, 0, tiled=True)
    raw = (kernel_first, kernel_second, bias_first, bias_second)
    own, *raw = lax.optimization_barrier((own,) + raw)
    other = lax.ppermute(own, "col", [(i, i ^ 1) for i in range(col_count)])
    result = class_chains(row_count, part_cols, own, other, *chain_matrices(*raw))

    half_count = col_count // HALVES
    order = sorted(range(step * step), key=lambda index: class_order()[index])
    halves = [
        [i // half_count * col_count + h * half_count + i % half_count for i in order]
        for h in range(HALVES)
    ]
    back = lax.all_to_all(result, both, 0, 0, axis_index_groups=halves, tiled=True)
    back = back.reshape(step, step, part_cols, part_rows, 2 * channels)
    back = jnp.transpose(back, (3, 0, 2, 1, 4)).reshape(tile_rows, tile_cols, 2 * channels)
    return back[..., :channels], back[..., channels:]


def solution(mesh):
    row_count, col_count = mesh.shape["row"], mesh.shape["col"]
    classes = DILATION_STEP * DILATION_STEP
    paired = row_count * col_count == HALVES * classes and col_count % (2 * HALVES) == 0
    in_specs = (P("row", "col", None), P(), P(), P(), P(), P("row", "col", None))
    out_specs = (P("row", "col", None), P("row", "col", None))

    def whole(feature_map, *others):
        size = feature_map.shape[0]
        part_rows, part_cols = size // row_count // DILATION_STEP, size // col_count // DILATION_STEP
        fits = size % (DILATION_STEP * row_count) == 0 and size % (DILATION_STEP * col_count) == 0
        fits = fits and part_rows % 16 == 0 and CONVS % part_cols == 0
        per_device = by_classes if paired and fits else by_tiles
        return jax.shard_map(
            per_device, mesh=mesh, in_specs=in_specs, out_specs=out_specs, check_vma=False
        )(feature_map, *others)

    return whole
```

```python
import functools

import jax
import jax.numpy as jnp
from jax import lax
from jax.experimental import pallas as pl
from jax.experimental.pallas import tpu as pltpu
from jax.sharding import PartitionSpec as P

DILATION_STEP = 4
HALVES = 2
CONVS = 4


root_half = 0.7071067811865476
inv_root_tau = 0.3989422804014327
both = ("row", "col")


def with_halo(array, sides, width):
    for axis, dim in sides:
        size, length = (lax.axis_size(axis), array.shape[dim])
        up = [(i, (i + 1) % size) for i in range(size - 1)]
        down = [(j, i) for i, j in up]
        last = lax.slice_in_dim(array, length - width, length, axis=dim)
        first = lax.slice_in_dim(array, 0, width, axis=dim)
        before = lax.ppermute(last, axis, up)
        after = lax.ppermute(first, axis, down)
        array = jnp.concatenate([before, array, after], axis=dim)
    return array


def gelu_value(value_array):
    return 0.5 * value_array * (1.0 + lax.erf(value_array * root_half))


def gelu_slope(value_array):
    return (
        0.5 * (1.0 + lax.erf(value_array * root_half))
        + value_array * jnp.exp(-0.5 * value_array * value_array) * inv_root_tau
    )


def gelu_pair(value_array):
    share = 0.5 + 0.5 * lax.erf(value_array * root_half)
    bell = jnp.exp(-0.5 * value_array * value_array) * inv_root_tau
    return value_array * share, share + value_array * bell


def conv(padded_input, conv_kernel, step):
    return lax.conv_general_dilated(
        padded_input[None],
        conv_kernel,
        (1, 1),
        "VALID",
        rhs_dilation=(step, step),
        dimension_numbers=("NHWC", "HWIO", "NHWC"),
        preferred_element_type=jnp.float32,
    )[0]


def dilated_conv(padded_input, conv_kernel):
    return conv(padded_input, conv_kernel, DILATION_STEP)


def reversed_kernel(conv_kernel):
    return jnp.transpose(conv_kernel[::-1, ::-1], (0, 1, 3, 2))


def extend(value_array):
    return with_halo(value_array, (("row", 0), ("col", 1)), DILATION_STEP)


def mirror(tile):
    row_count = lax.axis_size("row")
    col_count = lax.axis_size("col")
    tile_rows, tile_cols, channels = tile.shape
    unit_len = tile_rows // col_count
    col_ratio = col_count // row_count
    spread_parts = tile.reshape(1, 1, col_ratio, row_count, unit_len, tile_cols * channels)
    spread_parts = lax.all_to_all(spread_parts, "row", split_axis=3, concat_axis=1, tiled=True)
    across_parts = spread_parts.reshape(1, col_count, unit_len, 1, tile_cols * channels)
    across_parts = lax.all_to_all(across_parts, "col", split_axis=1, concat_axis=3, tiled=True)
    settle_parts = across_parts.reshape(1, 1, unit_len, row_count, tile_rows * channels)
    settle_parts = lax.all_to_all(settle_parts, "row", split_axis=3, concat_axis=1, tiled=True)
    turned = settle_parts.reshape(tile_cols, tile_rows, channels)
    return jnp.transpose(turned, (1, 0, 2))


def add_rounded(first, second):
    return (first.astype(jnp.float32) + second.astype(jnp.float32)).astype(jnp.bfloat16)


def by_tiles(feature_map, kernel_first, bias_first, kernel_second, bias_second, cotangent):
    symmetric = add_rounded(feature_map, mirror(feature_map))
    pre_first = dilated_conv(extend(symmetric), kernel_first) + bias_first
    hidden = gelu_value(pre_first).astype(jnp.bfloat16)
    pre_second = dilated_conv(extend(hidden), kernel_second) + bias_second
    output = (symmetric.astype(jnp.float32) + gelu_value(pre_second)).astype(jnp.bfloat16)
    grad_second = (cotangent.astype(jnp.float32) * gelu_slope(pre_second)).astype(jnp.bfloat16)
    hidden_gradient = dilated_conv(extend(grad_second), reversed_kernel(kernel_second))
    grad_first = (hidden_gradient * gelu_slope(pre_first)).astype(jnp.bfloat16)
    total_sum = cotangent.astype(jnp.float32) + dilated_conv(
        extend(grad_first), reversed_kernel(kernel_first)
    )
    grad_sym = total_sum.astype(jnp.bfloat16)
    return output, add_rounded(grad_sym, mirror(grad_sym))


def matrix_kernel(weight_first, weight_second, bias_first, bias_second, *outputs):
    first, second, third, fourth, first_bias, second_bias = outputs
    taps, channels = weight_first.shape[0], weight_first.shape[2]
    gap = jnp.zeros(weight_first.shape[2:], weight_first.dtype)
    for weight, ahead, behind in (
        (weight_first, first, fourth),
        (weight_second, second, third),
    ):
        for p in range(taps):
            for q in range(taps):
                upper = jnp.concatenate([weight[q, p], gap], 1)
                lower = jnp.concatenate([gap, weight[p, q]], 1)
                block = jnp.concatenate([upper, lower], 0)
                columns = pl.ds(2 * channels * q, 2 * channels)
                if ahead is second:
                    ahead[pl.ds(2 * channels * p, 2 * channels), columns] = block
                else:
                    joint = jnp.concatenate([weight[q, p], weight[p, q]], 1)
                    ahead[pl.ds(channels * p, channels), columns] = joint
                p_back, q_back = taps - 1 - p, taps - 1 - q
                behind[
                    pl.ds(2 * channels * q_back, 2 * channels),
                    pl.ds(2 * channels * p_back, 2 * channels),
                ] = block
    rest = slice(taps * channels, first.shape[0])
    first[rest] = jnp.zeros_like(first[rest])
    for bias, wide in ((bias_first, first_bias), (bias_second, second_bias)):
        wide[...] = jnp.concatenate([bias[...], bias[...]], 1)


def chain_matrices(weight_first, weight_second, bias_first, bias_second):
    taps, channels = weight_first.shape[0], weight_first.shape[2]
    size = taps * 2 * channels
    vmem = pl.BlockSpec(memory_space=pltpu.VMEM)
    return pl.pallas_call(
        matrix_kernel,
        out_shape=[
            jax.ShapeDtypeStruct(((taps + 1) * channels, size), jnp.bfloat16),
            *[jax.ShapeDtypeStruct((size, size), jnp.bfloat16)] * 3,
        ]
        + [jax.ShapeDtypeStruct((1, 2 * channels), jnp.float32)] * 2,
        in_specs=[vmem] * 4,
        out_specs=[vmem] * 6,
        compiler_params=pltpu.CompilerParams(vmem_limit_bytes=16 * 2**20),
    )(weight_first, weight_second, bias_first[None], bias_second[None])


def class_order():
    step = range(DILATION_STEP)
    uneven = [[(a, b), (b, a)] for a in step for b in step if a < b]
    return sum(uneven, []) + [(a, a) for a in step]


def part_kernel(tile_cols, tile, parts):
    step = DILATION_STEP
    part_cols = tile_cols // step
    part_rows = tile.shape[0] // (tile_cols * step)
    for index, (a, b) in enumerate(class_order()):
        columns = [
            tile[pl.ds(a * tile_cols + k * step + b, part_rows, stride=step * tile_cols), :]
            for k in range(part_cols)
        ]
        part = jnp.concatenate(columns, 0).astype(jnp.bfloat16)
        r, c = divmod(index, parts.shape[2])
        for half in range(HALVES):
            parts[r, half, c] = part


def class_parts(row_count, feature_map, cotangent):
    tile_rows, tile_cols, channels = feature_map.shape
    classes = DILATION_STEP * DILATION_STEP
    cells = tile_rows * tile_cols
    shape = (row_count, HALVES, classes // row_count, cells // classes, 2 * channels)
    tile = jnp.concatenate([feature_map, cotangent], 2).astype(jnp.float32)
    return pl.pallas_call(
        functools.partial(part_kernel, tile_cols),
        out_shape=jax.ShapeDtypeStruct(shape, jnp.bfloat16),
        in_specs=[pl.BlockSpec(memory_space=pltpu.VMEM)],
        out_specs=pl.BlockSpec(memory_space=pltpu.VMEM),
        compiler_params=pltpu.CompilerParams(vmem_limit_bytes=16 * 2**20),
    )(tile.reshape(cells, 2 * channels))


def class_kernel(
    row_count,
    part_cols,
    own,
    other,
    weight_first,
    weight_second,
    weight_third,
    weight_fourth,
    bias_first,
    bias_second,
    result,
    turning,
    window,
):
    blocks, part, width = own.shape
    channels = width // 2
    part_rows = part // part_cols
    col_count = blocks // row_count
    half_count = col_count // HALVES
    class_cols, class_rows = col_count * part_cols, row_count * part_rows
    share = class_cols // HALVES
    count = share + CONVS
    column = lax.axis_index("col")
    half = lax.div(column, half_count)
    place = lax.axis_index("row") * half_count + lax.rem(column, half_count)
    even = place >= len(class_order()) - DILATION_STEP
    begin = half * (share - CONVS)
    cells = count * class_rows
    low = lax.broadcasted_iota(jnp.int32, (cells, width), 1) < channels
    row = lax.broadcasted_iota(jnp.int32, (1, class_rows, width), 1)

    pieces = []
    for r in range(row_count):
        reach = pl.ds(r * col_count + half * ((share - CONVS) // part_cols), count // part_cols)
        pieces.append(own[reach].reshape(count, part_rows, width))
    straight = jnp.concatenate(pieces, 1).astype(jnp.float32).reshape(cells, width)

    for r in range(row_count):
        reach = slice(r * col_count, (r + 1) * col_count)
        piece = jnp.where(even, own[reach], other[reach]).astype(jnp.float32)
        piece = piece.reshape(class_cols, part_rows, width)
        for k in range(class_cols):
            turning[pl.ds(k * class_rows + r * part_rows, part_rows), :] = piece[k]
    turned = jnp.concatenate(
        [turning[pl.ds(begin + i, class_cols, stride=class_rows), :] for i in range(count)], 0
    )

    def swapped(value):
        return pltpu.roll(value, channels, 1)

    chunks = 2
    size = cells // chunks
    rows = [slice(k * size, (k + 1) * size) for k in range(chunks)]
    low = low[:size]

    def tap_sum(images, k, matrix, dimension, doubled=False):
        gap = jnp.zeros((class_rows, width), jnp.bfloat16)
        image = images[k]
        before = images[k - 1][-class_rows:] if k else gap
        before = jnp.concatenate([before, image[:-class_rows]], 0)
        after = images[k + 1][:class_rows] if k + 1 < chunks else gap
        after = jnp.concatenate([image[class_rows:], after], 0)
        columns = [jnp.where(low, before, image), after] if doubled else [before, image, after]
        taps = lax.dot_general(
            jnp.concatenate(columns, 1),
            matrix[...],
            (((1,), (dimension,)), ((), ())),
            preferred_element_type=jnp.float32,
        )
        taps = taps.reshape(count // chunks, class_rows, 3 * width)
        above = jnp.where(row == 0, 0.0, pltpu.roll(taps[:, :, :width], 1, 1))
        below = pltpu.roll(taps[:, :, 2 * width :], class_rows - 1, 1)
        below = jnp.where(row == class_rows - 1, 0.0, below)
        return (above + taps[:, :, width : 2 * width] + below).reshape(size, width)

    symmetric, gradient = [], []
    for k in range(chunks):
        total = straight[rows[k]] + turned[rows[k]]
        symmetric.append(jnp.where(low, total, swapped(total)).astype(jnp.bfloat16))
        gradient.append(jnp.where(low, swapped(straight[rows[k]]), turned[rows[k]]))

    hidden, slope_first = [], []
    for k in range(chunks):
        pre_first = tap_sum(symmetric, k, weight_first, 0, True) + bias_first[...]
        value, slope = gelu_pair(pre_first)
        hidden.append(value.astype(jnp.bfloat16))
        slope_first.append(slope)
    output, grad_second = [], []
    for k in range(chunks):
        pre_second = tap_sum(hidden, k, weight_second, 0) + bias_second[...]
        value, slope = gelu_pair(pre_second)
        output.append(symmetric[k].astype(jnp.float32) + value)
        grad_second.append((gradient[k] * slope).astype(jnp.bfloat16))
    grad_first = [
        (tap_sum(grad_second, k, weight_third, 1) * slope_first[k]).astype(jnp.bfloat16)
        for k in range(chunks)
    ]
    for k in range(chunks):
        grad_sym = (gradient[k] + tap_sum(grad_first, k, weight_fourth, 1)).astype(jnp.bfloat16)
        grad_sym = grad_sym.astype(jnp.float32)
        finished = jnp.where(low, output[k], grad_sym + swapped(grad_sym)).astype(jnp.bfloat16)
        share_cols = count // chunks
        window[k * share_cols : (k + 1) * share_cols] = finished.reshape(share_cols, class_rows, width)

    for index, (a, b) in enumerate(class_order()):
        r, c = divmod(index, half_count)
        kept = window[pl.ds(half * CONVS + c * part_cols, part_cols)]
        kept = kept[:, r * part_rows : (r + 1) * part_rows]
        result[a * DILATION_STEP + b] = kept.reshape(part, width)


def class_chains(row_count, part_cols, own, other, *parameters):
    blocks, part, width = own.shape
    class_cols, class_rows = blocks // row_count * part_cols, row_count * (part // part_cols)
    count = class_cols // HALVES + CONVS
    return pl.pallas_call(
        functools.partial(class_kernel, row_count, part_cols),
        out_shape=jax.ShapeDtypeStruct((blocks // HALVES, part, width), jnp.bfloat16),
        in_specs=[pl.BlockSpec(memory_space=pltpu.VMEM)] * 8,
        out_specs=pl.BlockSpec(memory_space=pltpu.VMEM),
        scratch_shapes=[
            pltpu.VMEM((class_cols * class_rows, width), jnp.float32),
            pltpu.VMEM((count, class_rows, width), jnp.bfloat16),
        ],
        compiler_params=pltpu.CompilerParams(vmem_limit_bytes=32 * 2**20),
    )(own, other, *parameters)


def by_classes(feature_map, kernel_first, bias_first, kernel_second, bias_second, cotangent):
    row_count, col_count = lax.axis_size("row"), lax.axis_size("col")
    tile_rows, tile_cols, channels = feature_map.shape
    step = DILATION_STEP
    part_rows, part_cols = tile_rows // step, tile_cols // step

    parts = class_parts(row_count, feature_map, cotangent)
    parts = parts.reshape(row_count * col_count, part_cols * part_rows, 2 * channels)
    own = lax.all_to_all(parts, both, 0, 0, tiled=True)
    raw = (kernel_first, kernel_second, bias_first, bias_second)
    own, *raw = lax.optimization_barrier((own,) + raw)
    other = lax.ppermute(own, "col", [(i, i ^ 1) for i in range(col_count)])
    result = class_chains(row_count, part_cols, own, other, *chain_matrices(*raw))

    half_count = col_count // HALVES
    order = sorted(range(step * step), key=lambda index: class_order()[index])
    halves = [
        [i // half_count * col_count + h * half_count + i % half_count for i in order]
        for h in range(HALVES)
    ]
    back = lax.all_to_all(result, both, 0, 0, axis_index_groups=halves, tiled=True)
    back = back.reshape(step, step, part_cols, part_rows, 2 * channels)
    back = jnp.transpose(back, (3, 0, 2, 1, 4)).reshape(tile_rows, tile_cols, 2 * channels)
    return back[..., :channels], back[..., channels:]


def solution(mesh):
    row_count, col_count = mesh.shape["row"], mesh.shape["col"]
    classes = DILATION_STEP * DILATION_STEP
    paired = row_count * col_count == HALVES * classes and col_count % (2 * HALVES) == 0
    in_specs = (P("row", "col", None), P(), P(), P(), P(), P("row", "col", None))
    out_specs = (P("row", "col", None), P("row", "col", None))

    def whole(feature_map, *others):
        size = feature_map.shape[0]
        part_rows, part_cols = size // row_count // DILATION_STEP, size // col_count // DILATION_STEP
        fits = size % (DILATION_STEP * row_count) == 0 and size % (DILATION_STEP * col_count) == 0
        fits = fits and part_rows % 16 == 0 and CONVS % part_cols == 0
        per_device = by_classes if paired and fits else by_tiles
        return jax.shard_map(
            per_device, mesh=mesh, in_specs=in_specs, out_specs=out_specs, check_vma=False
        )(feature_map, *others)

    return whole
```

```python
import functools

import jax
import jax.numpy as jnp
from jax import lax
from jax.experimental import pallas as pl
from jax.experimental.pallas import tpu as pltpu
from jax.sharding import PartitionSpec as P

DILATION_STEP = 4
HALVES = 2
CONVS = 4


root_half = 0.7071067811865476
inv_root_tau = 0.3989422804014327
both = ("row", "col")


def with_halo(array, sides, width):
    for axis, dim in sides:
        size, length = (lax.axis_size(axis), array.shape[dim])
        up = [(i, (i + 1) % size) for i in range(size - 1)]
        down = [(j, i) for i, j in up]
        last = lax.slice_in_dim(array, length - width, length, axis=dim)
        first = lax.slice_in_dim(array, 0, width, axis=dim)
        before = lax.ppermute(last, axis, up)
        after = lax.ppermute(first, axis, down)
        array = jnp.concatenate([before, array, after], axis=dim)
    return array


def gelu_value(value_array):
    return 0.5 * value_array * (1.0 + lax.erf(value_array * root_half))


def gelu_slope(value_array):
    return (
        0.5 * (1.0 + lax.erf(value_array * root_half))
        + value_array * jnp.exp(-0.5 * value_array * value_array) * inv_root_tau
    )


def gelu_pair(value_array):
    share = 0.5 + 0.5 * lax.erf(value_array * root_half)
    bell = jnp.exp(-0.5 * value_array * value_array) * inv_root_tau
    return value_array * share, share + value_array * bell


def conv(padded_input, conv_kernel, step):
    return lax.conv_general_dilated(
        padded_input[None],
        conv_kernel,
        (1, 1),
        "VALID",
        rhs_dilation=(step, step),
        dimension_numbers=("NHWC", "HWIO", "NHWC"),
        preferred_element_type=jnp.float32,
    )[0]


def dilated_conv(padded_input, conv_kernel):
    return conv(padded_input, conv_kernel, DILATION_STEP)


def reversed_kernel(conv_kernel):
    return jnp.transpose(conv_kernel[::-1, ::-1], (0, 1, 3, 2))


def extend(value_array):
    return with_halo(value_array, (("row", 0), ("col", 1)), DILATION_STEP)


def mirror(tile):
    row_count = lax.axis_size("row")
    col_count = lax.axis_size("col")
    tile_rows, tile_cols, channels = tile.shape
    unit_len = tile_rows // col_count
    col_ratio = col_count // row_count
    spread_parts = tile.reshape(1, 1, col_ratio, row_count, unit_len, tile_cols * channels)
    spread_parts = lax.all_to_all(spread_parts, "row", split_axis=3, concat_axis=1, tiled=True)
    across_parts = spread_parts.reshape(1, col_count, unit_len, 1, tile_cols * channels)
    across_parts = lax.all_to_all(across_parts, "col", split_axis=1, concat_axis=3, tiled=True)
    settle_parts = across_parts.reshape(1, 1, unit_len, row_count, tile_rows * channels)
    settle_parts = lax.all_to_all(settle_parts, "row", split_axis=3, concat_axis=1, tiled=True)
    turned = settle_parts.reshape(tile_cols, tile_rows, channels)
    return jnp.transpose(turned, (1, 0, 2))


def add_rounded(first, second):
    return (first.astype(jnp.float32) + second.astype(jnp.float32)).astype(jnp.bfloat16)


def by_tiles(feature_map, kernel_first, bias_first, kernel_second, bias_second, cotangent):
    symmetric = add_rounded(feature_map, mirror(feature_map))
    pre_first = dilated_conv(extend(symmetric), kernel_first) + bias_first
    hidden = gelu_value(pre_first).astype(jnp.bfloat16)
    pre_second = dilated_conv(extend(hidden), kernel_second) + bias_second
    output = (symmetric.astype(jnp.float32) + gelu_value(pre_second)).astype(jnp.bfloat16)
    grad_second = (cotangent.astype(jnp.float32) * gelu_slope(pre_second)).astype(jnp.bfloat16)
    hidden_gradient = dilated_conv(extend(grad_second), reversed_kernel(kernel_second))
    grad_first = (hidden_gradient * gelu_slope(pre_first)).astype(jnp.bfloat16)
    total_sum = cotangent.astype(jnp.float32) + dilated_conv(
        extend(grad_first), reversed_kernel(kernel_first)
    )
    grad_sym = total_sum.astype(jnp.bfloat16)
    return output, add_rounded(grad_sym, mirror(grad_sym))


def matrix_kernel(weight_first, weight_second, bias_first, bias_second, *outputs):
    first, second, third, fourth, first_bias, second_bias = outputs
    taps, channels = weight_first.shape[0], weight_first.shape[2]
    gap = jnp.zeros(weight_first.shape[2:], weight_first.dtype)
    for weight, ahead, behind in (
        (weight_first, first, fourth),
        (weight_second, second, third),
    ):
        for p in range(taps):
            for q in range(taps):
                upper = jnp.concatenate([weight[q, p], gap], 1)
                lower = jnp.concatenate([gap, weight[p, q]], 1)
                block = jnp.concatenate([upper, lower], 0)
                columns = pl.ds(2 * channels * q, 2 * channels)
                if ahead is second:
                    ahead[pl.ds(2 * channels * p, 2 * channels), columns] = block
                else:
                    joint = jnp.concatenate([weight[q, p], weight[p, q]], 1)
                    ahead[pl.ds(channels * p, channels), columns] = joint
                p_back, q_back = taps - 1 - p, taps - 1 - q
                behind[
                    pl.ds(2 * channels * q_back, 2 * channels),
                    pl.ds(2 * channels * p_back, 2 * channels),
                ] = block
    rest = slice(taps * channels, first.shape[0])
    first[rest] = jnp.zeros_like(first[rest])
    for bias, wide in ((bias_first, first_bias), (bias_second, second_bias)):
        wide[...] = jnp.concatenate([bias[...], bias[...]], 1)


def chain_matrices(weight_first, weight_second, bias_first, bias_second):
    taps, channels = weight_first.shape[0], weight_first.shape[2]
    size = taps * 2 * channels
    vmem = pl.BlockSpec(memory_space=pltpu.VMEM)
    return pl.pallas_call(
        matrix_kernel,
        out_shape=[
            jax.ShapeDtypeStruct(((taps + 1) * channels, size), jnp.bfloat16),
            *[jax.ShapeDtypeStruct((size, size), jnp.bfloat16)] * 3,
        ]
        + [jax.ShapeDtypeStruct((1, 2 * channels), jnp.float32)] * 2,
        in_specs=[vmem] * 4,
        out_specs=[vmem] * 6,
        compiler_params=pltpu.CompilerParams(vmem_limit_bytes=16 * 2**20),
    )(weight_first, weight_second, bias_first[None], bias_second[None])


def class_order():
    step = range(DILATION_STEP)
    uneven = [[(a, b), (b, a)] for a in step for b in step if a < b]
    return sum(uneven, []) + [(a, a) for a in step]


def part_kernel(tile_cols, tile, parts):
    step = DILATION_STEP
    part_cols = tile_cols // step
    part_rows = tile.shape[0] // (tile_cols * step)
    for index, (a, b) in enumerate(class_order()):
        columns = [
            tile[pl.ds(a * tile_cols + k * step + b, part_rows, stride=step * tile_cols), :]
            for k in range(part_cols)
        ]
        part = jnp.concatenate(columns, 0).astype(jnp.bfloat16)
        r, c = divmod(index, parts.shape[2])
        for half in range(HALVES):
            parts[r, half, c] = part


def class_parts(row_count, feature_map, cotangent):
    tile_rows, tile_cols, channels = feature_map.shape
    classes = DILATION_STEP * DILATION_STEP
    cells = tile_rows * tile_cols
    shape = (row_count, HALVES, classes // row_count, cells // classes, 2 * channels)
    tile = jnp.concatenate([feature_map, cotangent], 2).astype(jnp.float32)
    return pl.pallas_call(
        functools.partial(part_kernel, tile_cols),
        out_shape=jax.ShapeDtypeStruct(shape, jnp.bfloat16),
        in_specs=[pl.BlockSpec(memory_space=pltpu.VMEM)],
        out_specs=pl.BlockSpec(memory_space=pltpu.VMEM),
        compiler_params=pltpu.CompilerParams(vmem_limit_bytes=16 * 2**20),
    )(tile.reshape(cells, 2 * channels))


def class_kernel(
    row_count,
    part_cols,
    own,
    other,
    weight_first,
    weight_second,
    weight_third,
    weight_fourth,
    bias_first,
    bias_second,
    result,
    turning,
    window,
):
    blocks, part, width = own.shape
    channels = width // 2
    part_rows = part // part_cols
    col_count = blocks // row_count
    half_count = col_count // HALVES
    class_cols, class_rows = col_count * part_cols, row_count * part_rows
    share = class_cols // HALVES
    count = share + CONVS
    column = lax.axis_index("col")
    half = lax.div(column, half_count)
    place = lax.axis_index("row") * half_count + lax.rem(column, half_count)
    even = place >= len(class_order()) - DILATION_STEP
    begin = half * (share - CONVS)
    cells = count * class_rows
    low = lax.broadcasted_iota(jnp.int32, (cells, width), 1) < channels
    row = lax.broadcasted_iota(jnp.int32, (1, class_rows, width), 1)

    pieces = []
    for r in range(row_count):
        reach = pl.ds(r * col_count + half * ((share - CONVS) // part_cols), count // part_cols)
        pieces.append(own[reach].reshape(count, part_rows, width))
    straight = jnp.concatenate(pieces, 1).astype(jnp.float32).reshape(cells, width)

    for r in range(row_count):
        reach = slice(r * col_count, (r + 1) * col_count)
        piece = jnp.where(even, own[reach], other[reach]).astype(jnp.float32)
        piece = piece.reshape(class_cols, part_rows, width)
        for k in range(class_cols):
            turning[pl.ds(k * class_rows + r * part_rows, part_rows), :] = piece[k]
    turned = jnp.concatenate(
        [turning[pl.ds(begin + i, class_cols, stride=class_rows), :] for i in range(count)], 0
    )

    def swapped(value):
        return pltpu.roll(value, channels, 1)

    chunks = 2
    size = cells // chunks
    rows = [slice(k * size, (k + 1) * size) for k in range(chunks)]
    low = low[:size]

    def tap_sum(images, k, matrix, dimension, doubled=False):
        gap = jnp.zeros((class_rows, width), jnp.bfloat16)
        image = images[k]
        before = images[k - 1][-class_rows:] if k else gap
        before = jnp.concatenate([before, image[:-class_rows]], 0)
        after = images[k + 1][:class_rows] if k + 1 < chunks else gap
        after = jnp.concatenate([image[class_rows:], after], 0)
        columns = [jnp.where(low, before, image), after] if doubled else [before, image, after]
        taps = lax.dot_general(
            jnp.concatenate(columns, 1),
            matrix[...],
            (((1,), (dimension,)), ((), ())),
            preferred_element_type=jnp.float32,
        )
        taps = taps.reshape(count // chunks, class_rows, 3 * width)
        above = jnp.where(row == 0, 0.0, pltpu.roll(taps[:, :, :width], 1, 1))
        below = pltpu.roll(taps[:, :, 2 * width :], class_rows - 1, 1)
        below = jnp.where(row == class_rows - 1, 0.0, below)
        return (above + taps[:, :, width : 2 * width] + below).reshape(size, width)

    symmetric, gradient = [], []
    for k in range(chunks):
        total = straight[rows[k]] + turned[rows[k]]
        symmetric.append(jnp.where(low, total, swapped(total)).astype(jnp.bfloat16))
        gradient.append(jnp.where(low, swapped(straight[rows[k]]), turned[rows[k]]))

    hidden, slope_first = [], []
    for k in range(chunks):
        pre_first = tap_sum(symmetric, k, weight_first, 0, True) + bias_first[...]
        value, slope = gelu_pair(pre_first)
        hidden.append(value.astype(jnp.bfloat16))
        slope_first.append(slope)
    output, grad_second = [], []
    for k in range(chunks):
        pre_second = tap_sum(hidden, k, weight_second, 0) + bias_second[...]
        value, slope = gelu_pair(pre_second)
        output.append(symmetric[k].astype(jnp.float32) + value)
        grad_second.append((gradient[k] * slope).astype(jnp.bfloat16))
    grad_first = [
        (tap_sum(grad_second, k, weight_third, 1) * slope_first[k]).astype(jnp.bfloat16)
        for k in range(chunks)
    ]
    for k in range(chunks):
        grad_sym = (gradient[k] + tap_sum(grad_first, k, weight_fourth, 1)).astype(jnp.bfloat16)
        grad_sym = grad_sym.astype(jnp.float32)
        finished = jnp.where(low, output[k], grad_sym + swapped(grad_sym)).astype(jnp.bfloat16)
        share_cols = count // chunks
        window[k * share_cols : (k + 1) * share_cols] = finished.reshape(share_cols, class_rows, width)

    classes = result.shape[0]
    for index in range(classes):
        r, c = divmod(index, half_count)
        kept = window[pl.ds(half * CONVS + c * part_cols, part_cols)]
        kept = kept[:, r * part_rows : (r + 1) * part_rows]
        result[classes - 1 - index] = kept.reshape(part, width)


def class_chains(row_count, part_cols, own, other, *parameters):
    blocks, part, width = own.shape
    class_cols, class_rows = blocks // row_count * part_cols, row_count * (part // part_cols)
    count = class_cols // HALVES + CONVS
    return pl.pallas_call(
        functools.partial(class_kernel, row_count, part_cols),
        out_shape=jax.ShapeDtypeStruct((blocks // HALVES, part, width), jnp.bfloat16),
        in_specs=[pl.BlockSpec(memory_space=pltpu.VMEM)] * 8,
        out_specs=pl.BlockSpec(memory_space=pltpu.VMEM),
        scratch_shapes=[
            pltpu.VMEM((class_cols * class_rows, width), jnp.float32),
            pltpu.VMEM((count, class_rows, width), jnp.bfloat16),
        ],
        compiler_params=pltpu.CompilerParams(vmem_limit_bytes=32 * 2**20),
    )(own, other, *parameters)


def by_classes(feature_map, kernel_first, bias_first, kernel_second, bias_second, cotangent):
    row_count, col_count = lax.axis_size("row"), lax.axis_size("col")
    tile_rows, tile_cols, channels = feature_map.shape
    step = DILATION_STEP
    part_rows, part_cols = tile_rows // step, tile_cols // step

    parts = class_parts(row_count, feature_map, cotangent)
    parts = parts.reshape(row_count * col_count, part_cols * part_rows, 2 * channels)
    own = lax.all_to_all(parts, both, 0, 0, tiled=True)
    raw = (kernel_first, kernel_second, bias_first, bias_second)
    own, *raw = lax.optimization_barrier((own,) + raw)
    other = lax.ppermute(own, "col", [(i, i ^ 1) for i in range(col_count)])
    result = class_chains(row_count, part_cols, own, other, *chain_matrices(*raw))

    half_count, classes = col_count // HALVES, step * step
    halves = [
        [i // half_count * col_count + h * half_count + i % half_count for i in range(classes)][::-1]
        for h in range(HALVES)
    ]
    back = lax.all_to_all(result, both, 0, 0, axis_index_groups=halves, tiled=True)
    order = sorted(range(classes), key=lambda index: class_order()[index])
    back = jnp.concatenate([back[classes - 1 - i : classes - i] for i in order], 0)
    back = back.reshape(step, step, part_cols, part_rows, 2 * channels)
    back = jnp.transpose(back, (3, 0, 2, 1, 4)).reshape(tile_rows, tile_cols, 2 * channels)
    return back[..., :channels], back[..., channels:]


def solution(mesh):
    row_count, col_count = mesh.shape["row"], mesh.shape["col"]
    classes = DILATION_STEP * DILATION_STEP
    paired = row_count * col_count == HALVES * classes and col_count % (2 * HALVES) == 0
    in_specs = (P("row", "col", None), P(), P(), P(), P(), P("row", "col", None))
    out_specs = (P("row", "col", None), P("row", "col", None))

    def whole(feature_map, *others):
        size = feature_map.shape[0]
        part_rows, part_cols = size // row_count // DILATION_STEP, size // col_count // DILATION_STEP
        fits = size % (DILATION_STEP * row_count) == 0 and size % (DILATION_STEP * col_count) == 0
        fits = fits and part_rows % 16 == 0 and CONVS % part_cols == 0
        per_device = by_classes if paired and fits else by_tiles
        return jax.shard_map(
            per_device, mesh=mesh, in_specs=in_specs, out_specs=out_specs, check_vma=False
        )(feature_map, *others)

    return whole
```

```python
import functools

import jax
import jax.numpy as jnp
from jax import lax
from jax.experimental import pallas as pl
from jax.experimental.pallas import tpu as pltpu
from jax.sharding import PartitionSpec as P

DILATION_STEP = 4
HALVES = 2
CONVS = 4


root_half = 0.7071067811865476
inv_root_tau = 0.3989422804014327
both = ("row", "col")


def with_halo(array, sides, width):
    for axis, dim in sides:
        size, length = (lax.axis_size(axis), array.shape[dim])
        up = [(i, (i + 1) % size) for i in range(size - 1)]
        down = [(j, i) for i, j in up]
        last = lax.slice_in_dim(array, length - width, length, axis=dim)
        first = lax.slice_in_dim(array, 0, width, axis=dim)
        before = lax.ppermute(last, axis, up)
        after = lax.ppermute(first, axis, down)
        array = jnp.concatenate([before, array, after], axis=dim)
    return array


def gelu_value(value_array):
    return 0.5 * value_array * (1.0 + lax.erf(value_array * root_half))


def gelu_slope(value_array):
    return (
        0.5 * (1.0 + lax.erf(value_array * root_half))
        + value_array * jnp.exp(-0.5 * value_array * value_array) * inv_root_tau
    )


def gelu_pair(value_array):
    share = 0.5 + 0.5 * lax.erf(value_array * root_half)
    bell = jnp.exp(-0.5 * value_array * value_array) * inv_root_tau
    return value_array * share, share + value_array * bell


def conv(padded_input, conv_kernel, step):
    return lax.conv_general_dilated(
        padded_input[None],
        conv_kernel,
        (1, 1),
        "VALID",
        rhs_dilation=(step, step),
        dimension_numbers=("NHWC", "HWIO", "NHWC"),
        preferred_element_type=jnp.float32,
    )[0]


def dilated_conv(padded_input, conv_kernel):
    return conv(padded_input, conv_kernel, DILATION_STEP)


def reversed_kernel(conv_kernel):
    return jnp.transpose(conv_kernel[::-1, ::-1], (0, 1, 3, 2))


def extend(value_array):
    return with_halo(value_array, (("row", 0), ("col", 1)), DILATION_STEP)


def mirror(tile):
    row_count = lax.axis_size("row")
    col_count = lax.axis_size("col")
    tile_rows, tile_cols, channels = tile.shape
    unit_len = tile_rows // col_count
    col_ratio = col_count // row_count
    spread_parts = tile.reshape(1, 1, col_ratio, row_count, unit_len, tile_cols * channels)
    spread_parts = lax.all_to_all(spread_parts, "row", split_axis=3, concat_axis=1, tiled=True)
    across_parts = spread_parts.reshape(1, col_count, unit_len, 1, tile_cols * channels)
    across_parts = lax.all_to_all(across_parts, "col", split_axis=1, concat_axis=3, tiled=True)
    settle_parts = across_parts.reshape(1, 1, unit_len, row_count, tile_rows * channels)
    settle_parts = lax.all_to_all(settle_parts, "row", split_axis=3, concat_axis=1, tiled=True)
    turned = settle_parts.reshape(tile_cols, tile_rows, channels)
    return jnp.transpose(turned, (1, 0, 2))


def add_rounded(first, second):
    return (first.astype(jnp.float32) + second.astype(jnp.float32)).astype(jnp.bfloat16)


def by_tiles(feature_map, kernel_first, bias_first, kernel_second, bias_second, cotangent):
    symmetric = add_rounded(feature_map, mirror(feature_map))
    pre_first = dilated_conv(extend(symmetric), kernel_first) + bias_first
    hidden = gelu_value(pre_first).astype(jnp.bfloat16)
    pre_second = dilated_conv(extend(hidden), kernel_second) + bias_second
    output = (symmetric.astype(jnp.float32) + gelu_value(pre_second)).astype(jnp.bfloat16)
    grad_second = (cotangent.astype(jnp.float32) * gelu_slope(pre_second)).astype(jnp.bfloat16)
    hidden_gradient = dilated_conv(extend(grad_second), reversed_kernel(kernel_second))
    grad_first = (hidden_gradient * gelu_slope(pre_first)).astype(jnp.bfloat16)
    total_sum = cotangent.astype(jnp.float32) + dilated_conv(
        extend(grad_first), reversed_kernel(kernel_first)
    )
    grad_sym = total_sum.astype(jnp.bfloat16)
    return output, add_rounded(grad_sym, mirror(grad_sym))


def matrix_kernel(weight_first, weight_second, bias_first, bias_second, *outputs):
    first, second, third, fourth, first_bias, second_bias = outputs
    taps, channels = weight_first.shape[0], weight_first.shape[2]
    gap = jnp.zeros(weight_first.shape[2:], weight_first.dtype)
    for weight, ahead, behind in (
        (weight_first, first, fourth),
        (weight_second, second, third),
    ):
        for p in range(taps):
            for q in range(taps):
                upper = jnp.concatenate([weight[q, p], gap], 1)
                lower = jnp.concatenate([gap, weight[p, q]], 1)
                block = jnp.concatenate([upper, lower], 0)
                columns = pl.ds(2 * channels * q, 2 * channels)
                if ahead is second:
                    ahead[pl.ds(2 * channels * p, 2 * channels), columns] = block
                else:
                    joint = jnp.concatenate([weight[q, p], weight[p, q]], 1)
                    ahead[pl.ds(channels * p, channels), columns] = joint
                p_back, q_back = taps - 1 - p, taps - 1 - q
                behind[
                    pl.ds(2 * channels * q_back, 2 * channels),
                    pl.ds(2 * channels * p_back, 2 * channels),
                ] = block
    rest = slice(taps * channels, first.shape[0])
    first[rest] = jnp.zeros_like(first[rest])
    for bias, wide in ((bias_first, first_bias), (bias_second, second_bias)):
        wide[...] = jnp.concatenate([bias[...], bias[...]], 1)


def chain_matrices(weight_first, weight_second, bias_first, bias_second):
    taps, channels = weight_first.shape[0], weight_first.shape[2]
    size = taps * 2 * channels
    vmem = pl.BlockSpec(memory_space=pltpu.VMEM)
    return pl.pallas_call(
        matrix_kernel,
        out_shape=[
            jax.ShapeDtypeStruct(((taps + 1) * channels, size), jnp.bfloat16),
            *[jax.ShapeDtypeStruct((size, size), jnp.bfloat16)] * 3,
        ]
        + [jax.ShapeDtypeStruct((1, 2 * channels), jnp.float32)] * 2,
        in_specs=[vmem] * 4,
        out_specs=[vmem] * 6,
        compiler_params=pltpu.CompilerParams(vmem_limit_bytes=16 * 2**20),
    )(weight_first, weight_second, bias_first[None], bias_second[None])


def class_order():
    step = range(DILATION_STEP)
    pairs = [((a, a), (a + 1, a + 1)) for a in step[::2]]
    pairs += [((a, b), (b, a)) for a in step for b in step if a < b]
    return [c for pair in sorted(pairs) for c in pair][::-1]


def part_kernel(tile_cols, whole, parts, tile):
    step = DILATION_STEP
    part_cols = tile_cols // step
    part_rows = whole.shape[0] // (tile_cols * step)
    tile[: whole.shape[0]] = whole[...]
    for index, (a, b) in enumerate(class_order()):
        columns = [
            tile[pl.ds(a * tile_cols + k * step + b, part_rows, stride=step * tile_cols), :]
            for k in range(part_cols)
        ]
        part = jnp.concatenate(columns, 0).astype(jnp.bfloat16)
        r, c = divmod(index, parts.shape[2])
        for half in range(HALVES):
            parts[r, half, c] = part


def class_parts(row_count, feature_map, cotangent):
    tile_rows, tile_cols, channels = feature_map.shape
    classes = DILATION_STEP * DILATION_STEP
    cells = tile_rows * tile_cols
    shape = (row_count, HALVES, classes // row_count, cells // classes, 2 * channels)
    tile = jnp.concatenate([feature_map, cotangent], 2).astype(jnp.float32)
    return pl.pallas_call(
        functools.partial(part_kernel, tile_cols),
        out_shape=jax.ShapeDtypeStruct(shape, jnp.bfloat16),
        in_specs=[pl.BlockSpec(memory_space=pltpu.VMEM)],
        out_specs=pl.BlockSpec(memory_space=pltpu.VMEM),
        scratch_shapes=[pltpu.VMEM((cells + DILATION_STEP * tile_cols, 2 * channels), jnp.float32)],
        compiler_params=pltpu.CompilerParams(vmem_limit_bytes=16 * 2**20),
    )(tile.reshape(cells, 2 * channels))


def class_kernel(
    row_count,
    part_cols,
    own,
    other,
    weight_first,
    weight_second,
    weight_third,
    weight_fourth,
    bias_first,
    bias_second,
    result,
    turning,
    window,
):
    blocks, part, width = own.shape
    channels = width // 2
    part_rows = part // part_cols
    col_count = blocks // row_count
    half_count = col_count // HALVES
    class_cols, class_rows = col_count * part_cols, row_count * part_rows
    share = class_cols // HALVES
    count = share + CONVS
    column = lax.axis_index("col")
    half = lax.div(column, half_count)
    place = lax.axis_index("row") * half_count + lax.rem(column, half_count)
    evens = [index for index, (a, b) in enumerate(class_order()) if a == b]
    even = functools.reduce(jnp.logical_or, [place == index for index in evens])
    begin = half * (share - CONVS)
    cells = count * class_rows
    low = lax.broadcasted_iota(jnp.int32, (cells, width), 1) < channels
    row = lax.broadcasted_iota(jnp.int32, (1, class_rows, width), 1)

    pieces = []
    for r in range(row_count):
        reach = pl.ds(r * col_count + half * ((share - CONVS) // part_cols), count // part_cols)
        pieces.append(own[reach].reshape(count, part_rows, width))
    straight = jnp.concatenate(pieces, 1).astype(jnp.float32).reshape(cells, width)

    for r in range(row_count):
        reach = slice(r * col_count, (r + 1) * col_count)
        piece = jnp.where(even, own[reach], other[reach]).astype(jnp.float32)
        piece = piece.reshape(class_cols, part_rows, width)
        for k in range(class_cols):
            turning[pl.ds(k * class_rows + r * part_rows, part_rows), :] = piece[k]
    turned = jnp.concatenate(
        [turning[pl.ds(begin + i, class_cols, stride=class_rows), :] for i in range(count)], 0
    )

    def swapped(value):
        return pltpu.roll(value, channels, 1)

    chunks = 2
    size = cells // chunks
    rows = [slice(k * size, (k + 1) * size) for k in range(chunks)]
    low = low[:size]

    def tap_sum(images, k, matrix, dimension, doubled=False):
        gap = jnp.zeros((class_rows, width), jnp.bfloat16)
        image = images[k]
        before = images[k - 1][-class_rows:] if k else gap
        before = jnp.concatenate([before, image[:-class_rows]], 0)
        after = images[k + 1][:class_rows] if k + 1 < chunks else gap
        after = jnp.concatenate([image[class_rows:], after], 0)
        columns = [jnp.where(low, before, image), after] if doubled else [before, image, after]
        taps = lax.dot_general(
            jnp.concatenate(columns, 1),
            matrix[...],
            (((1,), (dimension,)), ((), ())),
            preferred_element_type=jnp.float32,
        )
        taps = taps.reshape(count // chunks, class_rows, 3 * width)
        above = jnp.where(row == 0, 0.0, pltpu.roll(taps[:, :, :width], 1, 1))
        below = pltpu.roll(taps[:, :, 2 * width :], class_rows - 1, 1)
        below = jnp.where(row == class_rows - 1, 0.0, below)
        return (above + taps[:, :, width : 2 * width] + below).reshape(size, width)

    symmetric, gradient = [], []
    for k in range(chunks):
        total = straight[rows[k]] + turned[rows[k]]
        symmetric.append(jnp.where(low, total, swapped(total)).astype(jnp.bfloat16))
        gradient.append(jnp.where(low, swapped(straight[rows[k]]), turned[rows[k]]))

    hidden, slope_first = [], []
    for k in range(chunks):
        pre_first = tap_sum(symmetric, k, weight_first, 0, True) + bias_first[...]
        value, slope = gelu_pair(pre_first)
        hidden.append(value.astype(jnp.bfloat16))
        slope_first.append(slope)
    output, grad_second = [], []
    for k in range(chunks):
        pre_second = tap_sum(hidden, k, weight_second, 0) + bias_second[...]
        value, slope = gelu_pair(pre_second)
        output.append(symmetric[k].astype(jnp.float32) + value)
        grad_second.append((gradient[k] * slope).astype(jnp.bfloat16))
    grad_first = [
        (tap_sum(grad_second, k, weight_third, 1) * slope_first[k]).astype(jnp.bfloat16)
        for k in range(chunks)
    ]
    for k in range(chunks):
        grad_sym = (gradient[k] + tap_sum(grad_first, k, weight_fourth, 1)).astype(jnp.bfloat16)
        grad_sym = grad_sym.astype(jnp.float32)
        finished = jnp.where(low, output[k], grad_sym + swapped(grad_sym)).astype(jnp.bfloat16)
        share_cols = count // chunks
        window[k * share_cols : (k + 1) * share_cols] = finished.reshape(share_cols, class_rows, width)

    for index, (a, b) in enumerate(class_order()):
        r, c = divmod(index, half_count)
        kept = window[pl.ds(half * CONVS + c * part_cols, part_cols)]
        kept = kept[:, r * part_rows : (r + 1) * part_rows]
        result[a * DILATION_STEP + b] = kept.reshape(part, width)


def class_chains(row_count, part_cols, own, other, *parameters):
    blocks, part, width = own.shape
    class_cols, class_rows = blocks // row_count * part_cols, row_count * (part // part_cols)
    count = class_cols // HALVES + CONVS
    return pl.pallas_call(
        functools.partial(class_kernel, row_count, part_cols),
        out_shape=jax.ShapeDtypeStruct((blocks // HALVES, part, width), jnp.bfloat16),
        in_specs=[pl.BlockSpec(memory_space=pltpu.VMEM)] * 8,
        out_specs=pl.BlockSpec(memory_space=pltpu.VMEM),
        scratch_shapes=[
            pltpu.VMEM(((class_cols + 1) * class_rows, width), jnp.float32),
            pltpu.VMEM((count, class_rows, width), jnp.bfloat16),
        ],
        compiler_params=pltpu.CompilerParams(vmem_limit_bytes=32 * 2**20),
    )(own, other, *parameters)


def by_classes(feature_map, kernel_first, bias_first, kernel_second, bias_second, cotangent):
    row_count, col_count = lax.axis_size("row"), lax.axis_size("col")
    tile_rows, tile_cols, channels = feature_map.shape
    step = DILATION_STEP
    part_rows, part_cols = tile_rows // step, tile_cols // step

    parts = class_parts(row_count, feature_map, cotangent)
    parts = parts.reshape(row_count * col_count, part_cols * part_rows, 2 * channels)
    own = lax.all_to_all(parts, both, 0, 0, tiled=True)
    raw = (kernel_first, kernel_second, bias_first, bias_second)
    own, *raw = lax.optimization_barrier((own,) + raw)
    other = lax.ppermute(own, "col", [(i, i ^ 1) for i in range(col_count)])
    result = class_chains(row_count, part_cols, own, other, *chain_matrices(*raw))

    half_count = col_count // HALVES
    order = sorted(range(step * step), key=lambda index: class_order()[index])
    halves = [
        [i // half_count * col_count + h * half_count + i % half_count for i in order]
        for h in range(HALVES)
    ]
    back = lax.all_to_all(result, both, 0, 0, axis_index_groups=halves, tiled=True)
    back = back.reshape(step, step, part_cols, part_rows, 2 * channels)
    back = jnp.transpose(back, (3, 0, 2, 1, 4)).reshape(tile_rows, tile_cols, 2 * channels)
    return back[..., :channels], back[..., channels:]


def solution(mesh):
    row_count, col_count = mesh.shape["row"], mesh.shape["col"]
    classes = DILATION_STEP * DILATION_STEP
    paired = row_count * col_count == HALVES * classes and col_count % (2 * HALVES) == 0
    in_specs = (P("row", "col", None), P(), P(), P(), P(), P("row", "col", None))
    out_specs = (P("row", "col", None), P("row", "col", None))

    def whole(feature_map, *others):
        size = feature_map.shape[0]
        part_rows, part_cols = size // row_count // DILATION_STEP, size // col_count // DILATION_STEP
        fits = size % (DILATION_STEP * row_count) == 0 and size % (DILATION_STEP * col_count) == 0
        fits = fits and part_rows % 16 == 0 and CONVS % part_cols == 0
        per_device = by_classes if paired and fits else by_tiles
        return jax.shard_map(
            per_device, mesh=mesh, in_specs=in_specs, out_specs=out_specs, check_vma=False
        )(feature_map, *others)

    return whole
```

```python
import functools

import jax
import jax.numpy as jnp
from jax import lax
from jax.experimental import pallas as pl
from jax.experimental.pallas import tpu as pltpu
from jax.sharding import PartitionSpec as P

DILATION_STEP = 4
HALVES = 2
CONVS = 4


root_half = 0.7071067811865476
inv_root_tau = 0.3989422804014327
both = ("row", "col")


def with_halo(array, sides, width):
    for axis, dim in sides:
        size, length = (lax.axis_size(axis), array.shape[dim])
        up = [(i, (i + 1) % size) for i in range(size - 1)]
        down = [(j, i) for i, j in up]
        last = lax.slice_in_dim(array, length - width, length, axis=dim)
        first = lax.slice_in_dim(array, 0, width, axis=dim)
        before = lax.ppermute(last, axis, up)
        after = lax.ppermute(first, axis, down)
        array = jnp.concatenate([before, array, after], axis=dim)
    return array


def gelu_value(value_array):
    return 0.5 * value_array * (1.0 + lax.erf(value_array * root_half))


def gelu_slope(value_array):
    return (
        0.5 * (1.0 + lax.erf(value_array * root_half))
        + value_array * jnp.exp(-0.5 * value_array * value_array) * inv_root_tau
    )


def gelu_pair(value_array):
    share = 0.5 + 0.5 * lax.erf(value_array * root_half)
    bell = jnp.exp(-0.5 * value_array * value_array) * inv_root_tau
    return value_array * share, share + value_array * bell


def conv(padded_input, conv_kernel, step):
    return lax.conv_general_dilated(
        padded_input[None],
        conv_kernel,
        (1, 1),
        "VALID",
        rhs_dilation=(step, step),
        dimension_numbers=("NHWC", "HWIO", "NHWC"),
        preferred_element_type=jnp.float32,
    )[0]


def dilated_conv(padded_input, conv_kernel):
    return conv(padded_input, conv_kernel, DILATION_STEP)


def reversed_kernel(conv_kernel):
    return jnp.transpose(conv_kernel[::-1, ::-1], (0, 1, 3, 2))


def extend(value_array):
    return with_halo(value_array, (("row", 0), ("col", 1)), DILATION_STEP)


def mirror(tile):
    row_count = lax.axis_size("row")
    col_count = lax.axis_size("col")
    tile_rows, tile_cols, channels = tile.shape
    unit_len = tile_rows // col_count
    col_ratio = col_count // row_count
    spread_parts = tile.reshape(1, 1, col_ratio, row_count, unit_len, tile_cols * channels)
    spread_parts = lax.all_to_all(spread_parts, "row", split_axis=3, concat_axis=1, tiled=True)
    across_parts = spread_parts.reshape(1, col_count, unit_len, 1, tile_cols * channels)
    across_parts = lax.all_to_all(across_parts, "col", split_axis=1, concat_axis=3, tiled=True)
    settle_parts = across_parts.reshape(1, 1, unit_len, row_count, tile_rows * channels)
    settle_parts = lax.all_to_all(settle_parts, "row", split_axis=3, concat_axis=1, tiled=True)
    turned = settle_parts.reshape(tile_cols, tile_rows, channels)
    return jnp.transpose(turned, (1, 0, 2))


def add_rounded(first, second):
    return (first.astype(jnp.float32) + second.astype(jnp.float32)).astype(jnp.bfloat16)


def by_tiles(feature_map, kernel_first, bias_first, kernel_second, bias_second, cotangent):
    symmetric = add_rounded(feature_map, mirror(feature_map))
    pre_first = dilated_conv(extend(symmetric), kernel_first) + bias_first
    hidden = gelu_value(pre_first).astype(jnp.bfloat16)
    pre_second = dilated_conv(extend(hidden), kernel_second) + bias_second
    output = (symmetric.astype(jnp.float32) + gelu_value(pre_second)).astype(jnp.bfloat16)
    grad_second = (cotangent.astype(jnp.float32) * gelu_slope(pre_second)).astype(jnp.bfloat16)
    hidden_gradient = dilated_conv(extend(grad_second), reversed_kernel(kernel_second))
    grad_first = (hidden_gradient * gelu_slope(pre_first)).astype(jnp.bfloat16)
    total_sum = cotangent.astype(jnp.float32) + dilated_conv(
        extend(grad_first), reversed_kernel(kernel_first)
    )
    grad_sym = total_sum.astype(jnp.bfloat16)
    return output, add_rounded(grad_sym, mirror(grad_sym))


def matrix_kernel(half_count, weight_first, weight_second, bias_first, bias_second, *outputs):
    first, second, third, fourth, first_bias, second_bias = outputs
    taps, channels = weight_first.shape[0], weight_first.shape[2]
    gap = jnp.zeros(weight_first.shape[2:], weight_first.dtype)
    half = lax.div(lax.axis_index("col"), half_count)
    for weight, ahead, behind in (
        (weight_first, first, fourth),
        (weight_second, second, third),
    ):
        for p in range(taps):
            along = half * (taps - 1) + (1 - 2 * half) * p
            for q in range(taps):
                upper = jnp.concatenate([weight[q, along], gap], 1)
                lower = jnp.concatenate([gap, weight[along, q]], 1)
                block = jnp.concatenate([upper, lower], 0)
                columns = pl.ds(2 * channels * q, 2 * channels)
                if ahead is second:
                    ahead[pl.ds(2 * channels * p, 2 * channels), columns] = block
                else:
                    joint = jnp.concatenate([weight[q, along], weight[along, q]], 1)
                    ahead[pl.ds(channels * p, channels), columns] = joint
                p_back, q_back = taps - 1 - p, taps - 1 - q
                behind[
                    pl.ds(2 * channels * q_back, 2 * channels),
                    pl.ds(2 * channels * p_back, 2 * channels),
                ] = block
    rest = slice(taps * channels, first.shape[0])
    first[rest] = jnp.zeros_like(first[rest])
    for bias, wide in ((bias_first, first_bias), (bias_second, second_bias)):
        wide[...] = jnp.concatenate([bias[...], bias[...]], 1)


def chain_matrices(half_count, weight_first, weight_second, bias_first, bias_second):
    taps, channels = weight_first.shape[0], weight_first.shape[2]
    size = taps * 2 * channels
    vmem = pl.BlockSpec(memory_space=pltpu.VMEM)
    return pl.pallas_call(
        functools.partial(matrix_kernel, half_count),
        out_shape=[
            jax.ShapeDtypeStruct(((taps + 1) * channels, size), jnp.bfloat16),
            *[jax.ShapeDtypeStruct((size, size), jnp.bfloat16)] * 3,
        ]
        + [jax.ShapeDtypeStruct((1, 2 * channels), jnp.float32)] * 2,
        in_specs=[vmem] * 4,
        out_specs=[vmem] * 6,
        compiler_params=pltpu.CompilerParams(vmem_limit_bytes=16 * 2**20),
    )(weight_first, weight_second, bias_first[None], bias_second[None])


def class_order():
    step = range(DILATION_STEP)
    pairs = [((a, a), (a + 1, a + 1)) for a in step[::2]]
    pairs += [((a, b), (b, a)) for a in step for b in step if a < b]
    return [c for pair in sorted(pairs) for c in pair][::-1]


def part_kernel(tile_cols, whole, parts, tile):
    step = DILATION_STEP
    part_cols = tile_cols // step
    part_rows = whole.shape[0] // (tile_cols * step)
    tile[: whole.shape[0]] = whole[...]
    for index, (a, b) in enumerate(class_order()):
        columns = [
            tile[pl.ds(a * tile_cols + k * step + b, part_rows, stride=step * tile_cols), :]
            for k in range(part_cols)
        ]
        part = jnp.concatenate(columns, 0).astype(jnp.bfloat16)
        r, c = divmod(index, parts.shape[2])
        for half in range(HALVES):
            parts[r, half, c] = part


def class_parts(row_count, feature_map, cotangent):
    tile_rows, tile_cols, channels = feature_map.shape
    classes = DILATION_STEP * DILATION_STEP
    cells = tile_rows * tile_cols
    shape = (row_count, HALVES, classes // row_count, cells // classes, 2 * channels)
    tile = jnp.concatenate([feature_map, cotangent], 2).astype(jnp.float32)
    return pl.pallas_call(
        functools.partial(part_kernel, tile_cols),
        out_shape=jax.ShapeDtypeStruct(shape, jnp.bfloat16),
        in_specs=[pl.BlockSpec(memory_space=pltpu.VMEM)],
        out_specs=pl.BlockSpec(memory_space=pltpu.VMEM),
        scratch_shapes=[pltpu.VMEM((cells + DILATION_STEP * tile_cols, 2 * channels), jnp.float32)],
        compiler_params=pltpu.CompilerParams(vmem_limit_bytes=16 * 2**20),
    )(tile.reshape(cells, 2 * channels))


def class_kernel(
    row_count,
    part_cols,
    own,
    other,
    weight_first,
    weight_second,
    weight_third,
    weight_fourth,
    bias_first,
    bias_second,
    result,
    turning,
    window,
):
    blocks, part, width = own.shape
    channels = width // 2
    part_rows = part // part_cols
    col_count = blocks // row_count
    half_count = col_count // HALVES
    class_cols, class_rows = col_count * part_cols, row_count * part_rows
    share = class_cols // HALVES
    count = share + CONVS
    column = lax.axis_index("col")
    half = lax.div(column, half_count)
    place = lax.axis_index("row") * half_count + lax.rem(column, half_count)
    evens = [index for index, (a, b) in enumerate(class_order()) if a == b]
    even = functools.reduce(jnp.logical_or, [place == index for index in evens])
    row = lax.broadcasted_iota(jnp.int32, (1, class_rows, width), 1)

    def inward(index, total):
        return half * (total - 1) + (1 - 2 * half) * index

    pieces = []
    for n in range(count // part_cols):
        blocks = [own[r * col_count + inward(n, col_count)] for r in range(row_count)]
        for k in range(part_cols):
            ends = [slice(m * part_rows, (m + 1) * part_rows) for m in (k, part_cols - 1 - k)]
            pieces += [jnp.where(half == 0, block[ends[0]], block[ends[1]]) for block in blocks]
    straight = jnp.concatenate(pieces, 0).astype(jnp.float32)

    for r in range(row_count):
        reach = slice(r * col_count, (r + 1) * col_count)
        piece = jnp.where(even, own[reach], other[reach]).astype(jnp.float32)
        piece = piece.reshape(class_cols, part_rows, width)
        for k in range(class_cols):
            turning[pl.ds(k * class_rows + r * part_rows, part_rows), :] = piece[k]
    turned = jnp.concatenate(
        [
            turning[pl.ds(inward(n, class_cols), class_cols, stride=class_rows), :]
            for n in range(count)
        ],
        0,
    )

    def low(value):
        return lax.broadcasted_iota(jnp.int32, value.shape, 1) < channels

    def swapped(value):
        return pltpu.roll(value, channels, 1)

    def tap_sum(image, begin, end, matrix, dimension, doubled=False):
        first, last = begin * class_rows, end * class_rows
        gap = [jnp.zeros((class_rows, width), image.dtype)] if begin == 0 else []
        before = image[max(first - class_rows, 0) : last - class_rows]
        before = jnp.concatenate(gap + [before], 0)
        after = image[first + class_rows : last + class_rows]
        image = image[first:last]
        columns = [jnp.where(low(image), before, image), after]
        def product(value, weights):
            return lax.dot_general(
                value, weights, (((1,), (dimension,)), ((), ())), preferred_element_type=jnp.float32
            )

        if doubled:
            taps = product(jnp.concatenate(columns, 1), matrix[...])
        elif dimension == 0:
            taps = product(jnp.concatenate([image, after], 1), matrix[width:, :])
            taps = taps + product(before, matrix[:width, :])
        else:
            taps = product(jnp.concatenate([image, after], 1), matrix[:, width:])
            taps = taps + product(before, matrix[:, :width])
        taps = taps.reshape(end - begin, class_rows, 3 * width)
        above = jnp.where(row == 0, 0.0, pltpu.roll(taps[:, :, :width], 1, 1))
        below = pltpu.roll(taps[:, :, 2 * width :], class_rows - 1, 1)
        below = jnp.where(row == class_rows - 1, 0.0, below)
        return (above + taps[:, :, width : 2 * width] + below).reshape(last - first, width)

    def runs(total):
        cut = (total + 1) // 2
        return (0, cut), (cut, total)

    def columns(value, begin, end):
        return value[begin * class_rows : end * class_rows]

    symmetric = straight + turned
    symmetric = jnp.where(low(symmetric), symmetric, swapped(symmetric)).astype(jnp.bfloat16)
    gradient = jnp.where(low(turned), swapped(straight), turned)

    hidden, slope_first = [], []
    for run in runs(count - 1):
        pre_first = tap_sum(symmetric, *run, weight_first, 0, True) + bias_first[...]
        value, slope = gelu_pair(pre_first)
        hidden.append(value.astype(jnp.bfloat16))
        slope_first.append(slope)
    hidden, slope_first = jnp.concatenate(hidden, 0), jnp.concatenate(slope_first, 0)
    output, grad_second = [], []
    for run in runs(count - 2):
        pre_second = tap_sum(hidden, *run, weight_second, 0) + bias_second[...]
        value, slope = gelu_pair(pre_second)
        output.append(columns(symmetric, *run).astype(jnp.float32) + value)
        grad_second.append((columns(gradient, *run) * slope).astype(jnp.bfloat16))
    output, grad_second = jnp.concatenate(output, 0), jnp.concatenate(grad_second, 0)
    grad_first = jnp.concatenate(
        [
            (tap_sum(grad_second, *run, weight_third, 1) * columns(slope_first, *run)).astype(
                jnp.bfloat16
            )
            for run in runs(count - 3)
        ],
        0,
    )
    for run in runs(share):
        total_sum = columns(gradient, *run) + tap_sum(grad_first, *run, weight_fourth, 1)
        grad_sym = total_sum.astype(jnp.bfloat16).astype(jnp.float32)
        grad_input = grad_sym + swapped(grad_sym)
        finished = jnp.where(low(grad_input), columns(output, *run), grad_input)
        finished = finished.astype(jnp.bfloat16).reshape(run[1] - run[0], class_rows, width)
        window[run[0] : run[1]] = finished

    for index, (a, b) in enumerate(class_order()):
        r, c = divmod(index, half_count)
        kept = [
            window[inward(c * part_cols + k, share), r * part_rows : (r + 1) * part_rows]
            for k in range(part_cols)
        ]
        result[a * DILATION_STEP + b] = jnp.concatenate(kept, 0)


def class_chains(row_count, part_cols, own, other, *parameters):
    blocks, part, width = own.shape
    class_cols, class_rows = blocks // row_count * part_cols, row_count * (part // part_cols)
    share = class_cols // HALVES
    return pl.pallas_call(
        functools.partial(class_kernel, row_count, part_cols),
        out_shape=jax.ShapeDtypeStruct((blocks // HALVES, part, width), jnp.bfloat16),
        in_specs=[pl.BlockSpec(memory_space=pltpu.VMEM)] * 8,
        out_specs=pl.BlockSpec(memory_space=pltpu.VMEM),
        scratch_shapes=[
            pltpu.VMEM(((class_cols + 1) * class_rows, width), jnp.float32),
            pltpu.VMEM((share, class_rows, width), jnp.bfloat16),
        ],
        compiler_params=pltpu.CompilerParams(vmem_limit_bytes=32 * 2**20),
    )(own, other, *parameters)


def by_classes(feature_map, kernel_first, bias_first, kernel_second, bias_second, cotangent):
    row_count, col_count = lax.axis_size("row"), lax.axis_size("col")
    tile_rows, tile_cols, channels = feature_map.shape
    step = DILATION_STEP
    part_rows, part_cols = tile_rows // step, tile_cols // step

    parts = class_parts(row_count, feature_map, cotangent)
    parts = parts.reshape(row_count * col_count, part_cols * part_rows, 2 * channels)
    own = lax.all_to_all(parts, both, 0, 0, tiled=True)
    half_count = col_count // HALVES
    raw = (kernel_first, kernel_second, bias_first, bias_second)
    own, *raw = lax.optimization_barrier((own,) + raw)
    other = lax.ppermute(own, "col", [(i, i ^ 1) for i in range(col_count)])
    result = class_chains(row_count, part_cols, own, other, *chain_matrices(half_count, *raw))

    order = sorted(range(step * step), key=lambda index: class_order()[index])
    halves = [
        [i // half_count * col_count + h * half_count + i % half_count for i in order]
        for h in range(HALVES)
    ]
    back = lax.all_to_all(result, both, 0, 0, axis_index_groups=halves, tiled=True)
    back = back.reshape(step, step, part_cols, part_rows, 2 * channels)
    back = jnp.transpose(back, (3, 0, 2, 1, 4)).reshape(tile_rows, tile_cols, 2 * channels)
    return back[..., :channels], back[..., channels:]


def solution(mesh):
    row_count, col_count = mesh.shape["row"], mesh.shape["col"]
    classes = DILATION_STEP * DILATION_STEP
    paired = row_count * col_count == HALVES * classes and col_count % (2 * HALVES) == 0
    in_specs = (P("row", "col", None), P(), P(), P(), P(), P("row", "col", None))
    out_specs = (P("row", "col", None), P("row", "col", None))

    def whole(feature_map, *others):
        size = feature_map.shape[0]
        part_rows, part_cols = size // row_count // DILATION_STEP, size // col_count // DILATION_STEP
        fits = size % (DILATION_STEP * row_count) == 0 and size % (DILATION_STEP * col_count) == 0
        fits = fits and part_rows % 16 == 0 and CONVS % part_cols == 0
        per_device = by_classes if paired and fits else by_tiles
        return jax.shard_map(
            per_device, mesh=mesh, in_specs=in_specs, out_specs=out_specs, check_vma=False
        )(feature_map, *others)

    return whole
```

```python
import functools

import jax
import jax.numpy as jnp
from jax import lax
from jax.experimental import pallas as pl
from jax.experimental.pallas import tpu as pltpu
from jax.sharding import PartitionSpec as P

DILATION_STEP = 4
HALVES = 2
CONVS = 4


root_half = 0.7071067811865476
inv_root_tau = 0.3989422804014327
both = ("row", "col")


def with_halo(array, sides, width):
    for axis, dim in sides:
        size, length = (lax.axis_size(axis), array.shape[dim])
        up = [(i, (i + 1) % size) for i in range(size - 1)]
        down = [(j, i) for i, j in up]
        last = lax.slice_in_dim(array, length - width, length, axis=dim)
        first = lax.slice_in_dim(array, 0, width, axis=dim)
        before = lax.ppermute(last, axis, up)
        after = lax.ppermute(first, axis, down)
        array = jnp.concatenate([before, array, after], axis=dim)
    return array


def gelu_value(value_array):
    return 0.5 * value_array * (1.0 + lax.erf(value_array * root_half))


def gelu_slope(value_array):
    return (
        0.5 * (1.0 + lax.erf(value_array * root_half))
        + value_array * jnp.exp(-0.5 * value_array * value_array) * inv_root_tau
    )


def gelu_pair(value_array):
    share = 0.5 + 0.5 * lax.erf(value_array * root_half)
    bell = jnp.exp(-0.5 * value_array * value_array) * inv_root_tau
    return value_array * share, share + value_array * bell


def conv(padded_input, conv_kernel, step):
    return lax.conv_general_dilated(
        padded_input[None],
        conv_kernel,
        (1, 1),
        "VALID",
        rhs_dilation=(step, step),
        dimension_numbers=("NHWC", "HWIO", "NHWC"),
        preferred_element_type=jnp.float32,
    )[0]


def dilated_conv(padded_input, conv_kernel):
    return conv(padded_input, conv_kernel, DILATION_STEP)


def reversed_kernel(conv_kernel):
    return jnp.transpose(conv_kernel[::-1, ::-1], (0, 1, 3, 2))


def extend(value_array):
    return with_halo(value_array, (("row", 0), ("col", 1)), DILATION_STEP)


def mirror(tile):
    row_count = lax.axis_size("row")
    col_count = lax.axis_size("col")
    tile_rows, tile_cols, channels = tile.shape
    unit_len = tile_rows // col_count
    col_ratio = col_count // row_count
    spread_parts = tile.reshape(1, 1, col_ratio, row_count, unit_len, tile_cols * channels)
    spread_parts = lax.all_to_all(spread_parts, "row", split_axis=3, concat_axis=1, tiled=True)
    across_parts = spread_parts.reshape(1, col_count, unit_len, 1, tile_cols * channels)
    across_parts = lax.all_to_all(across_parts, "col", split_axis=1, concat_axis=3, tiled=True)
    settle_parts = across_parts.reshape(1, 1, unit_len, row_count, tile_rows * channels)
    settle_parts = lax.all_to_all(settle_parts, "row", split_axis=3, concat_axis=1, tiled=True)
    turned = settle_parts.reshape(tile_cols, tile_rows, channels)
    return jnp.transpose(turned, (1, 0, 2))


def add_rounded(first, second):
    return (first.astype(jnp.float32) + second.astype(jnp.float32)).astype(jnp.bfloat16)


def by_tiles(feature_map, kernel_first, bias_first, kernel_second, bias_second, cotangent):
    symmetric = add_rounded(feature_map, mirror(feature_map))
    pre_first = dilated_conv(extend(symmetric), kernel_first) + bias_first
    hidden = gelu_value(pre_first).astype(jnp.bfloat16)
    pre_second = dilated_conv(extend(hidden), kernel_second) + bias_second
    output = (symmetric.astype(jnp.float32) + gelu_value(pre_second)).astype(jnp.bfloat16)
    grad_second = (cotangent.astype(jnp.float32) * gelu_slope(pre_second)).astype(jnp.bfloat16)
    hidden_gradient = dilated_conv(extend(grad_second), reversed_kernel(kernel_second))
    grad_first = (hidden_gradient * gelu_slope(pre_first)).astype(jnp.bfloat16)
    total_sum = cotangent.astype(jnp.float32) + dilated_conv(
        extend(grad_first), reversed_kernel(kernel_first)
    )
    grad_sym = total_sum.astype(jnp.bfloat16)
    return output, add_rounded(grad_sym, mirror(grad_sym))


def matrix_kernel(half_count, weight_first, weight_second, bias_first, bias_second, *outputs):
    first, second, third, fourth, first_bias, second_bias = outputs
    taps, channels = weight_first.shape[0], weight_first.shape[2]
    gap = jnp.zeros(weight_first.shape[2:], weight_first.dtype)
    half = lax.div(lax.axis_index("col"), half_count)
    for weight, ahead, behind in (
        (weight_first, first, fourth),
        (weight_second, second, third),
    ):
        for p in range(taps):
            along = half * (taps - 1) + (1 - 2 * half) * p
            for q in range(taps):
                upper = jnp.concatenate([weight[q, along], gap], 1)
                lower = jnp.concatenate([gap, weight[along, q]], 1)
                block = jnp.concatenate([upper, lower], 0)
                columns = pl.ds(2 * channels * q, 2 * channels)
                if ahead is second:
                    ahead[pl.ds(2 * channels * p, 2 * channels), columns] = block
                else:
                    joint = jnp.concatenate([weight[q, along], weight[along, q]], 1)
                    ahead[pl.ds(channels * p, channels), columns] = joint
                p_back, q_back = taps - 1 - p, taps - 1 - q
                behind[
                    pl.ds(2 * channels * q_back, 2 * channels),
                    pl.ds(2 * channels * p_back, 2 * channels),
                ] = block
    rest = slice(taps * channels, first.shape[0])
    first[rest] = jnp.zeros_like(first[rest])
    for bias, wide in ((bias_first, first_bias), (bias_second, second_bias)):
        wide[...] = jnp.concatenate([bias[...], bias[...]], 1)


def chain_matrices(half_count, weight_first, weight_second, bias_first, bias_second):
    taps, channels = weight_first.shape[0], weight_first.shape[2]
    size = taps * 2 * channels
    vmem = pl.BlockSpec(memory_space=pltpu.VMEM)
    return pl.pallas_call(
        functools.partial(matrix_kernel, half_count),
        out_shape=[
            jax.ShapeDtypeStruct(((taps + 1) * channels, size), jnp.bfloat16),
            *[jax.ShapeDtypeStruct((size, size), jnp.bfloat16)] * 3,
        ]
        + [jax.ShapeDtypeStruct((1, 2 * channels), jnp.float32)] * 2,
        in_specs=[vmem] * 4,
        out_specs=[vmem] * 6,
        compiler_params=pltpu.CompilerParams(vmem_limit_bytes=16 * 2**20),
    )(weight_first, weight_second, bias_first[None], bias_second[None])


def class_order():
    step = range(DILATION_STEP)
    pairs = [((a, a), (a + 1, a + 1)) for a in step[::2]]
    pairs += [((a, b), (b, a)) for a in step for b in step if a < b]
    return [c for pair in sorted(pairs) for c in pair][::-1]


def part_kernel(tile_cols, whole, parts, tile):
    step = DILATION_STEP
    part_cols = tile_cols // step
    part_rows = whole.shape[0] // (tile_cols * step)
    tile[: whole.shape[0]] = whole[...]
    for index, (a, b) in enumerate(class_order()):
        columns = [
            tile[pl.ds(a * tile_cols + k * step + b, part_rows, stride=step * tile_cols), :]
            for k in range(part_cols)
        ]
        part = jnp.concatenate(columns, 0).astype(jnp.bfloat16)
        r, c = divmod(index, parts.shape[2])
        for half in range(HALVES):
            parts[r, half, c] = part


def class_parts(row_count, feature_map, cotangent):
    tile_rows, tile_cols, channels = feature_map.shape
    classes = DILATION_STEP * DILATION_STEP
    cells = tile_rows * tile_cols
    shape = (row_count, HALVES, classes // row_count, cells // classes, 2 * channels)
    tile = jnp.concatenate([feature_map, cotangent], 2).astype(jnp.float32)
    return pl.pallas_call(
        functools.partial(part_kernel, tile_cols),
        out_shape=jax.ShapeDtypeStruct(shape, jnp.bfloat16),
        in_specs=[pl.BlockSpec(memory_space=pltpu.VMEM)],
        out_specs=pl.BlockSpec(memory_space=pltpu.VMEM),
        scratch_shapes=[pltpu.VMEM((cells + DILATION_STEP * tile_cols, 2 * channels), jnp.float32)],
        compiler_params=pltpu.CompilerParams(vmem_limit_bytes=16 * 2**20),
    )(tile.reshape(cells, 2 * channels))


def class_kernel(
    row_count,
    part_cols,
    own,
    other,
    weight_first,
    weight_second,
    weight_third,
    weight_fourth,
    bias_first,
    bias_second,
    result,
    turning,
    window,
):
    blocks, part, width = own.shape
    channels = width // 2
    part_rows = part // part_cols
    col_count = blocks // row_count
    half_count = col_count // HALVES
    class_cols, class_rows = col_count * part_cols, row_count * part_rows
    share = class_cols // HALVES
    count = share + CONVS
    column = lax.axis_index("col")
    half = lax.div(column, half_count)
    place = lax.axis_index("row") * half_count + lax.rem(column, half_count)
    evens = [index for index, (a, b) in enumerate(class_order()) if a == b]
    even = functools.reduce(jnp.logical_or, [place == index for index in evens])
    row = lax.broadcasted_iota(jnp.int32, (1, class_rows, width), 1)

    def chains(half):
        def inward(index, total):
            return total - 1 - index if half else index

        pieces = []
        for n in range(count // part_cols):
            blocks = [own[r * col_count + inward(n, col_count)] for r in range(row_count)]
            for k in range(part_cols):
                ends = [slice(m * part_rows, (m + 1) * part_rows) for m in (k, part_cols - 1 - k)]
                pieces += [block[ends[half]] for block in blocks]
        straight = jnp.concatenate(pieces, 0).astype(jnp.float32)

        for r in range(row_count):
            reach = slice(r * col_count, (r + 1) * col_count)
            piece = jnp.where(even, own[reach], other[reach]).astype(jnp.float32)
            piece = piece.reshape(class_cols, part_rows, width)
            for k in range(class_cols):
                turning[pl.ds(k * class_rows + r * part_rows, part_rows), :] = piece[k]
        turned = jnp.concatenate(
            [
                turning[pl.ds(inward(n, class_cols), class_cols, stride=class_rows), :]
                for n in range(count)
            ],
            0,
        )

        def low(value):
            return lax.broadcasted_iota(jnp.int32, value.shape, 1) < channels

        def swapped(value):
            return pltpu.roll(value, channels, 1)

        def tap_sum(image, begin, end, matrix, dimension, doubled=False):
            first, last = begin * class_rows, end * class_rows
            gap = [jnp.zeros((class_rows, width), image.dtype)] if begin == 0 else []
            before = image[max(first - class_rows, 0) : last - class_rows]
            before = jnp.concatenate(gap + [before], 0)
            after = image[first + class_rows : last + class_rows]
            image = image[first:last]
            columns = [jnp.where(low(image), before, image), after]
            def product(value, weights):
                return lax.dot_general(
                    value, weights, (((1,), (dimension,)), ((), ())), preferred_element_type=jnp.float32
                )

            if doubled:
                taps = product(jnp.concatenate(columns, 1), matrix[...])
            elif dimension == 0:
                taps = product(jnp.concatenate([image, after], 1), matrix[width:, :])
                taps = taps + product(before, matrix[:width, :])
            else:
                taps = product(jnp.concatenate([image, after], 1), matrix[:, width:])
                taps = taps + product(before, matrix[:, :width])
            taps = taps.reshape(end - begin, class_rows, 3 * width)
            above = jnp.where(row == 0, 0.0, pltpu.roll(taps[:, :, :width], 1, 1))
            below = pltpu.roll(taps[:, :, 2 * width :], class_rows - 1, 1)
            below = jnp.where(row == class_rows - 1, 0.0, below)
            return (above + taps[:, :, width : 2 * width] + below).reshape(last - first, width)

        def runs(total):
            cut = (total + 1) // 2
            return (0, cut), (cut, total)

        def columns(value, begin, end):
            return value[begin * class_rows : end * class_rows]

        symmetric = straight + turned
        symmetric = jnp.where(low(symmetric), symmetric, swapped(symmetric)).astype(jnp.bfloat16)
        gradient = jnp.where(low(turned), swapped(straight), turned)

        hidden, slope_first = [], []
        for run in runs(count - 1):
            pre_first = tap_sum(symmetric, *run, weight_first, 0, True) + bias_first[...]
            value, slope = gelu_pair(pre_first)
            hidden.append(value.astype(jnp.bfloat16))
            slope_first.append(slope)
        hidden, slope_first = jnp.concatenate(hidden, 0), jnp.concatenate(slope_first, 0)
        output, grad_second = [], []
        for run in runs(count - 2):
            pre_second = tap_sum(hidden, *run, weight_second, 0) + bias_second[...]
            value, slope = gelu_pair(pre_second)
            output.append(columns(symmetric, *run).astype(jnp.float32) + value)
            grad_second.append((columns(gradient, *run) * slope).astype(jnp.bfloat16))
        output, grad_second = jnp.concatenate(output, 0), jnp.concatenate(grad_second, 0)
        grad_first = jnp.concatenate(
            [
                (tap_sum(grad_second, *run, weight_third, 1) * columns(slope_first, *run)).astype(
                    jnp.bfloat16
                )
                for run in runs(count - 3)
            ],
            0,
        )
        for run in runs(share):
            total_sum = columns(gradient, *run) + tap_sum(grad_first, *run, weight_fourth, 1)
            grad_sym = total_sum.astype(jnp.bfloat16).astype(jnp.float32)
            grad_input = grad_sym + swapped(grad_sym)
            finished = jnp.where(low(grad_input), columns(output, *run), grad_input)
            finished = finished.astype(jnp.bfloat16).reshape(run[1] - run[0], class_rows, width)
            window[run[0] : run[1]] = finished

        for index, (a, b) in enumerate(class_order()):
            r, c = divmod(index, half_count)
            kept = [
                window[inward(c * part_cols + k, share), r * part_rows : (r + 1) * part_rows]
                for k in range(part_cols)
            ]
            result[a * DILATION_STEP + b] = jnp.concatenate(kept, 0)

    for index in range(HALVES):
        pl.when(half == index)(functools.partial(chains, index))


def class_chains(row_count, part_cols, own, other, *parameters):
    blocks, part, width = own.shape
    class_cols, class_rows = blocks // row_count * part_cols, row_count * (part // part_cols)
    share = class_cols // HALVES
    return pl.pallas_call(
        functools.partial(class_kernel, row_count, part_cols),
        out_shape=jax.ShapeDtypeStruct((blocks // HALVES, part, width), jnp.bfloat16),
        in_specs=[pl.BlockSpec(memory_space=pltpu.VMEM)] * 8,
        out_specs=pl.BlockSpec(memory_space=pltpu.VMEM),
        scratch_shapes=[
            pltpu.VMEM(((class_cols + 1) * class_rows, width), jnp.float32),
            pltpu.VMEM((share, class_rows, width), jnp.bfloat16),
        ],
        compiler_params=pltpu.CompilerParams(vmem_limit_bytes=32 * 2**20),
    )(own, other, *parameters)


def by_classes(feature_map, kernel_first, bias_first, kernel_second, bias_second, cotangent):
    row_count, col_count = lax.axis_size("row"), lax.axis_size("col")
    tile_rows, tile_cols, channels = feature_map.shape
    step = DILATION_STEP
    part_rows, part_cols = tile_rows // step, tile_cols // step

    parts = class_parts(row_count, feature_map, cotangent)
    parts = parts.reshape(row_count * col_count, part_cols * part_rows, 2 * channels)
    own = lax.all_to_all(parts, both, 0, 0, tiled=True)
    half_count = col_count // HALVES
    raw = (kernel_first, kernel_second, bias_first, bias_second)
    own, *raw = lax.optimization_barrier((own,) + raw)
    other = lax.ppermute(own, "col", [(i, i ^ 1) for i in range(col_count)])
    result = class_chains(row_count, part_cols, own, other, *chain_matrices(half_count, *raw))

    order = sorted(range(step * step), key=lambda index: class_order()[index])
    halves = [
        [i // half_count * col_count + h * half_count + i % half_count for i in order]
        for h in range(HALVES)
    ]
    back = lax.all_to_all(result, both, 0, 0, axis_index_groups=halves, tiled=True)
    back = back.reshape(step, step, part_cols, part_rows, 2 * channels)
    back = jnp.transpose(back, (3, 0, 2, 1, 4)).reshape(tile_rows, tile_cols, 2 * channels)
    return back[..., :channels], back[..., channels:]


def solution(mesh):
    row_count, col_count = mesh.shape["row"], mesh.shape["col"]
    classes = DILATION_STEP * DILATION_STEP
    paired = row_count * col_count == HALVES * classes and col_count % (2 * HALVES) == 0
    in_specs = (P("row", "col", None), P(), P(), P(), P(), P("row", "col", None))
    out_specs = (P("row", "col", None), P("row", "col", None))

    def whole(feature_map, *others):
        size = feature_map.shape[0]
        part_rows, part_cols = size // row_count // DILATION_STEP, size // col_count // DILATION_STEP
        fits = size % (DILATION_STEP * row_count) == 0 and size % (DILATION_STEP * col_count) == 0
        fits = fits and part_rows % 16 == 0 and CONVS % part_cols == 0
        per_device = by_classes if paired and fits else by_tiles
        return jax.shard_map(
            per_device, mesh=mesh, in_specs=in_specs, out_specs=out_specs, check_vma=False
        )(feature_map, *others)

    return whole
```

```python
import functools

import jax
import jax.numpy as jnp
from jax import lax
from jax.experimental import pallas as pl
from jax.experimental.pallas import tpu as pltpu
from jax.sharding import PartitionSpec as P

DILATION_STEP = 4
HALVES = 2
CONVS = 4


root_half = 0.7071067811865476
inv_root_tau = 0.3989422804014327
both = ("row", "col")


def with_halo(array, sides, width):
    for axis, dim in sides:
        size, length = (lax.axis_size(axis), array.shape[dim])
        up = [(i, (i + 1) % size) for i in range(size - 1)]
        down = [(j, i) for i, j in up]
        last = lax.slice_in_dim(array, length - width, length, axis=dim)
        first = lax.slice_in_dim(array, 0, width, axis=dim)
        before = lax.ppermute(last, axis, up)
        after = lax.ppermute(first, axis, down)
        array = jnp.concatenate([before, array, after], axis=dim)
    return array


def gelu_value(value_array):
    return 0.5 * value_array * (1.0 + lax.erf(value_array * root_half))


def gelu_slope(value_array):
    return (
        0.5 * (1.0 + lax.erf(value_array * root_half))
        + value_array * jnp.exp(-0.5 * value_array * value_array) * inv_root_tau
    )


def gelu_pair(value_array):
    share = 0.5 + 0.5 * lax.erf(value_array * root_half)
    bell = jnp.exp(-0.5 * value_array * value_array) * inv_root_tau
    return value_array * share, share + value_array * bell


def conv(padded_input, conv_kernel, step):
    return lax.conv_general_dilated(
        padded_input[None],
        conv_kernel,
        (1, 1),
        "VALID",
        rhs_dilation=(step, step),
        dimension_numbers=("NHWC", "HWIO", "NHWC"),
        preferred_element_type=jnp.float32,
    )[0]


def dilated_conv(padded_input, conv_kernel):
    return conv(padded_input, conv_kernel, DILATION_STEP)


def reversed_kernel(conv_kernel):
    return jnp.transpose(conv_kernel[::-1, ::-1], (0, 1, 3, 2))


def extend(value_array):
    return with_halo(value_array, (("row", 0), ("col", 1)), DILATION_STEP)


def mirror(tile):
    row_count = lax.axis_size("row")
    col_count = lax.axis_size("col")
    tile_rows, tile_cols, channels = tile.shape
    unit_len = tile_rows // col_count
    col_ratio = col_count // row_count
    spread_parts = tile.reshape(1, 1, col_ratio, row_count, unit_len, tile_cols * channels)
    spread_parts = lax.all_to_all(spread_parts, "row", split_axis=3, concat_axis=1, tiled=True)
    across_parts = spread_parts.reshape(1, col_count, unit_len, 1, tile_cols * channels)
    across_parts = lax.all_to_all(across_parts, "col", split_axis=1, concat_axis=3, tiled=True)
    settle_parts = across_parts.reshape(1, 1, unit_len, row_count, tile_rows * channels)
    settle_parts = lax.all_to_all(settle_parts, "row", split_axis=3, concat_axis=1, tiled=True)
    turned = settle_parts.reshape(tile_cols, tile_rows, channels)
    return jnp.transpose(turned, (1, 0, 2))


def add_rounded(first, second):
    return (first.astype(jnp.float32) + second.astype(jnp.float32)).astype(jnp.bfloat16)


def by_tiles(feature_map, kernel_first, bias_first, kernel_second, bias_second, cotangent):
    symmetric = add_rounded(feature_map, mirror(feature_map))
    pre_first = dilated_conv(extend(symmetric), kernel_first) + bias_first
    hidden = gelu_value(pre_first).astype(jnp.bfloat16)
    pre_second = dilated_conv(extend(hidden), kernel_second) + bias_second
    output = (symmetric.astype(jnp.float32) + gelu_value(pre_second)).astype(jnp.bfloat16)
    grad_second = (cotangent.astype(jnp.float32) * gelu_slope(pre_second)).astype(jnp.bfloat16)
    hidden_gradient = dilated_conv(extend(grad_second), reversed_kernel(kernel_second))
    grad_first = (hidden_gradient * gelu_slope(pre_first)).astype(jnp.bfloat16)
    total_sum = cotangent.astype(jnp.float32) + dilated_conv(
        extend(grad_first), reversed_kernel(kernel_first)
    )
    grad_sym = total_sum.astype(jnp.bfloat16)
    return output, add_rounded(grad_sym, mirror(grad_sym))


def matrix_kernel(half_count, weight_first, weight_second, bias_first, bias_second, *outputs):
    first, second, third, fourth, first_bias, second_bias = outputs
    taps, channels = weight_first.shape[0], weight_first.shape[2]
    gap = jnp.zeros(weight_first.shape[2:], weight_first.dtype)
    half = lax.div(lax.axis_index("col"), half_count)
    for weight, ahead, behind in (
        (weight_first, first, fourth),
        (weight_second, second, third),
    ):
        for p in range(taps):
            along = half * (taps - 1) + (1 - 2 * half) * p
            for q in range(taps):
                upper = jnp.concatenate([weight[q, along], gap], 1)
                lower = jnp.concatenate([gap, weight[along, q]], 1)
                block = jnp.concatenate([upper, lower], 0)
                columns = pl.ds(2 * channels * q, 2 * channels)
                if ahead is second:
                    ahead[pl.ds(2 * channels * p, 2 * channels), columns] = block
                else:
                    joint = jnp.concatenate([weight[q, along], weight[along, q]], 1)
                    ahead[pl.ds(channels * p, channels), columns] = joint
                p_back, q_back = taps - 1 - p, taps - 1 - q
                behind[
                    pl.ds(2 * channels * q_back, 2 * channels),
                    pl.ds(2 * channels * p_back, 2 * channels),
                ] = block
    rest = slice(taps * channels, first.shape[0])
    first[rest] = jnp.zeros_like(first[rest])
    for bias, wide in ((bias_first, first_bias), (bias_second, second_bias)):
        wide[...] = jnp.concatenate([bias[...], bias[...]], 1)


def chain_matrices(half_count, weight_first, weight_second, bias_first, bias_second):
    taps, channels = weight_first.shape[0], weight_first.shape[2]
    size = taps * 2 * channels
    vmem = pl.BlockSpec(memory_space=pltpu.VMEM)
    return pl.pallas_call(
        functools.partial(matrix_kernel, half_count),
        out_shape=[
            jax.ShapeDtypeStruct(((taps + 1) * channels, size), jnp.bfloat16),
            *[jax.ShapeDtypeStruct((size, size), jnp.bfloat16)] * 3,
        ]
        + [jax.ShapeDtypeStruct((1, 2 * channels), jnp.float32)] * 2,
        in_specs=[vmem] * 4,
        out_specs=[vmem] * 6,
        compiler_params=pltpu.CompilerParams(vmem_limit_bytes=16 * 2**20),
    )(weight_first, weight_second, bias_first[None], bias_second[None])


def class_order():
    step = range(DILATION_STEP)
    pairs = [((a, a), (a + 1, a + 1)) for a in step[::2]]
    pairs += [((a, b), (b, a)) for a in step for b in step if a < b]
    return [c for pair in sorted(pairs) for c in pair][::-1]


def part_kernel(tile_cols, whole, parts, tile):
    step = DILATION_STEP
    part_cols = tile_cols // step
    part_rows = whole.shape[0] // (tile_cols * step)
    tile[: whole.shape[0]] = whole[...]
    for index, (a, b) in enumerate(class_order()):
        columns = [
            tile[pl.ds(a * tile_cols + k * step + b, part_rows, stride=step * tile_cols), :]
            for k in range(part_cols)
        ]
        part = jnp.concatenate(columns, 0).astype(jnp.bfloat16)
        r, c = divmod(index, parts.shape[2])
        for half in range(HALVES):
            parts[r, half, c] = part


def class_parts(row_count, feature_map, cotangent):
    tile_rows, tile_cols, channels = feature_map.shape
    classes = DILATION_STEP * DILATION_STEP
    cells = tile_rows * tile_cols
    shape = (row_count, HALVES, classes // row_count, cells // classes, 2 * channels)
    tile = jnp.concatenate([feature_map, cotangent], 2).astype(jnp.float32)
    return pl.pallas_call(
        functools.partial(part_kernel, tile_cols),
        out_shape=jax.ShapeDtypeStruct(shape, jnp.bfloat16),
        in_specs=[pl.BlockSpec(memory_space=pltpu.VMEM)],
        out_specs=pl.BlockSpec(memory_space=pltpu.VMEM),
        scratch_shapes=[pltpu.VMEM((cells + DILATION_STEP * tile_cols, 2 * channels), jnp.float32)],
        compiler_params=pltpu.CompilerParams(vmem_limit_bytes=16 * 2**20),
    )(tile.reshape(cells, 2 * channels))


def class_kernel(
    row_count,
    part_cols,
    own,
    other,
    weight_first,
    weight_second,
    weight_third,
    weight_fourth,
    bias_first,
    bias_second,
    result,
    turning,
    window,
):
    blocks, part, width = own.shape
    channels = width // 2
    part_rows = part // part_cols
    col_count = blocks // row_count
    half_count = col_count // HALVES
    class_cols, class_rows = col_count * part_cols, row_count * part_rows
    share = class_cols // HALVES
    count = share + CONVS
    column = lax.axis_index("col")
    half = lax.div(column, half_count)
    place = lax.axis_index("row") * half_count + lax.rem(column, half_count)
    evens = [index for index, (a, b) in enumerate(class_order()) if a == b]
    even = functools.reduce(jnp.logical_or, [place == index for index in evens])
    row = lax.broadcasted_iota(jnp.int32, (1, class_rows, width), 1)

    def chains(half):
        def inward(index, total):
            return total - 1 - index if half else index

        pieces = []
        for n in range(count // part_cols):
            blocks = [own[r * col_count + inward(n, col_count)] for r in range(row_count)]
            for k in range(part_cols):
                ends = [slice(m * part_rows, (m + 1) * part_rows) for m in (k, part_cols - 1 - k)]
                pieces += [block[ends[half]] for block in blocks]
        straight = jnp.concatenate(pieces, 0).astype(jnp.float32)

        for r in range(row_count):
            reach = slice(r * col_count, (r + 1) * col_count)
            piece = jnp.where(even, own[reach], other[reach]).astype(jnp.float32)
            piece = piece.reshape(class_cols, part_rows, width)
            read = [inward(n, class_cols) - r * part_rows for n in range(count)]
            read = [n for n in read if 0 <= n < part_rows]
            low_row, high_row = min(read) // 8 * 8, (max(read) // 8 + 1) * 8
            for k in range(class_cols):
                rows = pl.ds(k * class_rows + r * part_rows + low_row, high_row - low_row)
                turning[rows, :] = piece[k, low_row:high_row]
        turned = jnp.concatenate(
            [
                turning[pl.ds(inward(n, class_cols), class_cols, stride=class_rows), :]
                for n in range(count)
            ],
            0,
        )

        def low(value):
            return lax.broadcasted_iota(jnp.int32, value.shape, 1) < channels

        def swapped(value):
            return pltpu.roll(value, channels, 1)

        def tap_sum(image, begin, end, matrix, dimension, doubled=False):
            first, last = begin * class_rows, end * class_rows
            gap = [jnp.zeros((class_rows, width), image.dtype)] if begin == 0 else []
            before = image[max(first - class_rows, 0) : last - class_rows]
            before = jnp.concatenate(gap + [before], 0)
            after = image[first + class_rows : last + class_rows]
            image = image[first:last]
            columns = [jnp.where(low(image), before, image), after]
            def product(value, weights):
                return lax.dot_general(
                    value, weights, (((1,), (dimension,)), ((), ())), preferred_element_type=jnp.float32
                )

            if doubled:
                taps = product(jnp.concatenate(columns, 1), matrix[...])
            elif dimension == 0:
                taps = product(jnp.concatenate([image, after], 1), matrix[width:, :])
                taps = taps + product(before, matrix[:width, :])
            else:
                taps = product(jnp.concatenate([image, after], 1), matrix[:, width:])
                taps = taps + product(before, matrix[:, :width])
            taps = taps.reshape(end - begin, class_rows, 3 * width)
            above = jnp.where(row == 0, 0.0, pltpu.roll(taps[:, :, :width], 1, 1))
            below = pltpu.roll(taps[:, :, 2 * width :], class_rows - 1, 1)
            below = jnp.where(row == class_rows - 1, 0.0, below)
            return (above + taps[:, :, width : 2 * width] + below).reshape(last - first, width)

        def runs(total):
            cut = (total + 1) // 2
            return (0, cut), (cut, total)

        def columns(value, begin, end):
            return value[begin * class_rows : end * class_rows]

        symmetric = straight + turned
        symmetric = jnp.where(low(symmetric), symmetric, swapped(symmetric)).astype(jnp.bfloat16)
        gradient = jnp.where(low(turned), swapped(straight), turned)

        hidden, slope_first = [], []
        for run in runs(count - 1):
            pre_first = tap_sum(symmetric, *run, weight_first, 0, True) + bias_first[...]
            value, slope = gelu_pair(pre_first)
            hidden.append(value.astype(jnp.bfloat16))
            slope_first.append(slope)
        hidden, slope_first = jnp.concatenate(hidden, 0), jnp.concatenate(slope_first, 0)
        output, grad_second = [], []
        for run in runs(count - 2):
            pre_second = tap_sum(hidden, *run, weight_second, 0) + bias_second[...]
            value, slope = gelu_pair(pre_second)
            output.append(columns(symmetric, *run).astype(jnp.float32) + value)
            grad_second.append((columns(gradient, *run) * slope).astype(jnp.bfloat16))
        output, grad_second = jnp.concatenate(output, 0), jnp.concatenate(grad_second, 0)
        grad_first = jnp.concatenate(
            [
                (tap_sum(grad_second, *run, weight_third, 1) * columns(slope_first, *run)).astype(
                    jnp.bfloat16
                )
                for run in runs(count - 3)
            ],
            0,
        )
        for run in runs(share):
            total_sum = columns(gradient, *run) + tap_sum(grad_first, *run, weight_fourth, 1)
            grad_sym = total_sum.astype(jnp.bfloat16).astype(jnp.float32)
            grad_input = grad_sym + swapped(grad_sym)
            finished = jnp.where(low(grad_input), columns(output, *run), grad_input)
            finished = finished.astype(jnp.bfloat16).reshape(run[1] - run[0], class_rows, width)
            window[run[0] : run[1]] = finished

        for index, (a, b) in enumerate(class_order()):
            r, c = divmod(index, half_count)
            kept = [
                window[inward(c * part_cols + k, share), r * part_rows : (r + 1) * part_rows]
                for k in range(part_cols)
            ]
            result[a * DILATION_STEP + b] = jnp.concatenate(kept, 0)

    for index in range(HALVES):
        pl.when(half == index)(functools.partial(chains, index))


def class_chains(row_count, part_cols, own, other, *parameters):
    blocks, part, width = own.shape
    class_cols, class_rows = blocks // row_count * part_cols, row_count * (part // part_cols)
    share = class_cols // HALVES
    return pl.pallas_call(
        functools.partial(class_kernel, row_count, part_cols),
        out_shape=jax.ShapeDtypeStruct((blocks // HALVES, part, width), jnp.bfloat16),
        in_specs=[pl.BlockSpec(memory_space=pltpu.VMEM)] * 8,
        out_specs=pl.BlockSpec(memory_space=pltpu.VMEM),
        scratch_shapes=[
            pltpu.VMEM(((class_cols + 1) * class_rows, width), jnp.float32),
            pltpu.VMEM((share, class_rows, width), jnp.bfloat16),
        ],
        compiler_params=pltpu.CompilerParams(vmem_limit_bytes=32 * 2**20),
    )(own, other, *parameters)


def by_classes(feature_map, kernel_first, bias_first, kernel_second, bias_second, cotangent):
    row_count, col_count = lax.axis_size("row"), lax.axis_size("col")
    tile_rows, tile_cols, channels = feature_map.shape
    step = DILATION_STEP
    part_rows, part_cols = tile_rows // step, tile_cols // step

    parts = class_parts(row_count, feature_map, cotangent)
    parts = parts.reshape(row_count * col_count, part_cols * part_rows, 2 * channels)
    own = lax.all_to_all(parts, both, 0, 0, tiled=True)
    half_count = col_count // HALVES
    raw = (kernel_first, kernel_second, bias_first, bias_second)
    own, *raw = lax.optimization_barrier((own,) + raw)
    other = lax.ppermute(own, "col", [(i, i ^ 1) for i in range(col_count)])
    result = class_chains(row_count, part_cols, own, other, *chain_matrices(half_count, *raw))

    order = sorted(range(step * step), key=lambda index: class_order()[index])
    halves = [
        [i // half_count * col_count + h * half_count + i % half_count for i in order]
        for h in range(HALVES)
    ]
    back = lax.all_to_all(result, both, 0, 0, axis_index_groups=halves, tiled=True)
    back = back.reshape(step, step, part_cols, part_rows, 2 * channels)
    back = jnp.transpose(back, (3, 0, 2, 1, 4)).reshape(tile_rows, tile_cols, 2 * channels)
    return back[..., :channels], back[..., channels:]


def solution(mesh):
    row_count, col_count = mesh.shape["row"], mesh.shape["col"]
    classes = DILATION_STEP * DILATION_STEP
    paired = row_count * col_count == HALVES * classes and col_count % (2 * HALVES) == 0
    in_specs = (P("row", "col", None), P(), P(), P(), P(), P("row", "col", None))
    out_specs = (P("row", "col", None), P("row", "col", None))

    def whole(feature_map, *others):
        size = feature_map.shape[0]
        part_rows, part_cols = size // row_count // DILATION_STEP, size // col_count // DILATION_STEP
        fits = size % (DILATION_STEP * row_count) == 0 and size % (DILATION_STEP * col_count) == 0
        fits = fits and part_rows % 16 == 0 and CONVS % part_cols == 0
        per_device = by_classes if paired and fits else by_tiles
        return jax.shard_map(
            per_device, mesh=mesh, in_specs=in_specs, out_specs=out_specs, check_vma=False
        )(feature_map, *others)

    return whole
```

```python
import functools

import jax
import jax.numpy as jnp
from jax import lax
from jax.experimental import pallas as pl
from jax.experimental.pallas import tpu as pltpu
from jax.sharding import PartitionSpec as P

DILATION_STEP = 4
HALVES = 2
CONVS = 4


root_half = 0.7071067811865476
inv_root_tau = 0.3989422804014327
both = ("row", "col")


def with_halo(array, sides, width):
    for axis, dim in sides:
        size, length = (lax.axis_size(axis), array.shape[dim])
        up = [(i, (i + 1) % size) for i in range(size - 1)]
        down = [(j, i) for i, j in up]
        last = lax.slice_in_dim(array, length - width, length, axis=dim)
        first = lax.slice_in_dim(array, 0, width, axis=dim)
        before = lax.ppermute(last, axis, up)
        after = lax.ppermute(first, axis, down)
        array = jnp.concatenate([before, array, after], axis=dim)
    return array


def gelu_value(value_array):
    return 0.5 * value_array * (1.0 + lax.erf(value_array * root_half))


def gelu_slope(value_array):
    return (
        0.5 * (1.0 + lax.erf(value_array * root_half))
        + value_array * jnp.exp(-0.5 * value_array * value_array) * inv_root_tau
    )


def gelu_pair(value_array):
    share = 0.5 + 0.5 * lax.erf(value_array * root_half)
    bell = jnp.exp(-0.5 * value_array * value_array) * inv_root_tau
    return value_array * share, share + value_array * bell


def conv(padded_input, conv_kernel, step):
    return lax.conv_general_dilated(
        padded_input[None],
        conv_kernel,
        (1, 1),
        "VALID",
        rhs_dilation=(step, step),
        dimension_numbers=("NHWC", "HWIO", "NHWC"),
        preferred_element_type=jnp.float32,
    )[0]


def dilated_conv(padded_input, conv_kernel):
    return conv(padded_input, conv_kernel, DILATION_STEP)


def reversed_kernel(conv_kernel):
    return jnp.transpose(conv_kernel[::-1, ::-1], (0, 1, 3, 2))


def extend(value_array):
    return with_halo(value_array, (("row", 0), ("col", 1)), DILATION_STEP)


def mirror(tile):
    row_count = lax.axis_size("row")
    col_count = lax.axis_size("col")
    tile_rows, tile_cols, channels = tile.shape
    unit_len = tile_rows // col_count
    col_ratio = col_count // row_count
    spread_parts = tile.reshape(1, 1, col_ratio, row_count, unit_len, tile_cols * channels)
    spread_parts = lax.all_to_all(spread_parts, "row", split_axis=3, concat_axis=1, tiled=True)
    across_parts = spread_parts.reshape(1, col_count, unit_len, 1, tile_cols * channels)
    across_parts = lax.all_to_all(across_parts, "col", split_axis=1, concat_axis=3, tiled=True)
    settle_parts = across_parts.reshape(1, 1, unit_len, row_count, tile_rows * channels)
    settle_parts = lax.all_to_all(settle_parts, "row", split_axis=3, concat_axis=1, tiled=True)
    turned = settle_parts.reshape(tile_cols, tile_rows, channels)
    return jnp.transpose(turned, (1, 0, 2))


def add_rounded(first, second):
    return (first.astype(jnp.float32) + second.astype(jnp.float32)).astype(jnp.bfloat16)


def by_tiles(feature_map, kernel_first, bias_first, kernel_second, bias_second, cotangent):
    symmetric = add_rounded(feature_map, mirror(feature_map))
    pre_first = dilated_conv(extend(symmetric), kernel_first) + bias_first
    hidden = gelu_value(pre_first).astype(jnp.bfloat16)
    pre_second = dilated_conv(extend(hidden), kernel_second) + bias_second
    output = (symmetric.astype(jnp.float32) + gelu_value(pre_second)).astype(jnp.bfloat16)
    grad_second = (cotangent.astype(jnp.float32) * gelu_slope(pre_second)).astype(jnp.bfloat16)
    hidden_gradient = dilated_conv(extend(grad_second), reversed_kernel(kernel_second))
    grad_first = (hidden_gradient * gelu_slope(pre_first)).astype(jnp.bfloat16)
    total_sum = cotangent.astype(jnp.float32) + dilated_conv(
        extend(grad_first), reversed_kernel(kernel_first)
    )
    grad_sym = total_sum.astype(jnp.bfloat16)
    return output, add_rounded(grad_sym, mirror(grad_sym))


def matrix_kernel(half_count, weight_first, weight_second, bias_first, bias_second, *outputs):
    first, second, third, fourth, first_bias, second_bias = outputs
    taps, channels = weight_first.shape[0], weight_first.shape[2]
    gap = jnp.zeros(weight_first.shape[2:], weight_first.dtype)
    half = lax.div(lax.axis_index("col"), half_count)
    for weight, ahead, behind in (
        (weight_first, first, fourth),
        (weight_second, second, third),
    ):
        for p in range(taps):
            along = half * (taps - 1) + (1 - 2 * half) * p
            for q in range(taps):
                upper = jnp.concatenate([weight[q, along], gap], 1)
                lower = jnp.concatenate([gap, weight[along, q]], 1)
                block = jnp.concatenate([upper, lower], 0)
                columns = pl.ds(2 * channels * q, 2 * channels)
                if ahead is second:
                    ahead[pl.ds(2 * channels * p, 2 * channels), columns] = block
                else:
                    joint = jnp.concatenate([weight[q, along], weight[along, q]], 1)
                    ahead[pl.ds(channels * p, channels), columns] = joint
                p_back, q_back = taps - 1 - p, taps - 1 - q
                behind[
                    pl.ds(2 * channels * q_back, 2 * channels),
                    pl.ds(2 * channels * p_back, 2 * channels),
                ] = block
    rest = slice(taps * channels, first.shape[0])
    first[rest] = jnp.zeros_like(first[rest])
    for bias, wide in ((bias_first, first_bias), (bias_second, second_bias)):
        wide[...] = jnp.concatenate([bias[...], bias[...]], 1)


def chain_matrices(half_count, weight_first, weight_second, bias_first, bias_second):
    taps, channels = weight_first.shape[0], weight_first.shape[2]
    size = taps * 2 * channels
    vmem = pl.BlockSpec(memory_space=pltpu.VMEM)
    return pl.pallas_call(
        functools.partial(matrix_kernel, half_count),
        out_shape=[
            jax.ShapeDtypeStruct(((taps + 1) * channels, size), jnp.bfloat16),
            *[jax.ShapeDtypeStruct((size, size), jnp.bfloat16)] * 3,
        ]
        + [jax.ShapeDtypeStruct((1, 2 * channels), jnp.float32)] * 2,
        in_specs=[vmem] * 4,
        out_specs=[vmem] * 6,
        compiler_params=pltpu.CompilerParams(vmem_limit_bytes=16 * 2**20),
    )(weight_first, weight_second, bias_first[None], bias_second[None])


def class_order():
    step = range(DILATION_STEP)
    pairs = [((a, a), (a + 1, a + 1)) for a in step[::2]]
    pairs += [((a, b), (b, a)) for a in step for b in step if a < b]
    return [c for pair in sorted(pairs) for c in pair][::-1]


def part_kernel(tile_cols, whole, parts, tile):
    step = DILATION_STEP
    part_cols = tile_cols // step
    part_rows = whole.shape[0] // (tile_cols * step)
    tile[: whole.shape[0]] = whole[...]
    for index, (a, b) in enumerate(class_order()):
        columns = [
            tile[pl.ds(a * tile_cols + k * step + b, part_rows, stride=step * tile_cols), :]
            for k in range(part_cols)
        ]
        part = jnp.concatenate(columns, 0).astype(jnp.bfloat16)
        r, c = divmod(index, parts.shape[2])
        for half in range(HALVES):
            parts[r, half, c] = part


def class_parts(row_count, feature_map, cotangent):
    tile_rows, tile_cols, channels = feature_map.shape
    classes = DILATION_STEP * DILATION_STEP
    cells = tile_rows * tile_cols
    shape = (row_count, HALVES, classes // row_count, cells // classes, 2 * channels)
    tile = jnp.concatenate([feature_map, cotangent], 2).astype(jnp.float32)
    return pl.pallas_call(
        functools.partial(part_kernel, tile_cols),
        out_shape=jax.ShapeDtypeStruct(shape, jnp.bfloat16),
        in_specs=[pl.BlockSpec(memory_space=pltpu.VMEM)],
        out_specs=pl.BlockSpec(memory_space=pltpu.VMEM),
        scratch_shapes=[pltpu.VMEM((cells + DILATION_STEP * tile_cols, 2 * channels), jnp.float32)],
        compiler_params=pltpu.CompilerParams(vmem_limit_bytes=16 * 2**20),
    )(tile.reshape(cells, 2 * channels))


def class_kernel(
    row_count,
    part_cols,
    own,
    other,
    weight_first,
    weight_second,
    weight_third,
    weight_fourth,
    bias_first,
    bias_second,
    result,
    turning,
    window,
):
    blocks, part, width = own.shape
    channels = width // 2
    part_rows = part // part_cols
    col_count = blocks // row_count
    half_count = col_count // HALVES
    class_cols, class_rows = col_count * part_cols, row_count * part_rows
    share = class_cols // HALVES
    count = share + CONVS
    column = lax.axis_index("col")
    half = lax.div(column, half_count)
    place = lax.axis_index("row") * half_count + lax.rem(column, half_count)
    evens = [index for index, (a, b) in enumerate(class_order()) if a == b]
    even = functools.reduce(jnp.logical_or, [place == index for index in evens])
    row = lax.broadcasted_iota(jnp.int32, (1, class_rows, width), 1)

    def chains(half, mirrored):
        def inward(index, total):
            return total - 1 - index if half else index

        pieces = []
        for n in range(count // part_cols):
            blocks = [own[r * col_count + inward(n, col_count)] for r in range(row_count)]
            for k in range(part_cols):
                ends = [slice(m * part_rows, (m + 1) * part_rows) for m in (k, part_cols - 1 - k)]
                pieces += [block[ends[half]] for block in blocks]
        straight = jnp.concatenate(pieces, 0).astype(jnp.float32)

        for r in range(row_count):
            reach = slice(r * col_count, (r + 1) * col_count)
            piece = mirrored[reach].astype(jnp.float32)
            piece = piece.reshape(class_cols, part_rows, width)
            read = [inward(n, class_cols) - r * part_rows for n in range(count)]
            read = [n for n in read if 0 <= n < part_rows]
            low_row, high_row = min(read) // 8 * 8, (max(read) // 8 + 1) * 8
            for k in range(class_cols):
                rows = pl.ds(k * class_rows + r * part_rows + low_row, high_row - low_row)
                turning[rows, :] = piece[k, low_row:high_row]
        turned = jnp.concatenate(
            [
                turning[pl.ds(inward(n, class_cols), class_cols, stride=class_rows), :]
                for n in range(count)
            ],
            0,
        )

        def low(value):
            return lax.broadcasted_iota(jnp.int32, value.shape, 1) < channels

        def swapped(value):
            return pltpu.roll(value, channels, 1)

        def tap_sum(image, begin, end, matrix, dimension, doubled=False):
            first, last = begin * class_rows, end * class_rows
            gap = [jnp.zeros((class_rows, width), image.dtype)] if begin == 0 else []
            before = image[max(first - class_rows, 0) : last - class_rows]
            before = jnp.concatenate(gap + [before], 0)
            after = image[first + class_rows : last + class_rows]
            image = image[first:last]
            columns = [jnp.where(low(image), before, image), after]
            def product(value, weights):
                return lax.dot_general(
                    value, weights, (((1,), (dimension,)), ((), ())), preferred_element_type=jnp.float32
                )

            if doubled:
                taps = product(jnp.concatenate(columns, 1), matrix[...])
            elif dimension == 0:
                taps = product(jnp.concatenate([image, after], 1), matrix[width:, :])
                taps = taps + product(before, matrix[:width, :])
            else:
                taps = product(jnp.concatenate([image, after], 1), matrix[:, width:])
                taps = taps + product(before, matrix[:, :width])
            taps = taps.reshape(end - begin, class_rows, 3 * width)
            above = jnp.where(row == 0, 0.0, pltpu.roll(taps[:, :, :width], 1, 1))
            below = pltpu.roll(taps[:, :, 2 * width :], class_rows - 1, 1)
            below = jnp.where(row == class_rows - 1, 0.0, below)
            return (above + taps[:, :, width : 2 * width] + below).reshape(last - first, width)

        def runs(total):
            cut = (total + 1) // 2
            return (0, cut), (cut, total)

        def columns(value, begin, end):
            return value[begin * class_rows : end * class_rows]

        symmetric = straight + turned
        symmetric = jnp.where(low(symmetric), symmetric, swapped(symmetric)).astype(jnp.bfloat16)
        gradient = jnp.where(low(turned), swapped(straight), turned)

        hidden, slope_first = [], []
        for run in runs(count - 1):
            pre_first = tap_sum(symmetric, *run, weight_first, 0, True) + bias_first[...]
            value, slope = gelu_pair(pre_first)
            hidden.append(value.astype(jnp.bfloat16))
            slope_first.append(slope)
        hidden, slope_first = jnp.concatenate(hidden, 0), jnp.concatenate(slope_first, 0)
        output, grad_second = [], []
        for run in runs(count - 2):
            pre_second = tap_sum(hidden, *run, weight_second, 0) + bias_second[...]
            value, slope = gelu_pair(pre_second)
            output.append(columns(symmetric, *run).astype(jnp.float32) + value)
            grad_second.append((columns(gradient, *run) * slope).astype(jnp.bfloat16))
        output, grad_second = jnp.concatenate(output, 0), jnp.concatenate(grad_second, 0)
        grad_first = jnp.concatenate(
            [
                (tap_sum(grad_second, *run, weight_third, 1) * columns(slope_first, *run)).astype(
                    jnp.bfloat16
                )
                for run in runs(count - 3)
            ],
            0,
        )
        for run in runs(share):
            total_sum = columns(gradient, *run) + tap_sum(grad_first, *run, weight_fourth, 1)
            grad_sym = total_sum.astype(jnp.bfloat16).astype(jnp.float32)
            grad_input = grad_sym + swapped(grad_sym)
            finished = jnp.where(low(grad_input), columns(output, *run), grad_input)
            finished = finished.astype(jnp.bfloat16).reshape(run[1] - run[0], class_rows, width)
            window[run[0] : run[1]] = finished

        for index, (a, b) in enumerate(class_order()):
            r, c = divmod(index, half_count)
            kept = [
                window[inward(c * part_cols + k, share), r * part_rows : (r + 1) * part_rows]
                for k in range(part_cols)
            ]
            result[a * DILATION_STEP + b] = jnp.concatenate(kept, 0)

    for index in range(HALVES):
        here = half == index
        pl.when(jnp.logical_and(here, even))(functools.partial(chains, index, own))
        pl.when(jnp.logical_and(here, jnp.logical_not(even)))(
            functools.partial(chains, index, other)
        )


def class_chains(row_count, part_cols, own, other, *parameters):
    blocks, part, width = own.shape
    class_cols, class_rows = blocks // row_count * part_cols, row_count * (part // part_cols)
    share = class_cols // HALVES
    return pl.pallas_call(
        functools.partial(class_kernel, row_count, part_cols),
        out_shape=jax.ShapeDtypeStruct((blocks // HALVES, part, width), jnp.bfloat16),
        in_specs=[pl.BlockSpec(memory_space=pltpu.VMEM)] * 8,
        out_specs=pl.BlockSpec(memory_space=pltpu.VMEM),
        scratch_shapes=[
            pltpu.VMEM(((class_cols + 1) * class_rows, width), jnp.float32),
            pltpu.VMEM((share, class_rows, width), jnp.bfloat16),
        ],
        compiler_params=pltpu.CompilerParams(vmem_limit_bytes=32 * 2**20),
    )(own, other, *parameters)


def by_classes(feature_map, kernel_first, bias_first, kernel_second, bias_second, cotangent):
    row_count, col_count = lax.axis_size("row"), lax.axis_size("col")
    tile_rows, tile_cols, channels = feature_map.shape
    step = DILATION_STEP
    part_rows, part_cols = tile_rows // step, tile_cols // step

    parts = class_parts(row_count, feature_map, cotangent)
    parts = parts.reshape(row_count * col_count, part_cols * part_rows, 2 * channels)
    own = lax.all_to_all(parts, both, 0, 0, tiled=True)
    half_count = col_count // HALVES
    raw = (kernel_first, kernel_second, bias_first, bias_second)
    own, *raw = lax.optimization_barrier((own,) + raw)
    other = lax.ppermute(own, "col", [(i, i ^ 1) for i in range(col_count)])
    result = class_chains(row_count, part_cols, own, other, *chain_matrices(half_count, *raw))

    order = sorted(range(step * step), key=lambda index: class_order()[index])
    halves = [
        [i // half_count * col_count + h * half_count + i % half_count for i in order]
        for h in range(HALVES)
    ]
    back = lax.all_to_all(result, both, 0, 0, axis_index_groups=halves, tiled=True)
    back = back.reshape(step, step, part_cols, part_rows, 2 * channels)
    back = jnp.transpose(back, (3, 0, 2, 1, 4)).reshape(tile_rows, tile_cols, 2 * channels)
    return back[..., :channels], back[..., channels:]


def solution(mesh):
    row_count, col_count = mesh.shape["row"], mesh.shape["col"]
    classes = DILATION_STEP * DILATION_STEP
    paired = row_count * col_count == HALVES * classes and col_count % (2 * HALVES) == 0
    in_specs = (P("row", "col", None), P(), P(), P(), P(), P("row", "col", None))
    out_specs = (P("row", "col", None), P("row", "col", None))

    def whole(feature_map, *others):
        size = feature_map.shape[0]
        part_rows, part_cols = size // row_count // DILATION_STEP, size // col_count // DILATION_STEP
        fits = size % (DILATION_STEP * row_count) == 0 and size % (DILATION_STEP * col_count) == 0
        fits = fits and part_rows % 16 == 0 and CONVS % part_cols == 0
        per_device = by_classes if paired and fits else by_tiles
        return jax.shard_map(
            per_device, mesh=mesh, in_specs=in_specs, out_specs=out_specs, check_vma=False
        )(feature_map, *others)

    return whole
```

```python
import functools

import jax
import jax.numpy as jnp
from jax import lax
from jax.experimental import pallas as pl
from jax.experimental.pallas import tpu as pltpu
from jax.sharding import PartitionSpec as P

DILATION_STEP = 4
HALVES = 2
CONVS = 4


root_half = 0.7071067811865476
inv_root_tau = 0.3989422804014327
both = ("row", "col")


def with_halo(array, sides, width):
    for axis, dim in sides:
        size, length = (lax.axis_size(axis), array.shape[dim])
        up = [(i, (i + 1) % size) for i in range(size - 1)]
        down = [(j, i) for i, j in up]
        last = lax.slice_in_dim(array, length - width, length, axis=dim)
        first = lax.slice_in_dim(array, 0, width, axis=dim)
        before = lax.ppermute(last, axis, up)
        after = lax.ppermute(first, axis, down)
        array = jnp.concatenate([before, array, after], axis=dim)
    return array


def gelu_value(value_array):
    return 0.5 * value_array * (1.0 + lax.erf(value_array * root_half))


def gelu_slope(value_array):
    return (
        0.5 * (1.0 + lax.erf(value_array * root_half))
        + value_array * jnp.exp(-0.5 * value_array * value_array) * inv_root_tau
    )


def gelu_pair(value_array):
    share = 0.5 + 0.5 * lax.erf(value_array * root_half)
    bell = jnp.exp(-0.5 * value_array * value_array) * inv_root_tau
    return value_array * share, share + value_array * bell


def conv(padded_input, conv_kernel, step):
    return lax.conv_general_dilated(
        padded_input[None],
        conv_kernel,
        (1, 1),
        "VALID",
        rhs_dilation=(step, step),
        dimension_numbers=("NHWC", "HWIO", "NHWC"),
        preferred_element_type=jnp.float32,
    )[0]


def dilated_conv(padded_input, conv_kernel):
    return conv(padded_input, conv_kernel, DILATION_STEP)


def reversed_kernel(conv_kernel):
    return jnp.transpose(conv_kernel[::-1, ::-1], (0, 1, 3, 2))


def extend(value_array):
    return with_halo(value_array, (("row", 0), ("col", 1)), DILATION_STEP)


def mirror(tile):
    row_count = lax.axis_size("row")
    col_count = lax.axis_size("col")
    tile_rows, tile_cols, channels = tile.shape
    unit_len = tile_rows // col_count
    col_ratio = col_count // row_count
    spread_parts = tile.reshape(1, 1, col_ratio, row_count, unit_len, tile_cols * channels)
    spread_parts = lax.all_to_all(spread_parts, "row", split_axis=3, concat_axis=1, tiled=True)
    across_parts = spread_parts.reshape(1, col_count, unit_len, 1, tile_cols * channels)
    across_parts = lax.all_to_all(across_parts, "col", split_axis=1, concat_axis=3, tiled=True)
    settle_parts = across_parts.reshape(1, 1, unit_len, row_count, tile_rows * channels)
    settle_parts = lax.all_to_all(settle_parts, "row", split_axis=3, concat_axis=1, tiled=True)
    turned = settle_parts.reshape(tile_cols, tile_rows, channels)
    return jnp.transpose(turned, (1, 0, 2))


def add_rounded(first, second):
    return (first.astype(jnp.float32) + second.astype(jnp.float32)).astype(jnp.bfloat16)


def by_tiles(feature_map, kernel_first, bias_first, kernel_second, bias_second, cotangent):
    symmetric = add_rounded(feature_map, mirror(feature_map))
    pre_first = dilated_conv(extend(symmetric), kernel_first) + bias_first
    hidden = gelu_value(pre_first).astype(jnp.bfloat16)
    pre_second = dilated_conv(extend(hidden), kernel_second) + bias_second
    output = (symmetric.astype(jnp.float32) + gelu_value(pre_second)).astype(jnp.bfloat16)
    grad_second = (cotangent.astype(jnp.float32) * gelu_slope(pre_second)).astype(jnp.bfloat16)
    hidden_gradient = dilated_conv(extend(grad_second), reversed_kernel(kernel_second))
    grad_first = (hidden_gradient * gelu_slope(pre_first)).astype(jnp.bfloat16)
    total_sum = cotangent.astype(jnp.float32) + dilated_conv(
        extend(grad_first), reversed_kernel(kernel_first)
    )
    grad_sym = total_sum.astype(jnp.bfloat16)
    return output, add_rounded(grad_sym, mirror(grad_sym))


def matrix_kernel(half_count, weight_first, weight_second, bias_first, bias_second, *outputs):
    first, second, third, fourth, first_bias, second_bias = outputs
    taps, channels = weight_first.shape[0], weight_first.shape[2]
    gap = jnp.zeros(weight_first.shape[2:], weight_first.dtype)
    half = lax.div(lax.axis_index("col"), half_count)
    for weight, ahead, behind in (
        (weight_first, first, fourth),
        (weight_second, second, third),
    ):
        for p in range(taps):
            along = half * (taps - 1) + (1 - 2 * half) * p
            for q in range(taps):
                upper = jnp.concatenate([weight[q, along], gap], 1)
                lower = jnp.concatenate([gap, weight[along, q]], 1)
                block = jnp.concatenate([upper, lower], 0)
                columns = pl.ds(2 * channels * q, 2 * channels)
                if ahead is second:
                    ahead[pl.ds(2 * channels * p, 2 * channels), columns] = block
                else:
                    joint = jnp.concatenate([weight[q, along], weight[along, q]], 1)
                    ahead[pl.ds(channels * p, channels), columns] = joint
                p_back, q_back = taps - 1 - p, taps - 1 - q
                behind[
                    pl.ds(2 * channels * q_back, 2 * channels),
                    pl.ds(2 * channels * p_back, 2 * channels),
                ] = block
    rest = slice(taps * channels, first.shape[0])
    first[rest] = jnp.zeros_like(first[rest])
    for bias, wide in ((bias_first, first_bias), (bias_second, second_bias)):
        wide[...] = jnp.concatenate([bias[...], bias[...]], 1)


def chain_matrices(half_count, weight_first, weight_second, bias_first, bias_second):
    taps, channels = weight_first.shape[0], weight_first.shape[2]
    size = taps * 2 * channels
    vmem = pl.BlockSpec(memory_space=pltpu.VMEM)
    return pl.pallas_call(
        functools.partial(matrix_kernel, half_count),
        out_shape=[
            jax.ShapeDtypeStruct(((taps + 1) * channels, size), jnp.bfloat16),
            *[jax.ShapeDtypeStruct((size, size), jnp.bfloat16)] * 3,
        ]
        + [jax.ShapeDtypeStruct((1, 2 * channels), jnp.float32)] * 2,
        in_specs=[vmem] * 4,
        out_specs=[vmem] * 6,
        compiler_params=pltpu.CompilerParams(vmem_limit_bytes=16 * 2**20),
    )(weight_first, weight_second, bias_first[None], bias_second[None])


def class_order():
    step = range(DILATION_STEP)
    pairs = [((a, a), (a + 1, a + 1)) for a in step[::2]]
    pairs += [((a, b), (b, a)) for a in step for b in step if a < b]
    return [c for pair in sorted(pairs) for c in pair][::-1]


def part_kernel(tile_cols, whole, parts, tile):
    step = DILATION_STEP
    part_cols = tile_cols // step
    part_rows = whole.shape[0] // (tile_cols * step)
    tile[: whole.shape[0]] = whole[...]
    for index, (a, b) in enumerate(class_order()):
        columns = [
            tile[pl.ds(a * tile_cols + k * step + b, part_rows, stride=step * tile_cols), :]
            for k in range(part_cols)
        ]
        part = jnp.concatenate(columns, 0).astype(jnp.bfloat16)
        r, c = divmod(index, parts.shape[2])
        for half in range(HALVES):
            parts[r, half, c] = part


def class_parts(row_count, feature_map, cotangent):
    tile_rows, tile_cols, channels = feature_map.shape
    classes = DILATION_STEP * DILATION_STEP
    cells = tile_rows * tile_cols
    shape = (row_count, HALVES, classes // row_count, cells // classes, 2 * channels)
    tile = jnp.concatenate([feature_map, cotangent], 2).astype(jnp.float32)
    return pl.pallas_call(
        functools.partial(part_kernel, tile_cols),
        out_shape=jax.ShapeDtypeStruct(shape, jnp.bfloat16),
        in_specs=[pl.BlockSpec(memory_space=pltpu.VMEM)],
        out_specs=pl.BlockSpec(memory_space=pltpu.VMEM),
        scratch_shapes=[pltpu.VMEM((cells + DILATION_STEP * tile_cols, 2 * channels), jnp.float32)],
        compiler_params=pltpu.CompilerParams(vmem_limit_bytes=16 * 2**20),
    )(tile.reshape(cells, 2 * channels))


def class_kernel(
    row_count,
    part_cols,
    own,
    other,
    weight_first,
    weight_second,
    weight_third,
    weight_fourth,
    bias_first,
    bias_second,
    result,
    turning,
    window,
):
    blocks, part, width = own.shape
    channels = width // 2
    part_rows = part // part_cols
    col_count = blocks // row_count
    half_count = col_count // HALVES
    class_cols, class_rows = col_count * part_cols, row_count * part_rows
    share = class_cols // HALVES
    count = share + CONVS
    column = lax.axis_index("col")
    half = lax.div(column, half_count)
    place = lax.axis_index("row") * half_count + lax.rem(column, half_count)
    evens = [index for index, (a, b) in enumerate(class_order()) if a == b]
    even = functools.reduce(jnp.logical_or, [place == index for index in evens])
    row = lax.broadcasted_iota(jnp.int32, (1, class_rows, width), 1)

    def chains(half, mirrored):
        def inward(index, total):
            return total - 1 - index if half else index

        pieces = []
        for n in range(count // part_cols):
            blocks = [own[r * col_count + inward(n, col_count)] for r in range(row_count)]
            for k in range(part_cols):
                ends = [slice(m * part_rows, (m + 1) * part_rows) for m in (k, part_cols - 1 - k)]
                pieces += [block[ends[half]] for block in blocks]
        straight = jnp.concatenate(pieces, 0).astype(jnp.float32)

        for r in range(row_count):
            reach = slice(r * col_count, (r + 1) * col_count)
            piece = mirrored[reach].astype(jnp.float32)
            piece = piece.reshape(class_cols, part_rows, width)
            read = [inward(n, class_cols) - r * part_rows for n in range(count)]
            read = [n for n in read if 0 <= n < part_rows]
            low_row, high_row = min(read) // 8 * 8, (max(read) // 8 + 1) * 8
            for k in range(class_cols):
                rows = pl.ds(k * class_rows + r * part_rows + low_row, high_row - low_row)
                turning[rows, :] = piece[k, low_row:high_row]
        turned = jnp.concatenate(
            [
                turning[pl.ds(inward(n, class_cols), class_cols, stride=class_rows), :]
                for n in range(count)
            ],
            0,
        )

        def low(value):
            return lax.broadcasted_iota(jnp.int32, value.shape, 1) < channels

        def swapped(value):
            return pltpu.roll(value, channels, 1)

        def tap_sum(image, begin, end, matrix, dimension, doubled=False):
            first, last = begin * class_rows, end * class_rows
            gap = [jnp.zeros((class_rows, width), image.dtype)] if begin == 0 else []
            before = image[max(first - class_rows, 0) : last - class_rows]
            before = jnp.concatenate(gap + [before], 0)
            after = image[first + class_rows : last + class_rows]
            image = image[first:last]
            columns = [jnp.where(low(image), before, image), after]
            def product(value, weights):
                return lax.dot_general(
                    value, weights, (((1,), (dimension,)), ((), ())), preferred_element_type=jnp.float32
                )

            if doubled:
                taps = product(jnp.concatenate(columns, 1), matrix[...])
            elif dimension == 0:
                taps = product(jnp.concatenate([image, after], 1), matrix[width:, :])
                taps = taps + product(before, matrix[:width, :])
            else:
                taps = product(jnp.concatenate([image, after], 1), matrix[:, width:])
                taps = taps + product(before, matrix[:, :width])
            taps = taps.reshape(end - begin, class_rows, 3 * width)
            above = jnp.where(row == 0, 0.0, pltpu.roll(taps[:, :, :width], 1, 1))
            below = pltpu.roll(taps[:, :, 2 * width :], class_rows - 1, 1)
            below = jnp.where(row == class_rows - 1, 0.0, below)
            return (above + taps[:, :, width : 2 * width] + below).reshape(last - first, width)

        def runs(total):
            cut = total * 3 // 5
            return (0, cut), (cut, total)

        def columns(value, begin, end):
            return value[begin * class_rows : end * class_rows]

        symmetric = straight + turned
        symmetric = jnp.where(low(symmetric), symmetric, swapped(symmetric)).astype(jnp.bfloat16)
        gradient = jnp.where(low(turned), swapped(straight), turned)

        hidden, slope_first = [], []
        for run in runs(count - 1):
            pre_first = tap_sum(symmetric, *run, weight_first, 0, True) + bias_first[...]
            value, slope = gelu_pair(pre_first)
            hidden.append(value.astype(jnp.bfloat16))
            slope_first.append(slope)
        hidden, slope_first = jnp.concatenate(hidden, 0), jnp.concatenate(slope_first, 0)
        output, grad_second = [], []
        for run in runs(count - 2):
            pre_second = tap_sum(hidden, *run, weight_second, 0) + bias_second[...]
            value, slope = gelu_pair(pre_second)
            output.append(columns(symmetric, *run).astype(jnp.float32) + value)
            grad_second.append((columns(gradient, *run) * slope).astype(jnp.bfloat16))
        output, grad_second = jnp.concatenate(output, 0), jnp.concatenate(grad_second, 0)
        grad_first = jnp.concatenate(
            [
                (tap_sum(grad_second, *run, weight_third, 1) * columns(slope_first, *run)).astype(
                    jnp.bfloat16
                )
                for run in runs(count - 3)
            ],
            0,
        )
        for run in runs(share):
            total_sum = columns(gradient, *run) + tap_sum(grad_first, *run, weight_fourth, 1)
            grad_sym = total_sum.astype(jnp.bfloat16).astype(jnp.float32)
            grad_input = grad_sym + swapped(grad_sym)
            finished = jnp.where(low(grad_input), columns(output, *run), grad_input)
            finished = finished.astype(jnp.bfloat16).reshape(run[1] - run[0], class_rows, width)
            window[run[0] : run[1]] = finished

        for index, (a, b) in enumerate(class_order()):
            r, c = divmod(index, half_count)
            kept = [
                window[inward(c * part_cols + k, share), r * part_rows : (r + 1) * part_rows]
                for k in range(part_cols)
            ]
            result[a * DILATION_STEP + b] = jnp.concatenate(kept, 0)

    for index in range(HALVES):
        here = half == index
        pl.when(jnp.logical_and(here, even))(functools.partial(chains, index, own))
        pl.when(jnp.logical_and(here, jnp.logical_not(even)))(
            functools.partial(chains, index, other)
        )


def class_chains(row_count, part_cols, own, other, *parameters):
    blocks, part, width = own.shape
    class_cols, class_rows = blocks // row_count * part_cols, row_count * (part // part_cols)
    share = class_cols // HALVES
    return pl.pallas_call(
        functools.partial(class_kernel, row_count, part_cols),
        out_shape=jax.ShapeDtypeStruct((blocks // HALVES, part, width), jnp.bfloat16),
        in_specs=[pl.BlockSpec(memory_space=pltpu.VMEM)] * 8,
        out_specs=pl.BlockSpec(memory_space=pltpu.VMEM),
        scratch_shapes=[
            pltpu.VMEM(((class_cols + 1) * class_rows, width), jnp.float32),
            pltpu.VMEM((share, class_rows, width), jnp.bfloat16),
        ],
        compiler_params=pltpu.CompilerParams(vmem_limit_bytes=32 * 2**20),
    )(own, other, *parameters)


def by_classes(feature_map, kernel_first, bias_first, kernel_second, bias_second, cotangent):
    row_count, col_count = lax.axis_size("row"), lax.axis_size("col")
    tile_rows, tile_cols, channels = feature_map.shape
    step = DILATION_STEP
    part_rows, part_cols = tile_rows // step, tile_cols // step

    parts = class_parts(row_count, feature_map, cotangent)
    parts = parts.reshape(row_count * col_count, part_cols * part_rows, 2 * channels)
    own = lax.all_to_all(parts, both, 0, 0, tiled=True)
    half_count = col_count // HALVES
    raw = (kernel_first, kernel_second, bias_first, bias_second)
    own, *raw = lax.optimization_barrier((own,) + raw)
    other = lax.ppermute(own, "col", [(i, i ^ 1) for i in range(col_count)])
    result = class_chains(row_count, part_cols, own, other, *chain_matrices(half_count, *raw))

    order = sorted(range(step * step), key=lambda index: class_order()[index])
    halves = [
        [i // half_count * col_count + h * half_count + i % half_count for i in order]
        for h in range(HALVES)
    ]
    back = lax.all_to_all(result, both, 0, 0, axis_index_groups=halves, tiled=True)
    back = back.reshape(step, step, part_cols, part_rows, 2 * channels)
    back = jnp.transpose(back, (3, 0, 2, 1, 4)).reshape(tile_rows, tile_cols, 2 * channels)
    return back[..., :channels], back[..., channels:]


def solution(mesh):
    row_count, col_count = mesh.shape["row"], mesh.shape["col"]
    classes = DILATION_STEP * DILATION_STEP
    paired = row_count * col_count == HALVES * classes and col_count % (2 * HALVES) == 0
    in_specs = (P("row", "col", None), P(), P(), P(), P(), P("row", "col", None))
    out_specs = (P("row", "col", None), P("row", "col", None))

    def whole(feature_map, *others):
        size = feature_map.shape[0]
        part_rows, part_cols = size // row_count // DILATION_STEP, size // col_count // DILATION_STEP
        fits = size % (DILATION_STEP * row_count) == 0 and size % (DILATION_STEP * col_count) == 0
        fits = fits and part_rows % 16 == 0 and CONVS % part_cols == 0
        per_device = by_classes if paired and fits else by_tiles
        return jax.shard_map(
            per_device, mesh=mesh, in_specs=in_specs, out_specs=out_specs, check_vma=False
        )(feature_map, *others)

    return whole
```

```python
import functools

import jax
import jax.numpy as jnp
from jax import lax
from jax.experimental import pallas as pl
from jax.experimental.pallas import tpu as pltpu
from jax.sharding import PartitionSpec as P

DILATION_STEP = 4
HALVES = 2
CONVS = 4


root_half = 0.7071067811865476
inv_root_tau = 0.3989422804014327
both = ("row", "col")


def with_halo(array, sides, width):
    for axis, dim in sides:
        size, length = (lax.axis_size(axis), array.shape[dim])
        up = [(i, (i + 1) % size) for i in range(size - 1)]
        down = [(j, i) for i, j in up]
        last = lax.slice_in_dim(array, length - width, length, axis=dim)
        first = lax.slice_in_dim(array, 0, width, axis=dim)
        before = lax.ppermute(last, axis, up)
        after = lax.ppermute(first, axis, down)
        array = jnp.concatenate([before, array, after], axis=dim)
    return array


def gelu_value(value_array):
    return 0.5 * value_array * (1.0 + lax.erf(value_array * root_half))


def gelu_slope(value_array):
    return (
        0.5 * (1.0 + lax.erf(value_array * root_half))
        + value_array * jnp.exp(-0.5 * value_array * value_array) * inv_root_tau
    )


def gelu_pair(value_array):
    share = 0.5 + 0.5 * lax.erf(value_array * root_half)
    bell = jnp.exp(-0.5 * value_array * value_array) * inv_root_tau
    return value_array * share, share + value_array * bell


def conv(padded_input, conv_kernel, step):
    return lax.conv_general_dilated(
        padded_input[None],
        conv_kernel,
        (1, 1),
        "VALID",
        rhs_dilation=(step, step),
        dimension_numbers=("NHWC", "HWIO", "NHWC"),
        preferred_element_type=jnp.float32,
    )[0]


def dilated_conv(padded_input, conv_kernel):
    return conv(padded_input, conv_kernel, DILATION_STEP)


def reversed_kernel(conv_kernel):
    return jnp.transpose(conv_kernel[::-1, ::-1], (0, 1, 3, 2))


def extend(value_array):
    return with_halo(value_array, (("row", 0), ("col", 1)), DILATION_STEP)


def mirror(tile):
    row_count = lax.axis_size("row")
    col_count = lax.axis_size("col")
    tile_rows, tile_cols, channels = tile.shape
    unit_len = tile_rows // col_count
    col_ratio = col_count // row_count
    spread_parts = tile.reshape(1, 1, col_ratio, row_count, unit_len, tile_cols * channels)
    spread_parts = lax.all_to_all(spread_parts, "row", split_axis=3, concat_axis=1, tiled=True)
    across_parts = spread_parts.reshape(1, col_count, unit_len, 1, tile_cols * channels)
    across_parts = lax.all_to_all(across_parts, "col", split_axis=1, concat_axis=3, tiled=True)
    settle_parts = across_parts.reshape(1, 1, unit_len, row_count, tile_rows * channels)
    settle_parts = lax.all_to_all(settle_parts, "row", split_axis=3, concat_axis=1, tiled=True)
    turned = settle_parts.reshape(tile_cols, tile_rows, channels)
    return jnp.transpose(turned, (1, 0, 2))


def add_rounded(first, second):
    return (first.astype(jnp.float32) + second.astype(jnp.float32)).astype(jnp.bfloat16)


def by_tiles(feature_map, kernel_first, bias_first, kernel_second, bias_second, cotangent):
    symmetric = add_rounded(feature_map, mirror(feature_map))
    pre_first = dilated_conv(extend(symmetric), kernel_first) + bias_first
    hidden = gelu_value(pre_first).astype(jnp.bfloat16)
    pre_second = dilated_conv(extend(hidden), kernel_second) + bias_second
    output = (symmetric.astype(jnp.float32) + gelu_value(pre_second)).astype(jnp.bfloat16)
    grad_second = (cotangent.astype(jnp.float32) * gelu_slope(pre_second)).astype(jnp.bfloat16)
    hidden_gradient = dilated_conv(extend(grad_second), reversed_kernel(kernel_second))
    grad_first = (hidden_gradient * gelu_slope(pre_first)).astype(jnp.bfloat16)
    total_sum = cotangent.astype(jnp.float32) + dilated_conv(
        extend(grad_first), reversed_kernel(kernel_first)
    )
    grad_sym = total_sum.astype(jnp.bfloat16)
    return output, add_rounded(grad_sym, mirror(grad_sym))


def matrix_kernel(half_count, weight_first, weight_second, bias_first, bias_second, *outputs):
    first, second, third, fourth, first_bias, second_bias = outputs
    taps, channels = weight_first.shape[0], weight_first.shape[2]
    gap = jnp.zeros(weight_first.shape[2:], weight_first.dtype)
    half = lax.div(lax.axis_index("col"), half_count)
    for weight, ahead, behind in (
        (weight_first, first, fourth),
        (weight_second, second, third),
    ):
        for p in range(taps):
            along = half * (taps - 1) + (1 - 2 * half) * p
            for q in range(taps):
                upper = jnp.concatenate([weight[q, along], gap], 1)
                lower = jnp.concatenate([gap, weight[along, q]], 1)
                block = jnp.concatenate([upper, lower], 0)
                columns = pl.ds(2 * channels * q, 2 * channels)
                if ahead is second:
                    ahead[pl.ds(2 * channels * p, 2 * channels), columns] = block
                else:
                    joint = jnp.concatenate([weight[q, along], weight[along, q]], 1)
                    ahead[pl.ds(channels * p, channels), columns] = joint
                p_back, q_back = taps - 1 - p, taps - 1 - q
                behind[
                    pl.ds(2 * channels * q_back, 2 * channels),
                    pl.ds(2 * channels * p_back, 2 * channels),
                ] = block
    rest = slice(taps * channels, first.shape[0])
    first[rest] = jnp.zeros_like(first[rest])
    for bias, wide in ((bias_first, first_bias), (bias_second, second_bias)):
        wide[...] = jnp.concatenate([bias[...], bias[...]], 1)


def chain_matrices(half_count, weight_first, weight_second, bias_first, bias_second):
    taps, channels = weight_first.shape[0], weight_first.shape[2]
    size = taps * 2 * channels
    vmem = pl.BlockSpec(memory_space=pltpu.VMEM)
    return pl.pallas_call(
        functools.partial(matrix_kernel, half_count),
        out_shape=[
            jax.ShapeDtypeStruct(((taps + 1) * channels, size), jnp.bfloat16),
            *[jax.ShapeDtypeStruct((size, size), jnp.bfloat16)] * 3,
        ]
        + [jax.ShapeDtypeStruct((1, 2 * channels), jnp.float32)] * 2,
        in_specs=[vmem] * 4,
        out_specs=[vmem] * 6,
        compiler_params=pltpu.CompilerParams(vmem_limit_bytes=16 * 2**20),
    )(weight_first, weight_second, bias_first[None], bias_second[None])


def class_order():
    step = range(DILATION_STEP)
    pairs = [((a, a), (a + 1, a + 1)) for a in step[::2]]
    pairs += [((a, b), (b, a)) for a in step for b in step if a < b]
    return [c for pair in sorted(pairs) for c in pair][::-1]


def part_kernel(tile_cols, whole, parts, tile):
    step = DILATION_STEP
    part_cols = tile_cols // step
    part_rows = whole.shape[0] // (tile_cols * step)
    tile[: whole.shape[0]] = whole[...]
    for index, (a, b) in enumerate(class_order()):
        columns = [
            tile[pl.ds(a * tile_cols + k * step + b, part_rows, stride=step * tile_cols), :]
            for k in range(part_cols)
        ]
        part = jnp.concatenate(columns, 0).astype(jnp.bfloat16)
        r, c = divmod(index, parts.shape[2])
        for half in range(HALVES):
            parts[r, half, c] = part


def class_parts(row_count, feature_map, cotangent):
    tile_rows, tile_cols, channels = feature_map.shape
    classes = DILATION_STEP * DILATION_STEP
    cells = tile_rows * tile_cols
    shape = (row_count, HALVES, classes // row_count, cells // classes, 2 * channels)
    tile = jnp.concatenate([feature_map, cotangent], 2).astype(jnp.float32)
    return pl.pallas_call(
        functools.partial(part_kernel, tile_cols),
        out_shape=jax.ShapeDtypeStruct(shape, jnp.bfloat16),
        in_specs=[pl.BlockSpec(memory_space=pltpu.VMEM)],
        out_specs=pl.BlockSpec(memory_space=pltpu.VMEM),
        scratch_shapes=[pltpu.VMEM((cells + DILATION_STEP * tile_cols, 2 * channels), jnp.float32)],
        compiler_params=pltpu.CompilerParams(vmem_limit_bytes=16 * 2**20),
    )(tile.reshape(cells, 2 * channels))


def class_kernel(
    row_count,
    part_cols,
    own,
    other,
    weight_first,
    weight_second,
    weight_third,
    weight_fourth,
    bias_first,
    bias_second,
    result,
    turning,
    window,
):
    blocks, part, width = own.shape
    channels = width // 2
    part_rows = part // part_cols
    col_count = blocks // row_count
    half_count = col_count // HALVES
    class_cols, class_rows = col_count * part_cols, row_count * part_rows
    share = class_cols // HALVES
    count = share + CONVS
    column = lax.axis_index("col")
    half = lax.div(column, half_count)
    place = lax.axis_index("row") * half_count + lax.rem(column, half_count)
    evens = [index for index, (a, b) in enumerate(class_order()) if a == b]
    even = functools.reduce(jnp.logical_or, [place == index for index in evens])
    row = lax.broadcasted_iota(jnp.int32, (1, class_rows, width), 1)

    def chains(half):
        def inward(index, total):
            return total - 1 - index if half else index

        pieces = []
        for n in range(count // part_cols):
            blocks = [own[r * col_count + inward(n, col_count)] for r in range(row_count)]
            for k in range(part_cols):
                ends = [slice(m * part_rows, (m + 1) * part_rows) for m in (k, part_cols - 1 - k)]
                pieces += [block[ends[half]] for block in blocks]
        straight = jnp.concatenate(pieces, 0).astype(jnp.float32)

        for r in range(row_count):
            reach = slice(r * col_count, (r + 1) * col_count)
            piece = jnp.where(even, own[reach], other[reach]).astype(jnp.float32)
            piece = piece.reshape(class_cols, part_rows, width)
            for k in range(class_cols):
                turning[pl.ds(k * class_rows + r * part_rows, part_rows), :] = piece[k]
        turned = jnp.concatenate(
            [
                turning[pl.ds(inward(n, class_cols), class_cols, stride=class_rows), :]
                for n in range(count)
            ],
            0,
        )

        def low(value):
            return lax.broadcasted_iota(jnp.int32, value.shape, 1) < channels

        def swapped(value):
            return pltpu.roll(value, channels, 1)

        def tap_sum(image, begin, end, matrix, dimension, doubled=False):
            first, last = begin * class_rows, end * class_rows
            gap = [jnp.zeros((class_rows, width), image.dtype)] if begin == 0 else []
            before = image[max(first - class_rows, 0) : last - class_rows]
            before = jnp.concatenate(gap + [before], 0)
            after = image[first + class_rows : last + class_rows]
            image = image[first:last]
            columns = [jnp.where(low(image), before, image), after]
            def product(value, weights):
                return lax.dot_general(
                    value, weights, (((1,), (dimension,)), ((), ())), preferred_element_type=jnp.float32
                )

            if doubled:
                taps = product(jnp.concatenate(columns, 1), matrix[...])
            elif dimension == 0:
                taps = product(jnp.concatenate([image, after], 1), matrix[width:, :])
                taps = taps + product(before, matrix[:width, :])
            else:
                taps = product(jnp.concatenate([image, after], 1), matrix[:, width:])
                taps = taps + product(before, matrix[:, :width])
            taps = taps.reshape(end - begin, class_rows, 3 * width)
            above = jnp.where(row == 0, 0.0, pltpu.roll(taps[:, :, :width], 1, 1))
            below = pltpu.roll(taps[:, :, 2 * width :], class_rows - 1, 1)
            below = jnp.where(row == class_rows - 1, 0.0, below)
            return (above + taps[:, :, width : 2 * width] + below).reshape(last - first, width)

        def runs(total):
            cut = total // 2
            return (0, cut), (cut, total)

        def columns(value, begin, end):
            return value[begin * class_rows : end * class_rows]

        symmetric = straight + turned
        symmetric = jnp.where(low(symmetric), symmetric, swapped(symmetric)).astype(jnp.bfloat16)
        gradient = jnp.where(low(turned), swapped(straight), turned)

        hidden, slope_first = [], []
        for run in runs(count - 1):
            pre_first = tap_sum(symmetric, *run, weight_first, 0, True) + bias_first[...]
            value, slope = gelu_pair(pre_first)
            hidden.append(value.astype(jnp.bfloat16))
            slope_first.append(slope)
        hidden, slope_first = jnp.concatenate(hidden, 0), jnp.concatenate(slope_first, 0)
        output, grad_second = [], []
        for run in runs(count - 2):
            pre_second = tap_sum(hidden, *run, weight_second, 0) + bias_second[...]
            value, slope = gelu_pair(pre_second)
            output.append(columns(symmetric, *run).astype(jnp.float32) + value)
            grad_second.append((columns(gradient, *run) * slope).astype(jnp.bfloat16))
        output, grad_second = jnp.concatenate(output, 0), jnp.concatenate(grad_second, 0)
        grad_first = jnp.concatenate(
            [
                (tap_sum(grad_second, *run, weight_third, 1) * columns(slope_first, *run)).astype(
                    jnp.bfloat16
                )
                for run in runs(count - 3)
            ],
            0,
        )
        for run in runs(share):
            total_sum = columns(gradient, *run) + tap_sum(grad_first, *run, weight_fourth, 1)
            grad_sym = total_sum.astype(jnp.bfloat16).astype(jnp.float32)
            grad_input = grad_sym + swapped(grad_sym)
            finished = jnp.where(low(grad_input), columns(output, *run), grad_input)
            finished = finished.astype(jnp.bfloat16).reshape(run[1] - run[0], class_rows, width)
            window[run[0] : run[1]] = finished

        for index, (a, b) in enumerate(class_order()):
            r, c = divmod(index, half_count)
            kept = [
                window[inward(c * part_cols + k, share), r * part_rows : (r + 1) * part_rows]
                for k in range(part_cols)
            ]
            result[a * DILATION_STEP + b] = jnp.concatenate(kept, 0)

    for index in range(HALVES):
        pl.when(half == index)(functools.partial(chains, index))


def class_chains(row_count, part_cols, own, other, *parameters):
    blocks, part, width = own.shape
    class_cols, class_rows = blocks // row_count * part_cols, row_count * (part // part_cols)
    share = class_cols // HALVES
    return pl.pallas_call(
        functools.partial(class_kernel, row_count, part_cols),
        out_shape=jax.ShapeDtypeStruct((blocks // HALVES, part, width), jnp.bfloat16),
        in_specs=[pl.BlockSpec(memory_space=pltpu.VMEM)] * 8,
        out_specs=pl.BlockSpec(memory_space=pltpu.VMEM),
        scratch_shapes=[
            pltpu.VMEM(((class_cols + 1) * class_rows, width), jnp.float32),
            pltpu.VMEM((share, class_rows, width), jnp.bfloat16),
        ],
        compiler_params=pltpu.CompilerParams(vmem_limit_bytes=32 * 2**20),
    )(own, other, *parameters)


def by_classes(feature_map, kernel_first, bias_first, kernel_second, bias_second, cotangent):
    row_count, col_count = lax.axis_size("row"), lax.axis_size("col")
    tile_rows, tile_cols, channels = feature_map.shape
    step = DILATION_STEP
    part_rows, part_cols = tile_rows // step, tile_cols // step

    parts = class_parts(row_count, feature_map, cotangent)
    parts = parts.reshape(row_count * col_count, part_cols * part_rows, 2 * channels)
    own = lax.all_to_all(parts, both, 0, 0, tiled=True)
    half_count = col_count // HALVES
    raw = (kernel_first, kernel_second, bias_first, bias_second)
    own, *raw = lax.optimization_barrier((own,) + raw)
    other = lax.ppermute(own, "col", [(i, i ^ 1) for i in range(col_count)])
    result = class_chains(row_count, part_cols, own, other, *chain_matrices(half_count, *raw))

    order = sorted(range(step * step), key=lambda index: class_order()[index])
    halves = [
        [i // half_count * col_count + h * half_count + i % half_count for i in order]
        for h in range(HALVES)
    ]
    back = lax.all_to_all(result, both, 0, 0, axis_index_groups=halves, tiled=True)
    back = back.reshape(step, step, part_cols, part_rows, 2 * channels)
    back = jnp.transpose(back, (3, 0, 2, 1, 4)).reshape(tile_rows, tile_cols, 2 * channels)
    return back[..., :channels], back[..., channels:]


def solution(mesh):
    row_count, col_count = mesh.shape["row"], mesh.shape["col"]
    classes = DILATION_STEP * DILATION_STEP
    paired = row_count * col_count == HALVES * classes and col_count % (2 * HALVES) == 0
    in_specs = (P("row", "col", None), P(), P(), P(), P(), P("row", "col", None))
    out_specs = (P("row", "col", None), P("row", "col", None))

    def whole(feature_map, *others):
        size = feature_map.shape[0]
        part_rows, part_cols = size // row_count // DILATION_STEP, size // col_count // DILATION_STEP
        fits = size % (DILATION_STEP * row_count) == 0 and size % (DILATION_STEP * col_count) == 0
        fits = fits and part_rows % 16 == 0 and CONVS % part_cols == 0
        per_device = by_classes if paired and fits else by_tiles
        return jax.shard_map(
            per_device, mesh=mesh, in_specs=in_specs, out_specs=out_specs, check_vma=False
        )(feature_map, *others)

    return whole
```
